128 devices in a mesh: xi: 8 (over x_hi, y), eta: 16 (over x_lo, z, core).
Axes of the slice: x: 4 (x_hi: 2, x_lo: 2; x = x_hi * 2 + x_lo), y: 4, z: 4, core: 2. Of those that a mesh axis runs over, the one named last changes fastest.
Arguments:
- flow_state: float32 [5, 1, 128, 1024], P(None, None, 'eta', 'xi'), may hold values from -6 to 6
- speed_xi: float32 [1, 128, 1024], P(None, 'eta', 'xi'), may hold values from -300 to 300
- sound_xi: float32 [1, 128, 1024], P(None, 'eta', 'xi'), may hold values from 300 to 3000
- speed_eta: float32 [1, 128, 1024], P(None, 'eta', 'xi'), may hold values from -300 to 300
- sound_eta: float32 [1, 128, 1024], P(None, 'eta', 'xi'), may hold values from 300 to 3000
- coupling: float32 [5, 5], replicated, may hold values from -2.5 to 2.5
- left_vectors: float32 [5, 5], replicated, may hold values from -1 to 2
- middle_vectors: float32 [5, 5], replicated, may hold values from -1 to 2
- right_vectors: float32 [5, 5], replicated, may hold values from -1 to 2
Outputs:
- final_state: float32 [5, 1, 128, 1024], P(None, None, 'eta', 'xi')
- increment: float32 [5, 1, 128, 1024], P(None, None, 'eta', 'xi')
The draws below stay inside these ranges and needn't reach their ends.
All inputs are finite; a program needn't handle non-finite values.
Results may differ from the reference program's by a relative error of at most 0.0003.
Values sent between devices are 32-bit elements; how exact they have to be, the bound alone decides.
No kernel may reach another device: no remote copies, remote signals or barrier semaphores. Data moves between devices by JAX's collectives and lax.ppermute only.
A program may use at most 64 MiB of HBM per device.

```python
import math
import jax
import jax.numpy as jnp
from jax import lax

KS = 1
STEPS = 2
NXI = 1024
NETA = 128


def draw_mixing(key, marker):
    perturb = jax.random.truncated_normal(jax.random.fold_in(key, marker), -4.0, 4.0, (5, 5), jnp.float32)
    return jnp.eye(5, dtype=jnp.float32) + 0.25 * perturb


def draw_left_vectors(key, part):
    return draw_mixing(key, 11)


def draw_middle_vectors(key, part):
    return draw_mixing(key, 12)


def draw_right_vectors(key, part):
    return draw_mixing(key, 13)


def block_levels(rng, dims, split, least, top_value):
    gain, own = 1.0, jax.random.fold_in(rng, 6)
    for axis_at, shards_of in split:
        heights = jnp.exp(jax.random.uniform(jax.random.fold_in(own, axis_at), (shards_of,), jnp.float32, least / len(split), top_value / len(split)))
        gain = gain * jnp.repeat(heights, dims[axis_at] // shards_of).reshape([-1 if axis == axis_at else 1 for axis in range(len(dims))])
    return gain


def scatter_about(own_key, extent, deviation, reach, pieces=(), kind=jnp.bfloat16):
    gain = block_levels(own_key, extent, pieces, -0.22, 0.18) if pieces else 1.0
    values = jax.random.normal(own_key, extent, jnp.float32) * deviation * gain
    return jnp.minimum(jnp.maximum(values, -reach), reach).astype(kind)


def setup_inputs(seed: int = 0) -> dict:
    arg_keys = jax.random.split(jax.random.key(seed), 10)
    flow_state = scatter_about(arg_keys[0], (5, KS, NETA, NXI), 1.0, 6.0, ((2, 16), (3, 8)), jnp.float32)
    speed_xi = jnp.clip(jax.random.uniform(arg_keys[1], (KS, NETA, NXI), jnp.float32, -300.0, 300.0) * block_levels(arg_keys[1], (KS, NETA, NXI), ((1, 16), (2, 8)), -0.4, 0.0), -300.0, 300.0)
    sound_xi = jnp.clip(jnp.exp(math.log(3000.0) - 2.3025851 * jax.random.uniform(arg_keys[2], (KS, NETA, NXI), jnp.float32) ** block_levels(arg_keys[2], (KS, NETA, NXI), ((1, 16), (2, 8)), -0.2, 0.2)), 300.0, 3000.0)
    speed_eta = jnp.clip(jax.random.uniform(arg_keys[3], (KS, NETA, NXI), jnp.float32, -300.0, 300.0) * block_levels(arg_keys[3], (KS, NETA, NXI), ((1, 16), (2, 8)), -0.4, 0.0), -300.0, 300.0)
    sound_eta = jnp.clip(jnp.exp(math.log(3000.0) - 2.3025851 * jax.random.uniform(arg_keys[4], (KS, NETA, NXI), jnp.float32) ** block_levels(arg_keys[4], (KS, NETA, NXI), ((1, 16), (2, 8)), -0.2, 0.2)), 300.0, 3000.0)
    coupling = scatter_about(arg_keys[5], (5, 5), 5 ** -0.5, 2.5, (), jnp.float32)
    left_vectors = draw_left_vectors(jax.random.fold_in(arg_keys[9], 71), 0)
    middle_vectors = draw_middle_vectors(jax.random.fold_in(arg_keys[9], 71), 0)
    right_vectors = draw_right_vectors(jax.random.fold_in(arg_keys[9], 71), 0)
    return {"flow_state": flow_state, "speed_xi": speed_xi, "sound_xi": sound_xi, "speed_eta": speed_eta, "sound_eta": sound_eta, "coupling": coupling, "left_vectors": left_vectors, "middle_vectors": middle_vectors, "right_vectors": right_vectors}


DAMPING = 0.01


def speeds(advective, acoustic):
    wave_signs = jnp.array([0.0, 0.0, 0.0, 1.0, -1.0], dtype=advective.dtype)
    wave_signs = wave_signs.reshape((5,) + (1,) * advective.ndim)
    return advective[None] + wave_signs * acoustic[None], jnp.abs(advective) + acoustic


def rotate(matrix, field):
    return jnp.einsum("ab,b...->a...", matrix, field, precision=lax.Precision.HIGHEST)


def compose(earlier, latter):
    return (latter[0] * earlier[0] + latter[1] * earlier[2],
            latter[0] * earlier[1] + latter[1] * earlier[3],
            latter[2] * earlier[0] + latter[3] * earlier[2],
            latter[2] * earlier[1] + latter[3] * earlier[3],
            latter[0] * earlier[4] + latter[1] * earlier[5] + latter[4],
            latter[2] * earlier[4] + latter[3] * earlier[5] + latter[5])


def cell_maps(source, advect_here, damp_here, advect_near, damp_far):
    diagonal = 1.0 + advect_here + damp_here
    blanks = jnp.zeros_like(source)
    unities = jnp.ones_like(source)
    return (blanks, unities, damp_far / diagonal, advect_near / diagonal, blanks, source / diagonal)


def apply_maps(prefix, upper_state, lower_state):
    return prefix[2] * upper_state + prefix[3] * lower_state + prefix[5]


def fixed_point(overall):
    determinant = (1.0 - overall[0]) * (1.0 - overall[3]) - overall[1] * overall[2]
    upper_state = ((1.0 - overall[3]) * overall[4] + overall[1] * overall[5]) / determinant
    lower_state = (overall[2] * overall[4] + (1.0 - overall[0]) * overall[5]) / determinant
    return upper_state, lower_state


def upwind_terms(eigen, radius):
    forward = jnp.maximum(eigen, 0.0) + 0.25 * radius
    backward = jnp.maximum(-eigen, 0.0) + 0.25 * radius
    return forward, backward, 0.25 * radius


def cyclic_solve(source, eigen, radius):
    forward, backward, damping = upwind_terms(eigen, radius)
    along = source.ndim - 1
    affine = cell_maps(source, forward, damping, jnp.roll(forward, 1, -1), jnp.roll(damping, 2, -1))
    prefix = lax.associative_scan(compose, affine, axis=along)
    upper_state, lower_state = fixed_point(tuple(part[..., -1] for part in prefix))
    forward_part = apply_maps(prefix, upper_state[..., None], lower_state[..., None])
    affine = cell_maps(forward_part, backward, damping, jnp.roll(backward, -1, -1), jnp.roll(damping, -2, -1))
    prefix = lax.associative_scan(compose, affine, reverse=True, axis=along)
    upper_state, lower_state = fixed_point(tuple(part[..., 0] for part in prefix))
    return apply_maps(prefix, upper_state[..., None], lower_state[..., None])


def shift_zero(field, offset):
    along = field.ndim - 2
    length = field.shape[along]
    widths = [(0, 0)] * field.ndim
    if offset > 0:
        widths[along] = (offset, 0)
        padded = jnp.pad(field, widths)
        return lax.slice_in_dim(padded, 0, length, axis=along)
    widths[along] = (0, -offset)
    padded = jnp.pad(field, widths)
    return lax.slice_in_dim(padded, -offset, -offset + length, axis=along)


def open_solve(source, eigen, radius):
    forward, backward, damping = upwind_terms(eigen, radius)
    along = source.ndim - 2
    affine = cell_maps(source, forward, damping, shift_zero(forward, 1), shift_zero(damping, 2))
    prefix = lax.associative_scan(compose, affine, axis=along)
    forward_part = prefix[5]
    affine = cell_maps(forward_part, backward, damping, shift_zero(backward, -1), shift_zero(damping, -2))
    prefix = lax.associative_scan(compose, affine, reverse=True, axis=along)
    return prefix[5]


def advance(flow_state, speed_xi, sound_xi, speed_eta, sound_eta, coupling, left_vectors, middle_vectors, right_vectors):
    eigen_xi, radius_xi = speeds(speed_xi, sound_xi)
    eigen_eta, radius_eta = speeds(speed_eta, sound_eta)
    pressure = rotate(coupling, flow_state)
    flux_xi = speed_xi * flow_state + sound_xi * pressure
    flux_eta = speed_eta * flow_state + sound_eta * pressure
    central_xi = jnp.roll(flux_xi, -1, -1) - jnp.roll(flux_xi, 1, -1)
    central_eta = shift_zero(flux_eta, -1) - shift_zero(flux_eta, 1)
    fourth_xi = (jnp.roll(flow_state, -2, -1) - 4.0 * jnp.roll(flow_state, -1, -1) + 6.0 * flow_state
                 - 4.0 * jnp.roll(flow_state, 1, -1) + jnp.roll(flow_state, 2, -1))
    fourth_eta = (shift_zero(flow_state, -2) - 4.0 * shift_zero(flow_state, -1) + 6.0 * flow_state
                  - 4.0 * shift_zero(flow_state, 1) + shift_zero(flow_state, 2))
    residual = (-0.5 * central_xi - 0.5 * central_eta
                - DAMPING * radius_xi * fourth_xi - DAMPING * radius_eta * fourth_eta)
    rotated = rotate(left_vectors, residual)
    along_xi = cyclic_solve(rotated, eigen_xi, radius_xi)
    along_eta = open_solve(rotate(middle_vectors, along_xi), eigen_eta, radius_eta)
    increment = rotate(right_vectors, along_eta)
    return flow_state + increment, increment


def reference(flow_state, speed_xi, sound_xi, speed_eta, sound_eta, coupling, left_vectors, middle_vectors, right_vectors):
    def one_plane(inputs):
        current = inputs[0]
        increment = jnp.zeros_like(current)
        for section in range(STEPS):
            current, increment = advance(current, inputs[1], inputs[2], inputs[3], inputs[4],
                                         coupling, left_vectors, middle_vectors, right_vectors)
        return current, increment

    planes = (jnp.moveaxis(flow_state, 1, 0), speed_xi, sound_xi, speed_eta, sound_eta)
    final_state, increment = lax.map(one_plane, planes)
    return jnp.moveaxis(final_state, 0, 1), jnp.moveaxis(increment, 0, 1)
```

```python
import jax
import jax.numpy as jnp
from jax import lax
from jax.experimental import pallas as pl
from jax.experimental.pallas import tpu as pltpu
from jax.sharding import PartitionSpec as P


ROWS = 8
CELLS = 128
COMPS = 5
SPANS = (1, 2, 4, 8, 16, 32, 64)
SET_OF = (0, 0, 0, 1, 2)
SIGNS = (0.0, 1.0, -1.0)
DAMPING = 0.01
DYNAMIC = 16
TYPES = 32
F32 = jnp.float32


def lanes():
    return lax.broadcasted_iota(jnp.int32, (ROWS, CELLS), 1)


def subs():
    return lax.broadcasted_iota(jnp.int32, (ROWS, CELLS), 0)


def roll(x, shift, axis):
    size = x.shape[axis]
    return pltpu.roll(x, shift % size, axis)


def rot(matrix, fields):
    out = []
    for a in range(COMPS):
        total = matrix[a, 0] * fields[0]
        for b in range(1, COMPS):
            total = total + matrix[a, b] * fields[b]
        out.append(total)
    return out


def place(tile, source, cell, count, slot):
    lane = lanes()
    moved = roll(source, slot - cell, 1)
    return jnp.where((lane >= slot) & (lane < slot + count), moved, tile)


def chain_levels(near, far, sign):
    lane = lanes()
    one = jnp.ones_like(near)
    zero = jnp.zeros_like(near)
    m = (near, far, one, zero)
    levels = []
    for span in SPANS:
        keep = lane >= span if sign > 0 else lane < CELLS - span
        levels.append(tuple(jnp.where(keep, part, 0.0) for part in m))
        e = tuple(roll(part, sign * span, 1) for part in m)
        n = (
            m[0] * e[0] + m[1] * e[2],
            m[0] * e[1] + m[1] * e[3],
            m[2] * e[0] + m[3] * e[2],
            m[2] * e[1] + m[3] * e[3],
        )
        m = tuple(jnp.where(keep, a, b) for a, b in zip(n, m))
    return levels, m[0], m[1]


def sweep(levels, source, sign):
    upper = source
    lower = None
    for index, span in enumerate(SPANS):
        m = levels[index]
        ru = roll(upper, sign * span, 1)
        if lower is None:
            upper, lower = upper + m[0] * ru, m[2] * ru
            continue
        rl = roll(lower, sign * span, 1)
        fresh = upper + m[0] * ru + m[1] * rl
        if index < len(SPANS) - 1:
            lower = lower + m[2] * ru + m[3] * rl
        upper = fresh
    return upper


def level_slots(direction, family):
    base = (direction * 3 + family) * len(SPANS) * 4
    return [[base + level * 4 + part for part in range(4)] for level in range(len(SPANS))]


def needed(level, part):
    if level == 0:
        return part in (0, 2)
    if level == len(SPANS) - 1:
        return part in (0, 1)
    return True


def load_levels(lv, direction, family):
    return [
        [lv[slot] if needed(level, part) else None for part, slot in enumerate(row)]
        for level, row in enumerate(level_slots(direction, family))
    ]


COEF = 5


def xi_static_kernel(speed, sound, lv, resp, coef, pack):
    lane = lanes()
    u = speed[...]
    s = sound[...]
    damping = 0.25 * (jnp.abs(u) + s)
    damp_far = roll(damping, 2, 1)
    damp_far_back = roll(damping, -2, 1)
    for family in range(3):
        eigen = u + SIGNS[family] * s
        a = jnp.maximum(eigen, 0.0) + damping
        b = jnp.maximum(-eigen, 0.0) + damping
        da = 1.0 / (1.0 + a + damping)
        db = 1.0 / (1.0 + b + damping)
        near = jnp.where(lane == 0, 0.0, roll(a, 1, 1) * da)
        far = jnp.where(lane < 2, 1.0, damp_far) * da
        near_back = jnp.where(lane == CELLS - 1, 0.0, roll(b, -1, 1) * db)
        far_back = jnp.where(lane >= CELLS - 2, 1.0, damp_far_back) * db
        levels, y_w2, y_w1 = chain_levels(near, far, 1)
        back, z_x2, z_x1 = chain_levels(near_back, far_back, -1)
        for direction, group in ((0, levels), (1, back)):
            for level, row in enumerate(level_slots(direction, family)):
                for part, slot in enumerate(row):
                    if needed(level, part):
                        lv[slot] = group[level][part]
        z_w1 = sweep(back, db * y_w1, -1)
        z_w2 = sweep(back, db * y_w2, -1)
        for index, part in enumerate((z_w1, z_w2, z_x1, z_x2)):
            resp[family * 4 + index] = part
        for index, part in enumerate((a, b, damping, da, db)):
            coef[family * COEF + index] = part

        def fore(y):
            return (a * y + roll(damping * y, 1, 1), damping * y)

        def aft(z):
            return (b * z + roll(damping * z, -1, 1), damping * z)

        tile = jnp.zeros_like(u)
        f1, f2 = fore(y_w1), fore(y_w2)
        for slot, part in zip(range(10, 14), (f1[0], f2[0], f1[1], f2[1])):
            tile = place(tile, part, CELLS - 1, 1, slot)
        g1, g2 = aft(z_w1), aft(z_w2)
        for slot, part in zip(range(14, 18), (g1[0], g2[0], g1[1], g2[1])):
            tile = place(tile, part, 0, 1, slot)
        h1, h2 = aft(z_x1), aft(z_x2)
        for slot, part in zip(range(18, 22), (h1[0], h2[0], h1[1], h2[1])):
            tile = place(tile, part, 0, 1, slot)
        tile = place(tile, da, CELLS - 2, 2, 22)
        tile = place(tile, near, CELLS - 1, 1, 24)
        tile = place(tile, a, CELLS - 1, 1, 25)
        tile = place(tile, damping, CELLS - 2, 4, 26)
        pack[family] = tile


def halo_kernel(state, speed, sound, up, down):
    for f in range(7):
        source = state.at[f] if f < COMPS else (speed if f == COMPS else sound)
        up[2 * f : 2 * f + 2, :] = source[ROWS - 2 : ROWS, :]
        down[2 * f : 2 * f + 2, :] = source[0:2, :]
    up[14:16, :] = jnp.zeros((2, CELLS), F32)
    down[14:16, :] = jnp.zeros((2, CELLS), F32)


def residual_and_sweeps(q, hq, speeds, halo_speeds, coupling, left, lv, coef):
    lane = lanes()
    sub = subs()
    ux, sx, ue, se = speeds
    hu, hs = halo_speeds
    pressure = rot(coupling, q)
    hp = rot(coupling, hq)
    damp_x = DAMPING * (jnp.abs(ux) + sx)
    damp_e = DAMPING * (jnp.abs(ue) + se)
    residual = []
    flux = []
    for c in range(COMPS):
        fx = ux * q[c] + sx * pressure[c]
        fe = ue * q[c] + se * pressure[c]
        he = hu * hq[c] + hs * hp[c]
        flux.append(fx)

        def xi(x, offset):
            moved = roll(x, -offset, 1)
            inside = lane < CELLS - offset if offset > 0 else lane >= -offset
            return jnp.where(inside, moved, 0.0)

        def eta(x, h, offset):
            outer = sub < offset if offset > 0 else sub >= ROWS + offset
            return roll(jnp.where(outer, h, x), -offset, 0)

        central = (xi(fx, 1) - xi(fx, -1)) + (eta(fe, he, 1) - eta(fe, he, -1))
        fourth_x = xi(q[c], 2) - 4.0 * xi(q[c], 1) + 6.0 * q[c] - 4.0 * xi(q[c], -1) + xi(q[c], -2)
        fourth_e = (
            eta(q[c], hq[c], 2)
            - 4.0 * eta(q[c], hq[c], 1)
            + 6.0 * q[c]
            - 4.0 * eta(q[c], hq[c], -1)
            + eta(q[c], hq[c], -2)
        )
        residual.append(-0.5 * central - damp_x * fourth_x - damp_e * fourth_e)
    rotated = rot(left, residual)
    lq = rot(left, q)
    lf = rot(left, flux)
    ahead = [load_levels(lv, 0, family) for family in range(3)]
    back = [load_levels(lv, 1, family) for family in range(3)]
    z_local = []
    tiles = []
    for c in range(COMPS):
        family = SET_OF[c]
        a, b, g, da, db = (coef[family * COEF + k] for k in range(COEF))
        y = sweep(ahead[family], da * rotated[c], 1)
        z = sweep(back[family], db * y, -1)
        z_local.append(z)
        gy = g * y
        gz = g * z
        tile = jnp.zeros_like(y)
        tile = place(tile, a * y + roll(gy, 1, 1), CELLS - 1, 1, 0)
        tile = place(tile, gy, CELLS - 1, 1, 1)
        tile = place(tile, b * z + roll(gz, -1, 1), 0, 1, 2)
        tile = place(tile, gz, 0, 1, 3)
        tile = place(tile, lq[c], CELLS - 2, 4, 4)
        tile = place(tile, lf[c], CELLS - 1, 2, 8)
        tiles.append(tile)
    return z_local, tiles


def pack_lines(tiles, count):
    blank = jnp.zeros((CELLS - COMPS * ROWS, CELLS), F32)
    return jnp.transpose(jnp.concatenate(tiles + [blank], axis=0))[:count]


def first_kernel(
    state, ux, sx, ue, se, lo, hi, coupling, left, lv, coef, pack, z_out, halo_out, send
):
    zero = jnp.zeros((7, ROWS, CELLS), F32)
    halo_out[...] = zero
    for f in range(7):
        halo_out[f, ROWS - 2 : ROWS, :] = lo[2 * f : 2 * f + 2, :]
        halo_out[f, 0:2, :] = hi[2 * f : 2 * f + 2, :]
    q = [state[c] for c in range(COMPS)]
    hq = [halo_out[c] for c in range(COMPS)]
    z, tiles = residual_and_sweeps(
        q,
        hq,
        (ux[...], sx[...], ue[...], se[...]),
        (halo_out[5], halo_out[6]),
        coupling,
        left,
        lv,
        coef,
    )
    for c in range(COMPS):
        z_out[c] = z[c]
        tiles[c] = tiles[c] + pack[SET_OF[c]]
    packed = pack_lines(tiles, TYPES)
    for peer in range(send.shape[0]):
        send[peer] = packed


def xi_interface(dyn, stat):
    w1, w2, x1, x2 = (dyn(k) for k in range(4))
    lq126, lq127, lq0, lq1 = (dyn(k) for k in range(4, 8))
    lf127, lf0 = dyn(8), dyn(9)
    f11, f12, f21, f22 = (stat(k) for k in range(10, 14))
    g11, g12, g21, g22 = (stat(k) for k in range(14, 18))
    h11, h12, h21, h22 = (stat(k) for k in range(18, 22))
    d126, d127, near127, a127 = (stat(k) for k in range(22, 26))
    g126, g127, g0, g1 = (stat(k) for k in range(26, 30))

    def prev(x, by=1):
        return roll(x, by, 0)

    def after(x, by=1):
        return roll(x, -by, 0)

    damp = 4.0 * DAMPING
    r0 = 0.5 * prev(lf127) - damp * g0 * (prev(lq126) - 4.0 * prev(lq127))
    r1 = -damp * g1 * prev(lq127)
    r127 = -0.5 * after(lf0) - damp * g127 * (after(lq1) - 4.0 * after(lq0))
    r126 = -damp * g126 * after(lq0)
    y126 = d126 * r126
    y127 = d127 * r127 + near127 * y126
    w1 = w1 + a127 * y127 + g126 * y126
    w2 = w2 + g127 * y127
    in1, in2 = cyclic(
        (prev(f11), prev(f12), prev(f21), prev(f22)), prev(w1) + r0, prev(w2) + r1, prev
    )
    x1 = x1 + g11 * in1 + g12 * in2
    x2 = x2 + g21 * in1 + g22 * in2
    out1, out2 = cyclic(
        (after(h11), after(h12), after(h21), after(h22)), after(x1) + y127, after(x2) + y126, after
    )
    return in1, in2, out1, out2


def cyclic(m, c1, c2, shift):
    for span in (1, 2, 4):
        e = tuple(shift(part, span) for part in m)
        e1 = shift(c1, span)
        e2 = shift(c2, span)
        c1, c2 = c1 + m[0] * e1 + m[1] * e2, c2 + m[2] * e1 + m[3] * e2
        m = (
            m[0] * e[0] + m[1] * e[2],
            m[0] * e[1] + m[1] * e[3],
            m[2] * e[0] + m[3] * e[2],
            m[2] * e[1] + m[3] * e[3],
        )
    p = 1.0 - m[0]
    r = 1.0 - m[3]
    inverse = 1.0 / (p * r - m[1] * m[2])
    return (r * c1 + m[1] * c2) * inverse, (m[2] * c1 + p * c2) * inverse


def signs_by_sub():
    sub = subs()
    return jnp.where(sub == 3, 1.0, 0.0) - jnp.where(sub == 4, 1.0, 0.0)


def eta_coefs(u, s, sign):
    g = jnp.broadcast_to(0.25 * (jnp.abs(u) + s), (ROWS, CELLS))
    e = u + sign * s
    return jnp.maximum(e, 0.0) + g, jnp.maximum(-e, 0.0) + g, g


def eta_rows(own_u, own_s, low, high):
    sign = signs_by_sub()
    table = {}
    for j, (u, s) in zip((-2, -1), low):
        table[j] = eta_coefs(u, s, sign)
    for j in range(ROWS):
        table[j] = eta_coefs(own_u[j : j + 1, :], own_s[j : j + 1, :], sign)
    for j, (u, s) in zip((8, 9), high):
        table[j] = eta_coefs(u, s, sign)
    return table


def eta_ahead(table, source, y1, y2):
    y = {-1: y1, -2: y2}
    for j in range(ROWS):
        a, b, g = table[j]
        total = source[j] if source is not None else None
        if y[j - 1] is not None:
            term = table[j - 1][0] * y[j - 1]
            total = term if total is None else total + term
        if y[j - 2] is not None:
            term = table[j - 2][2] * y[j - 2]
            total = term if total is None else total + term
        y[j] = total if total is None else total * (1.0 / (1.0 + a + g))
    return y


def eta_back(table, y, z1, z2):
    z = {8: z1, 9: z2}
    for j in reversed(range(ROWS)):
        a, b, g = table[j]
        total = y[j] if y is not None else None
        if z[j + 1] is not None:
            term = table[j + 1][1] * z[j + 1]
            total = term if total is None else total + term
        if z[j + 2] is not None:
            term = table[j + 2][2] * z[j + 2]
            total = term if total is None else total + term
        z[j] = total if total is None else total * (1.0 / (1.0 + b + g))
    return z


def eta_static(table):
    one = jnp.ones((ROWS, CELLS), F32)
    y1 = eta_ahead(table, None, one, None)
    y2 = eta_ahead(table, None, None, one)
    return (
        y1,
        y2,
        eta_back(table, y1, None, None),
        eta_back(table, y2, None, None),
        eta_back(table, None, one, None),
        eta_back(table, None, None, one),
    )


def own_table(ue, se, halo):
    u = ue[...]
    s = se[...]
    hu = halo[5]
    hs = halo[6]
    low = [(hu[k : k + 1, :], hs[k : k + 1, :]) for k in (6, 7)]
    high = [(hu[k : k + 1, :], hs[k : k + 1, :]) for k in (0, 1)]
    return eta_rows(u, s, low, high)


def middle_kernel(recv, static_recv, resp, z_in, ue, se, halo, middle, zeta_out, send, scratch):
    step = recv.shape[0] // 8
    static_step = static_recv.shape[0] // 8

    def dyn(k):
        return recv[pl.ds(k, 8, stride=step), :]

    def stat(k):
        return static_recv[pl.ds(k, 8, stride=static_step), :]

    entering = xi_interface(dyn, stat)
    mine = subs() == lax.axis_index("xi")
    rows = [jnp.sum(jnp.where(mine, part, 0.0), axis=0, keepdims=True) for part in entering]
    square = jnp.concatenate(rows + [jnp.zeros((CELLS - 4, CELLS), F32)], axis=0)
    columns = jnp.transpose(square)
    z = []
    for c in range(COMPS):
        family = SET_OF[c]
        total = z_in[c]
        for k in range(4):
            total = total + resp[family * 4 + k] * columns[ROWS * c : ROWS * c + ROWS, k : k + 1]
        z.append(total)
    mixed = rot(middle, z)
    for c in range(COMPS):
        scratch[ROWS * c : ROWS * c + ROWS, :] = mixed[c]
    scratch[ROWS * COMPS : 64, :] = jnp.zeros((64 - ROWS * COMPS, CELLS), F32)
    source = [scratch[pl.ds(j, 8, stride=ROWS), :] for j in range(ROWS)]
    table = own_table(ue, se, halo)
    y = eta_ahead(table, source, None, None)
    z = eta_back(table, y, None, None)
    for j in range(ROWS):
        zeta_out[j] = z[j]
    sub = subs()
    t0, t1, t2, t3 = y[7], y[6], z[0], z[1]
    tiles = [
        jnp.where(sub < 5, t0, roll(t3, 5, 0)),
        jnp.where(sub < 5, t1, roll(t3, 2, 0)),
        t2,
    ]
    if send.shape[1] == 40:
        tiles = tiles + [ue[...], se[...]]
    for peer in range(send.shape[0]):
        for k, tile in enumerate(tiles):
            send[peer, ROWS * k : ROWS * k + ROWS, :] = tile


def eta_maps(recv, maps):
    count = recv.shape[0]
    for e in range(count):
        u = recv[e, 24:32, :]
        s = recv[e, 32:40, :]
        below = max(e - 1, 0)
        above = min(e + 1, count - 1)
        low = [(recv[below, 24 + k : 25 + k, :], recv[below, 32 + k : 33 + k, :]) for k in (6, 7)]
        high = [(recv[above, 24 + k : 25 + k, :], recv[above, 32 + k : 33 + k, :]) for k in (0, 1)]
        y1, y2, z1, z2, u1, u2 = eta_static(eta_rows(u, s, low, high))
        parts = (y1[7], y2[7], y1[6], y2[6], z1[0], z2[0], z1[1], z2[1], u1[0], u2[0], u1[1], u2[1])
        for k, part in enumerate(parts):
            maps[12 * e + k] = part


def eta_interface(recv, maps):
    count = recv.shape[0]
    sub = subs()
    me = lax.axis_index("eta")
    leaving = []
    for e in range(count):
        p0 = recv[e, 0:8, :]
        p1 = recv[e, 8:16, :]
        p2 = recv[e, 16:24, :]
        leaving.append((p0, p1, p2, jnp.where(sub < 3, roll(p0, 3, 0), roll(p1, -2, 0))))
    zero = jnp.zeros((ROWS, CELLS), F32)
    s1, s2 = zero, zero
    forward = []
    mine = [zero, zero, zero, zero]
    for e in range(count):
        forward.append((s1, s2))
        here = me == e
        mine[0] = jnp.where(here, s1, mine[0])
        mine[1] = jnp.where(here, s2, mine[1])
        m = [maps[12 * e + k] for k in range(4)]
        s1, s2 = (
            leaving[e][0] + m[0] * s1 + m[1] * s2,
            leaving[e][1] + m[2] * s1 + m[3] * s2,
        )
    t1, t2 = zero, zero
    for e in reversed(range(count)):
        here = me == e
        mine[2] = jnp.where(here, t1, mine[2])
        mine[3] = jnp.where(here, t2, mine[3])
        m = [maps[12 * e + k] for k in range(4, 12)]
        s1, s2 = forward[e]
        t1, t2 = (
            leaving[e][2] + m[0] * s1 + m[1] * s2 + m[4] * t1 + m[5] * t2,
            leaving[e][3] + m[2] * s1 + m[3] * s2 + m[6] * t1 + m[7] * t2,
        )
    return mine


def eta_solution(zeta, table, entering):
    s1, s2, t1, t2 = entering
    _, _, z1, z2, u1, u2 = eta_static(table)
    z = {}
    for j in range(ROWS):
        z[j] = zeta[j] + z1[j] * s1 + z2[j] * s2 + u1[j] * t1 + u2[j] * t2
    return z


def second_kernel(
    recv, zeta, state, ux, sx, ue, se, halo, coupling, left, right, lv, coef, state_out, z_out, halo_out, maps, send,
    scratch,
):
    eta_maps(recv, maps)
    entering = eta_interface(recv, maps)
    table = own_table(ue, se, halo)
    z = eta_solution(zeta, table, entering)
    s1, s2, t1, t2 = entering

    def back_from(j, source):
        a, b, g = table[j]
        return (source + table[j + 1][1] * z[j + 1] + table[j + 2][2] * z[j + 2]) / (1.0 + b + g)

    z[-1] = back_from(-1, s1)
    z[-2] = back_from(-2, s2)
    inside = lax.axis_index("eta") > 0
    for j in range(ROWS):
        scratch[ROWS * j : ROWS * j + ROWS, :] = z[j]
    for slot, part in ((0, t1), (1, t2), (6, z[-2]), (7, z[-1])):
        if slot > 1:
            part = jnp.where(inside, part, 0.0)
        scratch[64 + ROWS * slot : 72 + ROWS * slot, :] = part
    scratch[80:112, :] = jnp.zeros((32, CELLS), F32)
    own = [scratch[pl.ds(c, 8, stride=ROWS), :] for c in range(COMPS)]
    rim = [scratch[pl.ds(64 + c, 8, stride=ROWS), :] for c in range(COMPS)]
    own = rot(right, own)
    rim = rot(right, rim)
    q = []
    hq = []
    for c in range(COMPS):
        q.append(state[c] + own[c])
        hq.append(halo[c] + rim[c])
        state_out[c] = q[c]
    z, tiles = residual_and_sweeps(
        q,
        hq,
        (ux[...], sx[...], ue[...], se[...]),
        (halo[5], halo[6]),
        coupling,
        left,
        lv,
        coef,
    )
    for c in range(COMPS):
        z_out[c] = z[c]
        halo_out[c] = hq[c]
    for k in range(COMPS, 7):
        halo_out[k] = halo[k]
    packed = pack_lines(tiles, DYNAMIC)
    for peer in range(send.shape[0]):
        send[peer] = packed


def last_kernel(recv, zeta, state, ue, se, halo, right, maps, final, increment, scratch):
    entering = eta_interface(recv, maps)
    z = eta_solution(zeta, own_table(ue, se, halo), entering)
    for j in range(ROWS):
        scratch[ROWS * j : ROWS * j + ROWS, :] = z[j]
    own = rot(right, [scratch[pl.ds(c, 8, stride=ROWS), :] for c in range(COMPS)])
    for c in range(COMPS):
        increment[c] = own[c]
        final[c] = state[c] + own[c]


def tiles_of(*shape):
    return jax.ShapeDtypeStruct(shape + (ROWS, CELLS), F32)


def call(kernel, name, operands, matrices, outs, scratch=()):
    return pl.pallas_call(
        kernel,
        out_shape=outs,
        in_specs=[
            pl.BlockSpec(memory_space=pltpu.SMEM if k in matrices else pltpu.VMEM)
            for k in range(len(operands))
        ],
        out_specs=[pl.BlockSpec(memory_space=pltpu.VMEM) for _ in outs],
        scratch_shapes=list(scratch),
        compiler_params=pltpu.CompilerParams(vmem_limit_bytes=32 << 20),
        name=name,
    )(*operands)


def per_device(
    flow_state,
    speed_xi,
    sound_xi,
    speed_eta,
    sound_eta,
    coupling,
    left_vectors,
    middle_vectors,
    right_vectors,
):
    xi_count = lax.axis_size("xi")
    eta_count = lax.axis_size("eta")
    state = flow_state[:, 0]
    ux, sx, ue, se = (part[0] for part in (speed_xi, sound_xi, speed_eta, sound_eta))
    edge = jax.ShapeDtypeStruct((16, CELLS), F32)
    up, down = call(halo_kernel, "halo", (state, ue, se), (), [edge, edge])
    ahead = [(i, i + 1) for i in range(eta_count - 1)]
    lo = lax.ppermute(up, "eta", ahead)
    hi = lax.ppermute(down, "eta", [(b, a) for a, b in ahead])
    lv, resp, coef, pack = call(
        xi_static_kernel,
        "xi_static",
        (ux, sx),
        (),
        [tiles_of(6 * len(SPANS) * 4), tiles_of(12), tiles_of(3 * COEF), tiles_of(3)],
    )
    z_local, halo, send = call(
        first_kernel,
        "first",
        (state, ux, sx, ue, se, lo, hi, coupling, left_vectors, lv, coef, pack),
        (7, 8),
        [tiles_of(COMPS), tiles_of(7), jax.ShapeDtypeStruct((xi_count, TYPES, CELLS), F32)],
    )
    static = lax.all_to_all(send, "xi", 0, 0, tiled=True).reshape(xi_count * TYPES, CELLS)

    def middle(recv, z_local, halo, rows):
        return call(
            middle_kernel,
            "middle",
            (recv, static, resp, z_local, ue, se, halo, middle_vectors),
            (7,),
            [tiles_of(ROWS), jax.ShapeDtypeStruct((eta_count, rows, CELLS), F32)],
            [pltpu.VMEM((64, CELLS), F32)],
        )

    zeta, send = middle(static, z_local, halo, 40)
    recv = lax.all_to_all(send, "eta", 0, 0, tiled=True)
    state, z_local, halo, maps, send = call(
        second_kernel,
        "second",
        (recv, zeta, state, ux, sx, ue, se, halo, coupling, left_vectors, right_vectors, lv, coef),
        (8, 9, 10),
        [
            tiles_of(COMPS),
            tiles_of(COMPS),
            tiles_of(7),
            tiles_of(12 * eta_count),
            jax.ShapeDtypeStruct((xi_count, DYNAMIC, CELLS), F32),
        ],
        [pltpu.VMEM((128, CELLS), F32)],
    )
    recv = lax.all_to_all(send, "xi", 0, 0, tiled=True).reshape(xi_count * DYNAMIC, CELLS)
    zeta, send = middle(recv, z_local, halo, 24)
    recv = lax.all_to_all(send, "eta", 0, 0, tiled=True)
    final, increment = call(
        last_kernel,
        "last",
        (recv, zeta, state, ue, se, halo, right_vectors, maps),
        (6,),
        [tiles_of(COMPS), tiles_of(COMPS)],
        [pltpu.VMEM((64, CELLS), F32)],
    )
    return final[:, None], increment[:, None]


def solution(mesh):
    return jax.shard_map(
        per_device,
        mesh=mesh,
        in_specs=(
            P(None, None, "eta", "xi"),
            P(None, "eta", "xi"),
            P(None, "eta", "xi"),
            P(None, "eta", "xi"),
            P(None, "eta", "xi"),
            P(),
            P(),
            P(),
            P(),
        ),
        out_specs=(P(None, None, "eta", "xi"), P(None, None, "eta", "xi")),
        check_vma=False,
    )
```

```python
import jax
import jax.numpy as jnp
from jax import lax
from jax.experimental import pallas as pl
from jax.experimental.pallas import tpu as pltpu
from jax.sharding import PartitionSpec as P


ROWS = 8
CELLS = 128
COMPS = 5
DAMPING = 0.01
GROUPS = 16
LINES = GROUPS * ROWS
FIELDS = 9
DYNAMIC = 56
STATIC = 48
STATS = 20
F32 = jnp.float32
COUPLING, LEFT, MIDDLE, RIGHT = range(4)
A, B, D, BACK_A, BACK_B, BACK_D = range(6)


def lanes():
    return lax.broadcasted_iota(jnp.int32, (ROWS, CELLS), 1)


def subs():
    return lax.broadcasted_iota(jnp.int32, (ROWS, CELLS), 0)


def roll(x, shift, axis):
    return pltpu.roll(x, shift % x.shape[axis], axis)


def rot(splat, which, fields):
    out = []
    for a in range(COMPS):
        total = splat[25 * which + 5 * a] * fields[0]
        for b in range(1, COMPS):
            total = total + splat[25 * which + 5 * a + b] * fields[b]
        out.append(total)
    return out


def place(tile, source, cell, count, slot):
    lane = lanes()
    moved = roll(source, slot - cell, 1)
    return jnp.where((lane >= slot) & (lane < slot + count), moved, tile)


def spread(row):
    return jnp.broadcast_to(row, (ROWS, CELLS))


def signs():
    sub = subs()
    return jnp.where(sub == 3, 1.0, 0.0) - jnp.where(sub == 4, 1.0, 0.0)


def upwind(u, s, sign):
    g = 0.25 * (jnp.abs(u) + s)
    e = u + sign * s
    return jnp.maximum(e, 0.0) + g, jnp.maximum(-e, 0.0) + g, g


def pack_kernel(
    state, ux, sx, ue, se, coupling, left, middle, right, send, tile_out, block, tile, m0, m1, m2, m3, sem
):
    fields = [pltpu.make_async_copy(state, block.at[0:COMPS], sem.at[0])]
    for k, source in enumerate((ux, sx, ue, se)):
        fields.append(pltpu.make_async_copy(source, block.at[COMPS + k], sem.at[1 + k]))
    scalars = (m0, m1, m2, m3)
    matrices = [
        pltpu.make_async_copy(source, scalars[k], sem.at[5 + k])
        for k, source in enumerate((coupling, left, middle, right))
    ]
    for copy in fields + matrices:
        copy.start()
    for copy in fields:
        copy.wait()
    out = [pltpu.make_async_copy(block, send.at[p], sem.at[9 + p]) for p in range(send.shape[0])]
    for copy in out:
        copy.start()
    for copy in matrices:
        copy.wait()
    lane = lanes()
    sub = subs()
    total = jnp.zeros((ROWS, CELLS), F32)
    for which, matrix in enumerate(scalars):
        row = jnp.zeros((ROWS, CELLS), F32)
        for a in range(COMPS):
            for b in range(COMPS):
                row = jnp.where(lane == COMPS * a + b, matrix[a, b], row)
        total = jnp.where(sub == which, row, total)
    tile[...] = total
    last = pltpu.make_async_copy(tile, tile_out, sem.at[9 + len(out)])
    last.start()
    for copy in out:
        copy.wait()
    last.wait()


def spread_matrices(tile, splat, lcol):
    sub = subs()
    for which in range(4):
        for n in range(COMPS * COMPS):
            splat[25 * which + n] = jnp.broadcast_to(tile[which : which + 1, n : n + 1], (ROWS, CELLS))
    for b in range(COMPS):
        column = jnp.zeros((ROWS, CELLS), F32)
        for a in range(COMPS):
            column = jnp.where(sub == a, splat[25 * LEFT + COMPS * a + b], column)
        lcol[b] = column


def line_coefs(u_block, s_block, out):
    sign = signs()
    zero = u_block(0) * 0.0

    def body(k, carry):
        a1, g1, g2, d1, d2 = carry
        ub = u_block(k)
        sb = s_block(k)
        for r in range(ROWS):
            i = k * ROWS + r
            a, b, g = upwind(spread(ub[r : r + 1, :]), spread(sb[r : r + 1, :]), sign)
            da = 1.0 / (1.0 + a + g)
            db = 1.0 / (1.0 + b + g)
            out[A, i] = a1 * da
            out[B, i] = g2 * da
            out[D, i] = da
            out[BACK_D, i + 2] = db
            out[BACK_A, i + 1] = b * d1
            out[BACK_B, i] = g * d2
            a1, g1, g2, d1, d2 = a, g, g1, db, d1
        return a1, g1, g2, d1, d2

    lax.fori_loop(0, GROUPS, body, (zero,) * 5)
    out[BACK_A, LINES + 1] = zero
    out[BACK_B, LINES] = zero
    out[BACK_B, LINES + 1] = zero


def at(i):
    return pl.ds(pl.multiple_of(i * ROWS, ROWS), ROWS)


def fluxes(qp, recv, splat, fx_scr, fe_scr):
    def body(k, carry):
        q = [qp[c, k + 1] for c in range(COMPS)]
        ux, sx, ue, se = (recv[k, 5 + f] for f in range(4))
        p = rot(splat, COUPLING, q)
        for c in range(COMPS):
            fx_scr[c, k] = ux * q[c] + sx * p[c]
            fe_scr[c, k + 1] = ue * q[c] + se * p[c]
        return carry

    lax.fori_loop(0, GROUPS, body, 0, unroll=2)


def residuals(qp, recv, splat, fx_scr, fe_scr, rot_scr, edge_scr):
    lane = lanes()
    sub = subs()
    for scr in (qp, fe_scr):
        for c in range(COMPS):
            scr[c, 0] = jnp.zeros((ROWS, CELLS), F32)
            scr[c, GROUPS + 1] = jnp.zeros((ROWS, CELLS), F32)

    def xi(x, offset):
        inside = lane < CELLS - offset if offset > 0 else lane >= -offset
        return jnp.where(inside, roll(x, -offset, 1), 0.0)

    def eta(scr, c, k, offset):
        if offset > 0:
            joined = jnp.where(sub < offset, scr[c, k + 2], scr[c, k + 1])
        else:
            joined = jnp.where(sub >= ROWS + offset, scr[c, k], scr[c, k + 1])
        return roll(joined, -offset, 0)

    def body(k, carry):
        ux, sx, ue, se = (recv[k, 5 + f] for f in range(4))
        damp_x = DAMPING * (jnp.abs(ux) + sx)
        damp_e = DAMPING * (jnp.abs(ue) + se)
        edge = jnp.zeros((ROWS, CELLS), F32)
        residual = []
        for c in range(COMPS):
            q = qp[c, k + 1]
            fx = fx_scr[c, k]
            central = (xi(fx, 1) - xi(fx, -1)) + (eta(fe_scr, c, k, 1) - eta(fe_scr, c, k, -1))
            q6 = 6.0 * q
            fourth_x = (xi(q, 2) + xi(q, -2)) - 4.0 * (xi(q, 1) + xi(q, -1)) + q6
            fourth_e = (
                (eta(qp, c, k, 2) + eta(qp, c, k, -2))
                - 4.0 * (eta(qp, c, k, 1) + eta(qp, c, k, -1))
                + q6
            )
            residual.append(-0.5 * central - damp_x * fourth_x - damp_e * fourth_e)
            edge = place(edge, q, CELLS - 2, 4, 4 * c)
            edge = place(edge, fx, CELLS - 1, 2, 20 + 2 * c)
        for c, part in enumerate(rot(splat, LEFT, residual)):
            rot_scr[c, at(k), :] = part
        edge_scr[at(k), :] = edge
        return carry

    lax.fori_loop(0, GROUPS, body, 0, unroll=2)


def to_lines(cells, out):
    for c in range(COMPS):
        out[pl.ds(c, LINES, stride=ROWS), :] = jnp.transpose(cells[c])


def blank_lines(out):
    zero = jnp.zeros((ROWS, CELLS), F32)
    for i in range(LINES):
        out[ROWS * i : ROWS * i + ROWS, :] = zero


def edge_types(edge_scr, lcol):
    turned = jnp.transpose(edge_scr[...])
    columns = [lcol[b] for b in range(COMPS)]

    def mix(base, stride):
        total = columns[0] * spread(turned[base : base + 1, :])
        for b in range(1, COMPS):
            row = base + stride * b
            total = total + columns[b] * spread(turned[row : row + 1, :])
        return total

    return [mix(k, 4) for k in range(4)] + [mix(20 + k, 2) for k in range(2)]


def ahead_step(coef, source, i, y1, y2):
    return coef[A, i] * y1 + (coef[D, i] * source + coef[B, i] * y2)


def back_step(coef, source, i, z1, z2):
    return coef[BACK_A, i + 2] * z1 + (coef[BACK_D, i + 2] * source + coef[BACK_B, i + 2] * z2)


def ahead(coef, lines, start=0, state=None):
    if state is None:
        zero = coef[D, 0] * 0.0
        state = (zero, zero)

    def body(i, carry):
        y1, y2 = carry
        y = ahead_step(coef, lines[at(i), :], i, y1, y2)
        lines[at(i), :] = y
        return y, y1

    return lax.fori_loop(start, LINES, body, state, unroll=8)


def back(coef, lines, out):
    zero = coef[D, 0] * 0.0

    def body(k, carry):
        i = LINES - 1 - k
        z1, z2 = carry
        z = back_step(coef, lines[at(i), :], i, z1, z2)
        out[at(i), :] = z
        return z, z1

    return lax.fori_loop(0, LINES, body, (zero, zero), unroll=8)


def dynamic_tiles(y127, y126, z0, z1, ends, types):
    a127, b0, g126, g127, g0, g1 = ends
    lq126, lq127, lq0, lq1, lf127, lf0 = types
    full = [a127 * y127 + g126 * y126, g127 * y127, b0 * z0 + g1 * z1, g0 * z0, lq126, lq127, lq0]
    sub = subs()
    for k, extra in enumerate((lq1, lf127, lf0)):
        full[2 * k] = jnp.where(sub < COMPS, full[2 * k], roll(extra, 5, 0))
        full[2 * k + 1] = jnp.where(sub < COMPS, full[2 * k + 1], roll(extra, 2, 0))
    return full


def block_ends(turned_u, turned_s):
    sign = signs()

    def cell(i):
        return upwind(spread(turned_u[i : i + 1, :]), spread(turned_s[i : i + 1, :]), sign)

    a127, _, g127 = cell(CELLS - 1)
    _, _, g126 = cell(CELLS - 2)
    _, b0, g0 = cell(0)
    _, _, g1 = cell(1)
    return a127, b0, g126, g127, g0, g1


def broadcast_tiles(send, tiles):
    for peer in range(send.shape[0]):
        for k, tile in enumerate(tiles):
            send[peer, ROWS * k : ROWS * k + ROWS, :] = tile


def first_kernel(
    mine, other, matrices, z_out, resp, coef, ends_out, splat, lcol, recv, send,
    qp, fx_scr, fe_scr, rot_scr, edge_scr, turned_u, turned_s, lines, y_w1, y_w2,
):
    spread_matrices(matrices[...], splat, lcol)
    core = lax.rem(lax.axis_index("eta"), 2)
    for k in range(GROUPS // 2):
        for f in range(FIELDS):
            recv[2 * k + core, f] = mine[k, f]
            recv[2 * k + 1 - core, f] = other[k, f]
    for source, target in ((5, turned_u), (6, turned_s)):
        for k in range(GROUPS):
            edge_scr[ROWS * k : ROWS * k + ROWS, :] = recv[k, source]
        target[...] = jnp.transpose(edge_scr[...])
    line_coefs(lambda k: turned_u[at(k), :], lambda k: turned_s[at(k), :], coef)
    for k in range(GROUPS):
        for c in range(COMPS):
            qp[c, k + 1] = recv[k, c]
    fluxes(qp, recv, splat, fx_scr, fe_scr)
    residuals(qp, recv, splat, fx_scr, fe_scr, rot_scr, edge_scr)
    types = edge_types(edge_scr, lcol)
    blank_lines(lines)
    to_lines(rot_scr, lines)

    zero = coef[D, 0] * 0.0
    y0 = coef[D, 0] * lines[0:ROWS, :]
    y1 = ahead_step(coef, lines[ROWS : 2 * ROWS, :], 1, y0, zero)
    p0 = coef[D, 0]
    p1 = coef[A, 1] * p0
    q1 = coef[D, 1]
    for ref, first, second in ((lines, y0, y1), (y_w1, p0, p1), (y_w2, zero, q1)):
        ref[0:ROWS, :] = first
        ref[ROWS : 2 * ROWS, :] = second

    def forward(i, carry):
        y1, y2, p1, p2, q1, q2 = carry
        near = coef[A, i]
        far = coef[B, i]
        y = near * y1 + (coef[D, i] * lines[at(i), :] + far * y2)
        p = near * p1 + far * p2
        q = near * q1 + far * q2
        lines[at(i), :] = y
        y_w1[at(i), :] = p
        y_w2[at(i), :] = q
        return y, y1, p, p1, q, q1

    y127, y126, p127, p126, q127, q126 = lax.fori_loop(
        2, LINES, forward, (y1, y0, p1, p0, q1, zero), unroll=7
    )

    def reverse(i, carry, last=None):
        z1, z2, p1, p2, q1, q2, u1, u2, v1, v2 = carry
        near = coef[BACK_A, i + 2]
        far = coef[BACK_B, i + 2]
        d = coef[BACK_D, i + 2]
        z = near * z1 + (d * lines[at(i), :] + far * z2)
        p = near * p1 + (d * y_w1[at(i), :] + far * p2)
        q = near * q1 + (d * y_w2[at(i), :] + far * q2)
        if last == 0:
            u, v = d, zero
        elif last == 1:
            u, v = near * u1, d
        else:
            u = near * u1 + far * u2
            v = near * v1 + far * v2
        z_out[at(i), :] = z
        for k, part in enumerate((p, q, u, v)):
            resp[k, at(i), :] = part
        return z, z1, p, p1, q, q1, u, u1, v, v1

    carry = (zero,) * 10
    carry = reverse(LINES - 1, carry, 0)
    carry = reverse(LINES - 2, carry, 1)
    carry = lax.fori_loop(0, LINES - 2, lambda k, x: reverse(LINES - 3 - k, x), carry, unroll=7)
    z0, z1, zp0, zp1, zq0, zq1, zu0, zu1, zv0, zv1 = carry

    ends = block_ends(turned_u, turned_s)
    a127, b0, g126, g127, g0, g1 = ends
    for k, part in enumerate(ends):
        ends_out[k] = part
    tiles = dynamic_tiles(y127, y126, z0, z1, ends, types)

    def fore(last, before):
        return a127 * last + g126 * before, g127 * last

    def aft(first, second):
        return b0 * first + g1 * second, g0 * first

    f1, f2 = fore(p127, p126), fore(q127, q126)
    g1_, g2_ = aft(zp0, zp1), aft(zq0, zq1)
    h1, h2 = aft(zu0, zu1), aft(zv0, zv1)
    sub = subs()
    raw = []
    for ref in (turned_u, turned_s):
        for i in (CELLS - 2, 0):
            raw.append(jnp.where(sub == 0, spread(ref[i : i + 1, :]), spread(ref[i + 1 : i + 2, :])))
    for one, two in ((f1, f2), (g1_, g2_), (h1, h2)):
        for k in range(2):
            tile = jnp.where(sub < COMPS, one[k], roll(two[k], 3, 0))
            if raw:
                tile = jnp.where(sub < 2, raw.pop(0), tile)
            tiles.append(tile)
    broadcast_tiles(send, tiles)


def solve_point(m, c1, c2):
    p = 1.0 - m[0]
    r = 1.0 - m[3]
    inverse = 1.0 / (p * r - m[1] * m[2])
    return (r * c1 + m[1] * c2) * inverse, (m[2] * c1 + p * c2) * inverse


def apply(m, x1, x2):
    return m[0] * x1 + m[1] * x2, m[2] * x1 + m[3] * x2


def after_map(f, m, c1, c2):
    product = (
        f[0] * m[0] + f[1] * m[2],
        f[0] * m[1] + f[1] * m[3],
        f[2] * m[0] + f[3] * m[2],
        f[2] * m[1] + f[3] * m[3],
    )
    c1, c2 = apply(f, c1, c2)
    return product, c1, c2


def unpack_static(recv, device, stats, slot):
    sub = subs()
    sign = signs()

    def sets(tile):
        return jnp.where(sub < 2, spread(tile[2:3, :]), tile)

    raw = []
    for k in range(6):
        tile = recv[device, DYNAMIC + ROWS * k : DYNAMIC + ROWS * k + ROWS, :]
        base = 4 * (k // 2) + 2 * (k % 2)
        stats[STATS * slot + base] = sets(tile)
        stats[STATS * slot + base + 1] = sets(roll(tile, -3, 0))
        if k < 4:
            raw += [spread(tile[0:1, :]), spread(tile[1:2, :])]
    cell = [upwind(raw[k], raw[k + 4], sign) for k in range(4)]
    a126, _, g126 = cell[0]
    a127, _, g127 = cell[1]
    parts = (
        1.0 / (1.0 + a126 + g126),
        1.0 / (1.0 + a127 + g127),
        a126,
        a127,
        g126,
        g127,
        cell[2][2],
        cell[3][2],
    )
    for k, part in enumerate(parts):
        stats[STATS * slot + 12 + k] = part


def entering(recv, stats, me):
    count = recv.shape[0]
    sub = subs()
    types = []
    for k in range(count):
        device = lax.rem(me + k, count)
        t = [recv[device, ROWS * n : ROWS * n + ROWS, :] for n in range(7)]
        for n in range(3):
            t.append(jnp.where(sub < 3, roll(t[2 * n], 3, 0), roll(t[2 * n + 1], -2, 0)))
        types.append(t)
    damp = 4.0 * DAMPING
    inward, inback, outward = [], [], []
    for k in range(count):
        d126, d127, a126, a127, g126, g127, g0, g1 = (
            stats[STATS * k + 12 + n] for n in range(8)
        )
        before = types[k - 1]
        later = types[(k + 1) % count]
        r0 = 0.5 * before[8] - damp * g0 * (before[4] - 4.0 * before[5])
        r1 = -damp * g1 * before[5]
        r127 = -0.5 * later[9] - damp * g127 * (later[7] - 4.0 * later[6])
        r126 = -damp * g126 * later[6]
        y126 = d126 * r126
        y127 = d127 * (r127 + a126 * y126)
        inward.append((r0, r1))
        inback.append((y127, y126))
        w1, w2 = types[k][0:2]
        outward.append((w1 + a127 * y127 + g126 * y126, w2 + g127 * y127))

    def maps(k, base):
        return [stats[STATS * k + base + n] for n in range(4)]

    m = None
    for k in range(count):
        f = maps(k, 0)
        if m is None:
            m, c1, c2 = f, outward[k][0], outward[k][1]
        else:
            m, c1, c2 = after_map(f, m, c1, c2)
            c1, c2 = c1 + outward[k][0], c2 + outward[k][1]
        nxt = inward[(k + 1) % count]
        c1, c2 = c1 + nxt[0], c2 + nxt[1]
    w = [solve_point(m, c1, c2)]
    for k in range(count - 1):
        n1, n2 = apply(maps(k, 0), *w[k])
        nxt = inward[k + 1]
        w.append((n1 + outward[k][0] + nxt[0], n2 + outward[k][1] + nxt[1]))
    m = None
    for k in [0] + list(range(count - 1, 0, -1)):
        h = maps(k, 8)
        s1, s2 = apply(maps(k, 4), *w[k])
        s1, s2 = s1 + types[k][2], s2 + types[k][3]
        if m is None:
            m, c1, c2 = h, s1, s2
        else:
            m, c1, c2 = after_map(h, m, c1, c2)
            c1, c2 = c1 + s1, c2 + s2
        nxt = inback[(k - 1) % count]
        c1, c2 = c1 + nxt[0], c2 + nxt[1]
    x = solve_point(m, c1, c2)
    return w[0] + x


def eta_solve(z_in, resp, enter, splat, eta_coef, lines, rot_scr):
    def correct(i, carry):
        total = z_in[at(i), :]
        for k in range(4):
            total = total + resp[k, at(i), :] * enter[k]
        lines[at(i), :] = total
        return carry

    lax.fori_loop(0, LINES, correct, 0, unroll=8)
    for k in range(GROUPS):
        z = [lines[pl.ds(64 * k + c, ROWS, stride=ROWS), :] for c in range(COMPS)]
        for c, part in enumerate(rot(splat, MIDDLE, z)):
            rot_scr[c, ROWS * k : ROWS * k + ROWS, :] = part
    to_lines(rot_scr, lines)
    ahead(eta_coef, lines)
    back(eta_coef, lines, lines)


def second_kernel(
    recv, z_in, resp, raw, splat, lcol, coef, ends, z_out, own, stats, eta_coef, send,
    qp, fx_scr, fe_scr, rot_scr, edge_scr, lines,
):
    me = lax.axis_index("xi")
    line_coefs(lambda k: raw[k, 7], lambda k: raw[k, 8], eta_coef)
    for k in range(recv.shape[0]):
        unpack_static(recv, lax.rem(me + k, recv.shape[0]), stats, k)
    enter = entering(recv, stats, me)
    eta_solve(z_in, resp, enter, splat, eta_coef, lines, rot_scr)
    for k in range(GROUPS):
        z = [lines[pl.ds(64 * k + c, ROWS, stride=ROWS), :] for c in range(COMPS)]
        for c, part in enumerate(rot(splat, RIGHT, z)):
            qp[c, k + 1] = raw[k, c] + part
    row = lax.axis_index("eta")
    for c in range(COMPS):
        own[c] = qp[c, row + 1]
    fluxes(qp, raw, splat, fx_scr, fe_scr)
    residuals(qp, raw, splat, fx_scr, fe_scr, rot_scr, edge_scr)
    types = edge_types(edge_scr, lcol)
    to_lines(rot_scr, lines)
    y127, y126 = ahead(coef, lines)
    z0, z1 = back(coef, lines, z_out)
    tiles = dynamic_tiles(y127, y126, z0, z1, [ends[k] for k in range(6)], types)
    broadcast_tiles(send, tiles)


def last_kernel(
    recv, z_in, resp, splat, eta_coef, own, stats, final, increment, rot_scr, lines, few
):
    enter = entering(recv, stats, lax.axis_index("xi"))
    eta_solve(z_in, resp, enter, splat, eta_coef, lines, rot_scr)
    row = lax.axis_index("eta")
    for j in range(ROWS):
        few[ROWS * j : ROWS * j + ROWS, :] = lines[at(row * ROWS + j), :]
    z = [few[pl.ds(c, ROWS, stride=ROWS), :] for c in range(COMPS)]
    for c, part in enumerate(rot(splat, RIGHT, z)):
        increment[c] = part
        final[c] = own[c] + part


def array(*shape):
    return jax.ShapeDtypeStruct(shape, F32)


def vmem(*shape):
    return pltpu.VMEM(shape, F32)


def call(kernel, name, operands, outs, scratch=()):
    return pl.pallas_call(
        kernel,
        out_shape=outs,
        in_specs=[pl.BlockSpec(memory_space=pltpu.VMEM) for _ in operands],
        out_specs=[pl.BlockSpec(memory_space=pltpu.VMEM) for _ in outs],
        scratch_shapes=list(scratch),
        compiler_params=pltpu.CompilerParams(vmem_limit_bytes=16 << 20),
        name=name,
    )(*operands)


def cell_scratch():
    return [
        vmem(COMPS, GROUPS + 2, ROWS, CELLS),
        vmem(COMPS, GROUPS, ROWS, CELLS),
        vmem(COMPS, GROUPS + 2, ROWS, CELLS),
        vmem(COMPS, LINES, CELLS),
        vmem(LINES, CELLS),
    ]


def per_device(
    flow_state,
    speed_xi,
    sound_xi,
    speed_eta,
    sound_eta,
    coupling,
    left_vectors,
    middle_vectors,
    right_vectors,
):
    xi_count = lax.axis_size("xi")
    flat = ROWS * LINES
    send, matrices = pl.pallas_call(
        pack_kernel,
        out_shape=[array(GROUPS // 2, FIELDS, ROWS, CELLS), array(ROWS, CELLS)],
        in_specs=[pl.BlockSpec(memory_space=pltpu.HBM)] * 9,
        out_specs=[pl.BlockSpec(memory_space=pltpu.HBM)] * 2,
        scratch_shapes=[vmem(FIELDS, ROWS, CELLS), vmem(ROWS, CELLS)]
        + [pltpu.SMEM((COMPS, COMPS), F32)] * 4
        + [pltpu.SemaphoreType.DMA((10 + GROUPS // 2,))],
        compiler_params=pltpu.CompilerParams(vmem_limit_bytes=60 << 20),
        name="pack",
    )(
        flow_state[:, 0],
        speed_xi[0],
        sound_xi[0],
        speed_eta[0],
        sound_eta[0],
        coupling,
        left_vectors,
        middle_vectors,
        right_vectors,
    )
    groups = [[2 * k + core for k in range(GROUPS // 2)] for core in range(2)]
    mine = lax.all_to_all(send, "eta", 0, 0, axis_index_groups=groups, tiled=True)
    other = lax.ppermute(mine, "eta", [(k, k ^ 1) for k in range(GROUPS)])
    z_local, resp, coef, ends, splat, lcol, raw, send = call(
        first_kernel,
        "first",
        (mine, other, matrices),
        [
            array(flat, CELLS),
            array(4, flat, CELLS),
            array(6, LINES + 2, ROWS, CELLS),
            array(6, ROWS, CELLS),
            array(100, ROWS, CELLS),
            array(COMPS, ROWS, CELLS),
            array(GROUPS, FIELDS, ROWS, CELLS),
            array(xi_count, DYNAMIC + STATIC, CELLS),
        ],
        cell_scratch()
        + [vmem(LINES, CELLS), vmem(LINES, CELLS), vmem(flat, CELLS), vmem(flat, CELLS), vmem(flat, CELLS)],
    )
    recv = lax.all_to_all(send, "xi", 0, 0, tiled=True)
    z_local, own, stats, eta_coef, send = call(
        second_kernel,
        "second",
        (recv, z_local, resp, raw, splat, lcol, coef, ends),
        [
            array(flat, CELLS),
            array(COMPS, ROWS, CELLS),
            array(STATS * xi_count, ROWS, CELLS),
            array(6, LINES + 2, ROWS, CELLS),
            array(xi_count, DYNAMIC, CELLS),
        ],
        cell_scratch() + [vmem(flat, CELLS)],
    )
    recv = lax.all_to_all(send, "xi", 0, 0, tiled=True)
    final, increment = call(
        last_kernel,
        "last",
        (recv, z_local, resp, splat, eta_coef, own, stats),
        [array(COMPS, ROWS, CELLS), array(COMPS, ROWS, CELLS)],
        [vmem(COMPS, LINES, CELLS), vmem(flat, CELLS), vmem(ROWS * ROWS, CELLS)],
    )
    return final[:, None], increment[:, None]


def solution(mesh):
    return jax.shard_map(
        per_device,
        mesh=mesh,
        in_specs=(
            P(None, None, "eta", "xi"),
            P(None, "eta", "xi"),
            P(None, "eta", "xi"),
            P(None, "eta", "xi"),
            P(None, "eta", "xi"),
            P(),
            P(),
            P(),
            P(),
        ),
        out_specs=(P(None, None, "eta", "xi"), P(None, None, "eta", "xi")),
        check_vma=False,
    )
```

```python
import jax
import jax.numpy as jnp
from jax import lax
from jax.experimental import pallas as pl
from jax.experimental.pallas import tpu as pltpu
from jax.sharding import PartitionSpec as P


ROWS = 8
CELLS = 128
COMPS = 5
DAMPING = 0.01
GROUPS = 16
LINES = GROUPS * ROWS
FIELDS = 9
DYNAMIC = 56
STATS = 20
F32 = jnp.float32
COUPLING, LEFT, MIDDLE, RIGHT = range(4)
A, B, D, BACK_A, BACK_B, BACK_D = range(6)


def lanes():
    return lax.broadcasted_iota(jnp.int32, (ROWS, CELLS), 1)


def subs():
    return lax.broadcasted_iota(jnp.int32, (ROWS, CELLS), 0)


def roll(x, shift, axis):
    return pltpu.roll(x, shift % x.shape[axis], axis)


def rot(splat, which, fields):
    out = []
    for a in range(COMPS):
        total = splat[25 * which + 5 * a] * fields[0]
        for b in range(1, COMPS):
            total = total + splat[25 * which + 5 * a + b] * fields[b]
        out.append(total)
    return out


def place(tile, source, cell, count, slot):
    lane = lanes()
    moved = roll(source, slot - cell, 1)
    return jnp.where((lane >= slot) & (lane < slot + count), moved, tile)


def spread(row):
    return jnp.broadcast_to(row, (ROWS, CELLS))


def signs():
    sub = subs()
    return jnp.where(sub == 3, 1.0, 0.0) - jnp.where(sub == 4, 1.0, 0.0)


def upwind(u, s, sign):
    g = 0.25 * (jnp.abs(u) + s)
    e = u + sign * s
    return jnp.maximum(e, 0.0) + g, jnp.maximum(-e, 0.0) + g, g


def pack_kernel(
    state, ux, sx, ue, se, coupling, left, middle, right, send, tile_out, block, tile, m0, m1, m2, m3, sem
):
    fields = [pltpu.make_async_copy(state, block.at[0:COMPS], sem.at[0])]
    for k, source in enumerate((ux, sx, ue, se)):
        fields.append(pltpu.make_async_copy(source, block.at[COMPS + k], sem.at[1 + k]))
    scalars = (m0, m1, m2, m3)
    matrices = [
        pltpu.make_async_copy(source, scalars[k], sem.at[5 + k])
        for k, source in enumerate((coupling, left, middle, right))
    ]
    for copy in fields + matrices:
        copy.start()
    for copy in fields:
        copy.wait()
    out = [pltpu.make_async_copy(block, send.at[p], sem.at[9 + p]) for p in range(send.shape[0])]
    for copy in out:
        copy.start()
    for copy in matrices:
        copy.wait()
    lane = lanes()
    sub = subs()
    total = jnp.zeros((ROWS, CELLS), F32)
    for which, matrix in enumerate(scalars):
        row = jnp.zeros((ROWS, CELLS), F32)
        for a in range(COMPS):
            for b in range(COMPS):
                row = jnp.where(lane == COMPS * a + b, matrix[a, b], row)
        total = jnp.where(sub == which, row, total)
    tile[...] = total
    last = pltpu.make_async_copy(tile, tile_out, sem.at[9 + len(out)])
    last.start()
    for copy in out:
        copy.wait()
    last.wait()


def splat_kernel(tile_ref, splat, lcol):
    tile = tile_ref[...]
    sub = subs()
    for which in range(4):
        for n in range(COMPS * COMPS):
            splat[25 * which + n] = jnp.broadcast_to(tile[which : which + 1, n : n + 1], (ROWS, CELLS))
    for b in range(COMPS):
        column = jnp.zeros((ROWS, CELLS), F32)
        for a in range(COMPS):
            column = jnp.where(sub == a, splat[25 * LEFT + COMPS * a + b], column)
        lcol[b] = column


def line_coefs(u_block, s_block, out):
    sign = signs()
    zero = u_block(0) * 0.0

    def body(k, carry):
        a1, g1, g2, d1, d2 = carry
        ub = u_block(k)
        sb = s_block(k)
        for r in range(ROWS):
            i = k * ROWS + r
            a, b, g = upwind(spread(ub[r : r + 1, :]), spread(sb[r : r + 1, :]), sign)
            da = 1.0 / (1.0 + a + g)
            db = 1.0 / (1.0 + b + g)
            out[A, i] = a1 * da
            out[B, i] = g2 * da
            out[D, i] = da
            out[BACK_D, i + 2] = db
            out[BACK_A, i + 1] = b * d1
            out[BACK_B, i] = g * d2
            a1, g1, g2, d1, d2 = a, g, g1, db, d1
        return a1, g1, g2, d1, d2

    lax.fori_loop(0, GROUPS, body, (zero,) * 5, unroll=GROUPS)
    out[BACK_A, LINES + 1] = zero
    out[BACK_B, LINES] = zero
    out[BACK_B, LINES + 1] = zero


def at(i):
    return pl.ds(pl.multiple_of(i * ROWS, ROWS), ROWS)


def eta_static_kernel(recv, out):
    line_coefs(lambda k: recv[k, 7], lambda k: recv[k, 8], out)


def fluxes(qp, recv, splat, fx_scr, fe_scr):
    def body(k, carry):
        q = [qp[c, at(k + 1), :] for c in range(COMPS)]
        ux, sx, ue, se = (recv[k, 5 + f] for f in range(4))
        p = rot(splat, COUPLING, q)
        for c in range(COMPS):
            fx_scr[c, k] = ux * q[c] + sx * p[c]
            fe_scr[c, at(k + 1), :] = ue * q[c] + se * p[c]
        return carry

    lax.fori_loop(0, GROUPS, body, 0, unroll=GROUPS)


def residuals(qp, recv, splat, fx_scr, fe_scr, rot_scr, edge_scr):
    lane = lanes()
    for scr in (qp, fe_scr):
        for c in range(COMPS):
            scr[c, 0:ROWS, :] = jnp.zeros((ROWS, CELLS), F32)
            scr[c, LINES + ROWS : LINES + 2 * ROWS, :] = jnp.zeros((ROWS, CELLS), F32)

    def xi(x, offset):
        inside = lane < CELLS - offset if offset > 0 else lane >= -offset
        return jnp.where(inside, roll(x, -offset, 1), 0.0)

    def eta(scr, c, k, offset):
        return scr[c, pl.ds((k + 1) * ROWS + offset, ROWS), :]

    def body(k, carry):
        ux, sx, ue, se = (recv[k, 5 + f] for f in range(4))
        damp_x = DAMPING * (jnp.abs(ux) + sx)
        damp_e = DAMPING * (jnp.abs(ue) + se)
        edge = jnp.zeros((ROWS, CELLS), F32)
        residual = []
        for c in range(COMPS):
            q = qp[c, at(k + 1), :]
            fx = fx_scr[c, k]
            central = (xi(fx, 1) - xi(fx, -1)) + (eta(fe_scr, c, k, 1) - eta(fe_scr, c, k, -1))
            q6 = 6.0 * q
            fourth_x = (xi(q, 2) + xi(q, -2)) - 4.0 * (xi(q, 1) + xi(q, -1)) + q6
            fourth_e = (
                (eta(qp, c, k, 2) + eta(qp, c, k, -2))
                - 4.0 * (eta(qp, c, k, 1) + eta(qp, c, k, -1))
                + q6
            )
            residual.append(-0.5 * central - damp_x * fourth_x - damp_e * fourth_e)
            edge = place(edge, q, CELLS - 2, 4, 4 * c)
            edge = place(edge, fx, CELLS - 1, 2, 20 + 2 * c)
        for c, part in enumerate(rot(splat, LEFT, residual)):
            rot_scr[c, at(k), :] = part
        edge_scr[at(k), :] = edge
        return carry

    lax.fori_loop(0, GROUPS, body, 0, unroll=GROUPS)


def to_lines(cells, out):
    for c in range(COMPS):
        out[pl.ds(c, LINES, stride=ROWS), :] = jnp.transpose(cells[c])


def blank_lines(out):
    zero = jnp.zeros((ROWS, CELLS), F32)
    for i in range(LINES):
        out[ROWS * i : ROWS * i + ROWS, :] = zero


def edge_types(edge_scr, lcol):
    turned = jnp.transpose(edge_scr[...])
    columns = [lcol[b] for b in range(COMPS)]

    def mix(base, stride):
        total = columns[0] * spread(turned[base : base + 1, :])
        for b in range(1, COMPS):
            row = base + stride * b
            total = total + columns[b] * spread(turned[row : row + 1, :])
        return total

    return [mix(k, 4) for k in range(4)] + [mix(20 + k, 2) for k in range(2)]


def ahead_step(coef, source, i, y1, y2):
    return coef[A, i] * y1 + (coef[D, i] * source + coef[B, i] * y2)


def back_step(coef, source, i, z1, z2):
    return coef[BACK_A, i + 2] * z1 + (coef[BACK_D, i + 2] * source + coef[BACK_B, i + 2] * z2)


def ahead(coef, lines, start=0, state=None):
    if state is None:
        zero = coef[D, 0] * 0.0
        state = (zero, zero)

    def body(i, carry):
        y1, y2 = carry
        y = ahead_step(coef, lines[at(i), :], i, y1, y2)
        lines[at(i), :] = y
        return y, y1

    return lax.fori_loop(start, LINES, body, state, unroll=LINES)


def back(coef, lines, out):
    zero = coef[D, 0] * 0.0

    def body(k, carry):
        i = LINES - 1 - k
        z1, z2 = carry
        z = back_step(coef, lines[at(i), :], i, z1, z2)
        out[at(i), :] = z
        return z, z1

    return lax.fori_loop(0, LINES, body, (zero, zero), unroll=LINES)


def dynamic_tiles(y127, y126, z0, z1, ends, types):
    a127, b0, g126, g127, g0, g1 = ends
    lq126, lq127, lq0, lq1, lf127, lf0 = types
    full = [a127 * y127 + g126 * y126, g127 * y127, b0 * z0 + g1 * z1, g0 * z0, lq126, lq127, lq0]
    sub = subs()
    for k, extra in enumerate((lq1, lf127, lf0)):
        full[2 * k] = jnp.where(sub < COMPS, full[2 * k], roll(extra, 5, 0))
        full[2 * k + 1] = jnp.where(sub < COMPS, full[2 * k + 1], roll(extra, 2, 0))
    return full


def block_ends(turned_u, turned_s):
    sign = signs()

    def cell(i):
        return upwind(spread(turned_u[i : i + 1, :]), spread(turned_s[i : i + 1, :]), sign)

    a127, _, g127 = cell(CELLS - 1)
    _, _, g126 = cell(CELLS - 2)
    _, b0, g0 = cell(0)
    _, _, g1 = cell(1)
    return a127, b0, g126, g127, g0, g1


def broadcast_tiles(send, tiles):
    for peer in range(send.shape[0]):
        for k, tile in enumerate(tiles):
            send[peer, ROWS * k : ROWS * k + ROWS, :] = tile


def first_kernel(
    mine, other, splat, lcol, z_out, resp, coef, ends_out, recv, send,
    qp, fx_scr, fe_scr, rot_scr, edge_scr, turned_u, turned_s, lines, y_w1, y_w2,
):
    core = lax.rem(lax.axis_index("eta"), 2)
    for k in range(GROUPS // 2):
        for f in range(FIELDS):
            recv[2 * k + core, f] = mine[k, f]
            recv[2 * k + 1 - core, f] = other[k, f]
    for source, target in ((5, turned_u), (6, turned_s)):
        for k in range(GROUPS):
            edge_scr[ROWS * k : ROWS * k + ROWS, :] = recv[k, source]
        target[...] = jnp.transpose(edge_scr[...])
    line_coefs(lambda k: turned_u[at(k), :], lambda k: turned_s[at(k), :], coef)
    for k in range(GROUPS):
        for c in range(COMPS):
            qp[c, ROWS * k + ROWS : ROWS * k + 2 * ROWS, :] = recv[k, c]
    fluxes(qp, recv, splat, fx_scr, fe_scr)
    residuals(qp, recv, splat, fx_scr, fe_scr, rot_scr, edge_scr)
    types = edge_types(edge_scr, lcol)
    blank_lines(lines)
    to_lines(rot_scr, lines)

    zero = coef[D, 0] * 0.0
    y0 = coef[D, 0] * lines[0:ROWS, :]
    y1 = ahead_step(coef, lines[ROWS : 2 * ROWS, :], 1, y0, zero)
    p0 = coef[D, 0]
    p1 = coef[A, 1] * p0
    q1 = coef[D, 1]
    for ref, first, second in ((lines, y0, y1), (y_w1, p0, p1), (y_w2, zero, q1)):
        ref[0:ROWS, :] = first
        ref[ROWS : 2 * ROWS, :] = second

    def forward(i, carry):
        y1, y2, p1, p2, q1, q2 = carry
        near = coef[A, i]
        far = coef[B, i]
        y = near * y1 + (coef[D, i] * lines[at(i), :] + far * y2)
        p = near * p1 + far * p2
        q = near * q1 + far * q2
        lines[at(i), :] = y
        y_w1[at(i), :] = p
        y_w2[at(i), :] = q
        return y, y1, p, p1, q, q1

    y127, y126, p127, p126, q127, q126 = lax.fori_loop(
        2, LINES, forward, (y1, y0, p1, p0, q1, zero), unroll=LINES - 2
    )

    def reverse(i, carry, last=None):
        z1, z2, p1, p2, q1, q2, u1, u2, v1, v2 = carry
        near = coef[BACK_A, i + 2]
        far = coef[BACK_B, i + 2]
        d = coef[BACK_D, i + 2]
        z = near * z1 + (d * lines[at(i), :] + far * z2)
        p = near * p1 + (d * y_w1[at(i), :] + far * p2)
        q = near * q1 + (d * y_w2[at(i), :] + far * q2)
        if last == 0:
            u, v = d, zero
        elif last == 1:
            u, v = near * u1, d
        else:
            u = near * u1 + far * u2
            v = near * v1 + far * v2
        z_out[at(i), :] = z
        for k, part in enumerate((p, q, u, v)):
            resp[k, at(i), :] = part
        return z, z1, p, p1, q, q1, u, u1, v, v1

    carry = (zero,) * 10
    carry = reverse(LINES - 1, carry, 0)
    carry = reverse(LINES - 2, carry, 1)
    carry = lax.fori_loop(0, LINES - 2, lambda k, x: reverse(LINES - 3 - k, x), carry, unroll=LINES - 2)
    z0, z1, zp0, zp1, zq0, zq1, zu0, zu1, zv0, zv1 = carry

    ends = block_ends(turned_u, turned_s)
    a127, b0, g126, g127, g0, g1 = ends
    for k, part in enumerate(ends):
        ends_out[k] = part
    tiles = dynamic_tiles(y127, y126, z0, z1, ends, types)

    def fore(last, before):
        return a127 * last + g126 * before, g127 * last

    def aft(first, second):
        return b0 * first + g1 * second, g0 * first

    f1, f2 = fore(p127, p126), fore(q127, q126)
    g1_, g2_ = aft(zp0, zp1), aft(zq0, zq1)
    h1, h2 = aft(zu0, zu1), aft(zv0, zv1)
    sub = subs()
    static = []
    raw = []
    for ref in (turned_u, turned_s):
        for i in (CELLS - 2, 0):
            raw.append(jnp.where(sub == 0, spread(ref[i : i + 1, :]), spread(ref[i + 1 : i + 2, :])))
    for one, two in ((f1, f2), (g1_, g2_), (h1, h2)):
        for k in range(2):
            tile = jnp.where(sub < COMPS, one[k], roll(two[k], 3, 0))
            if raw:
                tile = jnp.where(sub < 2, raw.pop(0), tile)
            static.append(tile)
    tiles = [jnp.where(core == 0, one, two) for one, two in zip(tiles, static)] + tiles[6:]
    broadcast_tiles(send, tiles)


def solve_point(m, c1, c2):
    p = 1.0 - m[0]
    r = 1.0 - m[3]
    inverse = 1.0 / (p * r - m[1] * m[2])
    return (r * c1 + m[1] * c2) * inverse, (m[2] * c1 + p * c2) * inverse


def apply(m, x1, x2):
    return m[0] * x1 + m[1] * x2, m[2] * x1 + m[3] * x2


def after_map(f, m, c1, c2):
    product = (
        f[0] * m[0] + f[1] * m[2],
        f[0] * m[1] + f[1] * m[3],
        f[2] * m[0] + f[3] * m[2],
        f[2] * m[1] + f[3] * m[3],
    )
    c1, c2 = apply(f, c1, c2)
    return product, c1, c2


def unpack_static(static, device, stats, slot):
    sub = subs()
    sign = signs()

    def sets(tile):
        return jnp.where(sub < 2, spread(tile[2:3, :]), tile)

    raw = []
    for k in range(6):
        tile = static(device, k)
        base = 4 * (k // 2) + 2 * (k % 2)
        stats[STATS * slot + base] = sets(tile)
        stats[STATS * slot + base + 1] = sets(roll(tile, -3, 0))
        if k < 4:
            raw += [spread(tile[0:1, :]), spread(tile[1:2, :])]
    cell = [upwind(raw[k], raw[k + 4], sign) for k in range(4)]
    a126, _, g126 = cell[0]
    a127, _, g127 = cell[1]
    parts = (
        1.0 / (1.0 + a126 + g126),
        1.0 / (1.0 + a127 + g127),
        a126,
        a127,
        g126,
        g127,
        cell[2][2],
        cell[3][2],
    )
    for k, part in enumerate(parts):
        stats[STATS * slot + 12 + k] = part


def entering(dynamic, count, stats, me):
    sub = subs()
    types = []
    for k in range(count):
        device = lax.rem(me + k, count)
        t = [dynamic(device, n) for n in range(7)]
        for n in range(3):
            t.append(jnp.where(sub < 3, roll(t[2 * n], 3, 0), roll(t[2 * n + 1], -2, 0)))
        types.append(t)
    damp = 4.0 * DAMPING
    inward, inback, outward = [], [], []
    for k in range(count):
        d126, d127, a126, a127, g126, g127, g0, g1 = (
            stats[STATS * k + 12 + n] for n in range(8)
        )
        before = types[k - 1]
        later = types[(k + 1) % count]
        r0 = 0.5 * before[8] - damp * g0 * (before[4] - 4.0 * before[5])
        r1 = -damp * g1 * before[5]
        r127 = -0.5 * later[9] - damp * g127 * (later[7] - 4.0 * later[6])
        r126 = -damp * g126 * later[6]
        y126 = d126 * r126
        y127 = d127 * (r127 + a126 * y126)
        inward.append((r0, r1))
        inback.append((y127, y126))
        w1, w2 = types[k][0:2]
        outward.append((w1 + a127 * y127 + g126 * y126, w2 + g127 * y127))

    def maps(k, base):
        return [stats[STATS * k + base + n] for n in range(4)]

    m = None
    for k in range(count):
        f = maps(k, 0)
        if m is None:
            m, c1, c2 = f, outward[k][0], outward[k][1]
        else:
            m, c1, c2 = after_map(f, m, c1, c2)
            c1, c2 = c1 + outward[k][0], c2 + outward[k][1]
        nxt = inward[(k + 1) % count]
        c1, c2 = c1 + nxt[0], c2 + nxt[1]
    w = [solve_point(m, c1, c2)]
    for k in range(count - 1):
        n1, n2 = apply(maps(k, 0), *w[k])
        nxt = inward[k + 1]
        w.append((n1 + outward[k][0] + nxt[0], n2 + outward[k][1] + nxt[1]))
    m = None
    for k in [0] + list(range(count - 1, 0, -1)):
        h = maps(k, 8)
        s1, s2 = apply(maps(k, 4), *w[k])
        s1, s2 = s1 + types[k][2], s2 + types[k][3]
        if m is None:
            m, c1, c2 = h, s1, s2
        else:
            m, c1, c2 = after_map(h, m, c1, c2)
            c1, c2 = c1 + s1, c2 + s2
        nxt = inback[(k - 1) % count]
        c1, c2 = c1 + nxt[0], c2 + nxt[1]
    x = solve_point(m, c1, c2)
    return w[0] + x


def eta_solve(z_in, resp, enter, splat, eta_coef, lines, rot_scr):
    def correct(i, carry):
        total = z_in[at(i), :]
        for k in range(4):
            total = total + resp[k, at(i), :] * enter[k]
        lines[at(i), :] = total
        return carry

    lax.fori_loop(0, LINES, correct, 0, unroll=LINES)
    for k in range(GROUPS):
        z = [lines[pl.ds(64 * k + c, ROWS, stride=ROWS), :] for c in range(COMPS)]
        for c, part in enumerate(rot(splat, MIDDLE, z)):
            rot_scr[c, ROWS * k : ROWS * k + ROWS, :] = part
    to_lines(rot_scr, lines)
    ahead(eta_coef, lines)
    back(eta_coef, lines, lines)


def second_kernel(
    mine, other, z_in, resp, raw, splat, lcol, coef, ends, eta_coef, z_out, own, stats, send,
    qp, fx_scr, fe_scr, rot_scr, edge_scr, lines,
):
    me = lax.axis_index("xi")
    count = mine.shape[0]
    swapped = lax.rem(lax.axis_index("eta"), 2) == 1

    def dynamic(device, n):
        rows = slice(ROWS * n, ROWS * n + ROWS)
        if n == 6:
            return mine[device, rows, :]
        return jnp.where(swapped, other[device, rows, :], mine[device, rows, :])

    def static(device, n):
        rows = slice(ROWS * n, ROWS * n + ROWS)
        return jnp.where(swapped, mine[device, rows, :], other[device, rows, :])

    for k in range(count):
        unpack_static(static, lax.rem(me + k, count), stats, k)
    enter = entering(dynamic, count, stats, me)
    eta_solve(z_in, resp, enter, splat, eta_coef, lines, rot_scr)
    for k in range(GROUPS):
        z = [lines[pl.ds(64 * k + c, ROWS, stride=ROWS), :] for c in range(COMPS)]
        for c, part in enumerate(rot(splat, RIGHT, z)):
            qp[c, ROWS * k + ROWS : ROWS * k + 2 * ROWS, :] = raw[k, c] + part
    row = lax.axis_index("eta")
    for c in range(COMPS):
        own[c] = qp[c, at(row + 1), :]
    fluxes(qp, raw, splat, fx_scr, fe_scr)
    residuals(qp, raw, splat, fx_scr, fe_scr, rot_scr, edge_scr)
    types = edge_types(edge_scr, lcol)
    to_lines(rot_scr, lines)
    y127, y126 = ahead(coef, lines)
    z0, z1 = back(coef, lines, z_out)
    tiles = dynamic_tiles(y127, y126, z0, z1, [ends[k] for k in range(6)], types)
    broadcast_tiles(send, tiles)


def last_kernel(
    recv, z_in, resp, splat, eta_coef, own, stats, final, increment, rot_scr, lines, few
):
    def dynamic(device, n):
        return recv[device, ROWS * n : ROWS * n + ROWS, :]

    enter = entering(dynamic, recv.shape[0], stats, lax.axis_index("xi"))
    eta_solve(z_in, resp, enter, splat, eta_coef, lines, rot_scr)
    row = lax.axis_index("eta")
    for j in range(ROWS):
        few[ROWS * j : ROWS * j + ROWS, :] = lines[at(row * ROWS + j), :]
    z = [few[pl.ds(c, ROWS, stride=ROWS), :] for c in range(COMPS)]
    for c, part in enumerate(rot(splat, RIGHT, z)):
        increment[c] = part
        final[c] = own[c] + part


def array(*shape):
    return jax.ShapeDtypeStruct(shape, F32)


def vmem(*shape):
    return pltpu.VMEM(shape, F32)


def call(kernel, name, operands, outs, scratch=()):
    return pl.pallas_call(
        kernel,
        out_shape=outs,
        in_specs=[pl.BlockSpec(memory_space=pltpu.VMEM) for _ in operands],
        out_specs=[pl.BlockSpec(memory_space=pltpu.VMEM) for _ in outs],
        scratch_shapes=list(scratch),
        compiler_params=pltpu.CompilerParams(vmem_limit_bytes=16 << 20),
        name=name,
    )(*operands)


def cell_scratch():
    return [
        vmem(COMPS, LINES + 2 * ROWS, CELLS),
        vmem(COMPS, GROUPS, ROWS, CELLS),
        vmem(COMPS, LINES + 2 * ROWS, CELLS),
        vmem(COMPS, LINES, CELLS),
        vmem(LINES, CELLS),
    ]


def per_device(
    flow_state,
    speed_xi,
    sound_xi,
    speed_eta,
    sound_eta,
    coupling,
    left_vectors,
    middle_vectors,
    right_vectors,
):
    xi_count = lax.axis_size("xi")
    flat = ROWS * LINES
    send, matrices = pl.pallas_call(
        pack_kernel,
        out_shape=[array(GROUPS // 2, FIELDS, ROWS, CELLS), array(ROWS, CELLS)],
        in_specs=[pl.BlockSpec(memory_space=pltpu.HBM)] * 9,
        out_specs=[pl.BlockSpec(memory_space=pltpu.HBM)] * 2,
        scratch_shapes=[vmem(FIELDS, ROWS, CELLS), vmem(ROWS, CELLS)]
        + [pltpu.SMEM((COMPS, COMPS), F32)] * 4
        + [pltpu.SemaphoreType.DMA((10 + GROUPS // 2,))],
        compiler_params=pltpu.CompilerParams(vmem_limit_bytes=60 << 20),
        name="pack",
    )(
        flow_state[:, 0],
        speed_xi[0],
        sound_xi[0],
        speed_eta[0],
        sound_eta[0],
        coupling,
        left_vectors,
        middle_vectors,
        right_vectors,
    )
    groups = [[2 * k + core for k in range(GROUPS // 2)] for core in range(2)]
    mine = lax.all_to_all(send, "eta", 0, 0, axis_index_groups=groups, tiled=True)
    swap = [(k, k ^ 1) for k in range(GROUPS)]
    other = lax.ppermute(mine, "eta", swap)
    splat, lcol = call(
        splat_kernel, "splat", (matrices,), [array(100, ROWS, CELLS), array(COMPS, ROWS, CELLS)]
    )
    z_local, resp, coef, ends, raw, send = call(
        first_kernel,
        "first",
        (mine, other, splat, lcol),
        [
            array(flat, CELLS),
            array(4, flat, CELLS),
            array(6, LINES + 2, ROWS, CELLS),
            array(6, ROWS, CELLS),
            array(GROUPS, FIELDS, ROWS, CELLS),
            array(xi_count, DYNAMIC, CELLS),
        ],
        cell_scratch()
        + [vmem(LINES, CELLS), vmem(LINES, CELLS), vmem(flat, CELLS), vmem(flat, CELLS), vmem(flat, CELLS)],
    )
    mine = lax.all_to_all(send, "xi", 0, 0, tiled=True)
    other = lax.ppermute(mine, "eta", swap)
    (eta_coef,) = call(eta_static_kernel, "eta_static", (raw,), [array(6, LINES + 2, ROWS, CELLS)])
    z_local, own, stats, send = call(
        second_kernel,
        "second",
        (mine, other, z_local, resp, raw, splat, lcol, coef, ends, eta_coef),
        [
            array(flat, CELLS),
            array(COMPS, ROWS, CELLS),
            array(STATS * xi_count, ROWS, CELLS),
            array(xi_count, DYNAMIC, CELLS),
        ],
        cell_scratch() + [vmem(flat, CELLS)],
    )
    recv = lax.all_to_all(send, "xi", 0, 0, tiled=True)
    final, increment = call(
        last_kernel,
        "last",
        (recv, z_local, resp, splat, eta_coef, own, stats),
        [array(COMPS, ROWS, CELLS), array(COMPS, ROWS, CELLS)],
        [vmem(COMPS, LINES, CELLS), vmem(flat, CELLS), vmem(ROWS * ROWS, CELLS)],
    )
    return final[:, None], increment[:, None]


def solution(mesh):
    return jax.shard_map(
        per_device,
        mesh=mesh,
        in_specs=(
            P(None, None, "eta", "xi"),
            P(None, "eta", "xi"),
            P(None, "eta", "xi"),
            P(None, "eta", "xi"),
            P(None, "eta", "xi"),
            P(),
            P(),
            P(),
            P(),
        ),
        out_specs=(P(None, None, "eta", "xi"), P(None, None, "eta", "xi")),
        check_vma=False,
    )
```

```python
import jax
import jax.numpy as jnp
from jax import lax
from jax.experimental import pallas as pl
from jax.experimental.pallas import tpu as pltpu
from jax.sharding import PartitionSpec as P


ROWS = 8
CELLS = 128
COMPS = 5
DAMPING = 0.01
GROUPS = 16
LINES = GROUPS * ROWS
FIELDS = 9
FIRST = 56
SECOND = 32
STATS = 20
F32 = jnp.float32
COUPLING, LEFT, MIDDLE, RIGHT = range(4)
A, B, D, BACK_A, BACK_B, BACK_D = range(6)


def lanes():
    return lax.broadcasted_iota(jnp.int32, (ROWS, CELLS), 1)


def subs():
    return lax.broadcasted_iota(jnp.int32, (ROWS, CELLS), 0)


def roll(x, shift, axis):
    return pltpu.roll(x, shift % x.shape[axis], axis)


def rot(splat, which, fields):
    out = []
    for a in range(COMPS):
        total = splat[25 * which + 5 * a] * fields[0]
        for b in range(1, COMPS):
            total = total + splat[25 * which + 5 * a + b] * fields[b]
        out.append(total)
    return out


def place(tile, source, cell, count, slot):
    lane = lanes()
    moved = roll(source, slot - cell, 1)
    return jnp.where((lane >= slot) & (lane < slot + count), moved, tile)


def spread(row):
    return jnp.broadcast_to(row, (ROWS, CELLS))


def signs():
    sub = subs()
    return jnp.where(sub == 3, 1.0, 0.0) - jnp.where(sub == 4, 1.0, 0.0)


def upwind(u, s, sign):
    g = 0.25 * (jnp.abs(u) + s)
    e = u + sign * s
    return jnp.maximum(e, 0.0) + g, jnp.maximum(-e, 0.0) + g, g


def pack_kernel(
    state, ux, sx, ue, se, coupling, left, middle, right, send, matrices, block, m0, m1, m2, m3, sem
):
    fields = [pltpu.make_async_copy(state, block.at[0:COMPS], sem.at[0])]
    for k, source in enumerate((ux, sx, ue, se)):
        fields.append(pltpu.make_async_copy(source, block.at[COMPS + k], sem.at[1 + k]))
    small = [
        pltpu.make_async_copy(source, target, sem.at[5 + k])
        for k, (source, target) in enumerate(zip((coupling, left, middle, right), (m0, m1, m2, m3)))
    ]
    for copy in fields + small:
        copy.start()
    for copy in fields:
        copy.wait()
    out = [pltpu.make_async_copy(block, send.at[p], sem.at[9 + p]) for p in range(send.shape[0])]
    for copy in out:
        copy.start()
    for k, source in enumerate((m0, m1, m2, m3)):
        small[k].wait()
        copy = pltpu.make_async_copy(source, matrices.at[k], sem.at[5 + k])
        copy.start()
        out.append(copy)
    for copy in out:
        copy.wait()


def splat_kernel(matrices, splat, lcol):
    sub = subs()
    for which in range(4):
        matrix = matrices[which]
        for a in range(COMPS):
            for b in range(COMPS):
                splat[25 * which + COMPS * a + b] = jnp.broadcast_to(
                    matrix[a : a + 1, b : b + 1], (ROWS, CELLS)
                )
    for b in range(COMPS):
        column = jnp.zeros((ROWS, CELLS), F32)
        for a in range(COMPS):
            column = jnp.where(sub == a, splat[25 * LEFT + COMPS * a + b], column)
        lcol[b] = column


def line_coefs(u_block, s_block, out):
    sign = signs()
    zero = u_block(0) * 0.0

    def body(k, carry):
        a1, g1, g2, d1, d2 = carry
        ub = u_block(k)
        sb = s_block(k)
        for r in range(ROWS):
            i = k * ROWS + r
            a, b, g = upwind(spread(ub[r : r + 1, :]), spread(sb[r : r + 1, :]), sign)
            da = 1.0 / (1.0 + a + g)
            db = 1.0 / (1.0 + b + g)
            out[A, i] = a1 * da
            out[B, i] = g2 * da
            out[D, i] = da
            out[BACK_D, i + 2] = db
            out[BACK_A, i + 1] = b * d1
            out[BACK_B, i] = g * d2
            a1, g1, g2, d1, d2 = a, g, g1, db, d1
        return a1, g1, g2, d1, d2

    lax.fori_loop(0, GROUPS, body, (zero,) * 5, unroll=GROUPS)
    out[BACK_A, LINES + 1] = zero
    out[BACK_B, LINES] = zero
    out[BACK_B, LINES + 1] = zero


def at(i):
    return pl.ds(pl.multiple_of(i * ROWS, ROWS), ROWS)


def eta_static_kernel(recv, out):
    line_coefs(lambda k: recv[k, 7], lambda k: recv[k, 8], out)


def fluxes(qp, recv, splat, fx_scr, fe_scr):
    def body(k, carry):
        q = [qp[c, at(k + 1), :] for c in range(COMPS)]
        ux, sx, ue, se = (recv[k, 5 + f] for f in range(4))
        p = rot(splat, COUPLING, q)
        for c in range(COMPS):
            fx_scr[c, k] = ux * q[c] + sx * p[c]
            fe_scr[c, at(k + 1), :] = ue * q[c] + se * p[c]
        return carry

    lax.fori_loop(0, GROUPS, body, 0, unroll=GROUPS)


def residuals(qp, recv, splat, fx_scr, fe_scr, rot_scr, edge_scr):
    lane = lanes()
    for scr in (qp, fe_scr):
        for c in range(COMPS):
            scr[c, 0:ROWS, :] = jnp.zeros((ROWS, CELLS), F32)
            scr[c, LINES + ROWS : LINES + 2 * ROWS, :] = jnp.zeros((ROWS, CELLS), F32)

    def xi(x, offset):
        inside = lane < CELLS - offset if offset > 0 else lane >= -offset
        return jnp.where(inside, roll(x, -offset, 1), 0.0)

    def eta(scr, c, k, offset):
        return scr[c, pl.ds((k + 1) * ROWS + offset, ROWS), :]

    def body(k, carry):
        ux, sx, ue, se = (recv[k, 5 + f] for f in range(4))
        damp_x = DAMPING * (jnp.abs(ux) + sx)
        damp_e = DAMPING * (jnp.abs(ue) + se)
        edge = jnp.zeros((ROWS, CELLS), F32)
        residual = []
        for c in range(COMPS):
            q = qp[c, at(k + 1), :]
            fx = fx_scr[c, k]
            central = (xi(fx, 1) - xi(fx, -1)) + (eta(fe_scr, c, k, 1) - eta(fe_scr, c, k, -1))
            q6 = 6.0 * q
            fourth_x = (xi(q, 2) + xi(q, -2)) - 4.0 * (xi(q, 1) + xi(q, -1)) + q6
            fourth_e = (
                (eta(qp, c, k, 2) + eta(qp, c, k, -2))
                - 4.0 * (eta(qp, c, k, 1) + eta(qp, c, k, -1))
                + q6
            )
            residual.append(-0.5 * central - damp_x * fourth_x - damp_e * fourth_e)
            edge = place(edge, q, CELLS - 2, 4, 4 * c)
            edge = place(edge, fx, CELLS - 1, 2, 20 + 2 * c)
        for c, part in enumerate(rot(splat, LEFT, residual)):
            rot_scr[c, at(k), :] = part
        edge_scr[at(k), :] = edge
        return carry

    lax.fori_loop(0, GROUPS, body, 0, unroll=GROUPS)


def to_lines(cells, out):
    for c in range(COMPS):
        out[pl.ds(c, LINES, stride=ROWS), :] = jnp.transpose(cells[c])


def blank_lines(out):
    zero = jnp.zeros((ROWS, CELLS), F32)
    for i in range(LINES):
        out[ROWS * i : ROWS * i + ROWS, :] = zero


def edge_types(edge_scr, lcol):
    turned = jnp.transpose(edge_scr[...])
    columns = [lcol[b] for b in range(COMPS)]

    def mix(base, stride):
        total = columns[0] * spread(turned[base : base + 1, :])
        for b in range(1, COMPS):
            row = base + stride * b
            total = total + columns[b] * spread(turned[row : row + 1, :])
        return total

    return [mix(k, 4) for k in range(4)] + [mix(20 + k, 2) for k in range(2)]


def ahead_step(coef, source, i, y1, y2):
    return coef[A, i] * y1 + (coef[D, i] * source + coef[B, i] * y2)


def back_step(coef, source, i, z1, z2):
    return coef[BACK_A, i + 2] * z1 + (coef[BACK_D, i + 2] * source + coef[BACK_B, i + 2] * z2)


def ahead(coef, lines, start=0, state=None):
    if state is None:
        zero = coef[D, 0] * 0.0
        state = (zero, zero)

    def body(i, carry):
        y1, y2 = carry
        y = ahead_step(coef, lines[at(i), :], i, y1, y2)
        lines[at(i), :] = y
        return y, y1

    return lax.fori_loop(start, LINES, body, state, unroll=LINES)


def back(coef, lines, out):
    zero = coef[D, 0] * 0.0

    def body(k, carry):
        i = LINES - 1 - k
        z1, z2 = carry
        z = back_step(coef, lines[at(i), :], i, z1, z2)
        out[at(i), :] = z
        return z, z1

    return lax.fori_loop(0, LINES, body, (zero, zero), unroll=LINES)


def join(full, extras):
    sub = subs()
    for k, extra in enumerate(extras):
        full[2 * k] = jnp.where(sub < COMPS, full[2 * k], roll(extra, 5, 0))
        full[2 * k + 1] = jnp.where(sub < COMPS, full[2 * k + 1], roll(extra, 2, 0))
    return full


def separate(tiles, extras):
    sub = subs()
    return tiles + [
        jnp.where(sub < 3, roll(tiles[2 * k], 3, 0), roll(tiles[2 * k + 1], -2, 0))
        for k in range(extras)
    ]


def leaving_ends(y127, y126, z0, z1, ends):
    a127, b0, g126, g127, g0, g1 = ends
    return [a127 * y127 + g126 * y126, g127 * y127, b0 * z0 + g1 * z1, g0 * z0]


def into_next(g0, g1, lq126, lq127, lf127):
    damp = 4.0 * DAMPING
    return 0.5 * lf127 - damp * g0 * (lq126 - 4.0 * lq127), -damp * g1 * lq127


def into_previous(coefs, lq0, lq1, lf0):
    d126, d127, a126, _, g126, g127 = coefs
    damp = 4.0 * DAMPING
    r127 = -0.5 * lf0 - damp * g127 * (lq1 - 4.0 * lq0)
    y126 = d126 * (-damp * g126 * lq0)
    return d127 * (r127 + a126 * y126), y126


def block_ends(turned_u, turned_s):
    sign = signs()

    def cell(i):
        return upwind(spread(turned_u[i : i + 1, :]), spread(turned_s[i : i + 1, :]), sign)

    a127, _, g127 = cell(CELLS - 1)
    _, _, g126 = cell(CELLS - 2)
    _, b0, g0 = cell(0)
    _, _, g1 = cell(1)
    return a127, b0, g126, g127, g0, g1


def broadcast_tiles(send, tiles):
    for peer in range(send.shape[0]):
        for k, tile in enumerate(tiles):
            send[peer, ROWS * k : ROWS * k + ROWS, :] = tile


def first_kernel(
    mine, other, splat, lcol, z_out, resp, coef, ends_out, recv, send,
    qp, fx_scr, fe_scr, rot_scr, edge_scr, turned_u, turned_s, lines, y_w1, y_w2,
):
    core = lax.rem(lax.axis_index("eta"), 2)
    for k in range(GROUPS // 2):
        for f in range(FIELDS):
            recv[2 * k + core, f] = mine[k, f]
            recv[2 * k + 1 - core, f] = other[k, f]
    for source, target in ((5, turned_u), (6, turned_s)):
        for k in range(GROUPS):
            edge_scr[ROWS * k : ROWS * k + ROWS, :] = recv[k, source]
        target[...] = jnp.transpose(edge_scr[...])
    line_coefs(lambda k: turned_u[at(k), :], lambda k: turned_s[at(k), :], coef)
    for k in range(GROUPS):
        for c in range(COMPS):
            qp[c, ROWS * k + ROWS : ROWS * k + 2 * ROWS, :] = recv[k, c]
    fluxes(qp, recv, splat, fx_scr, fe_scr)
    residuals(qp, recv, splat, fx_scr, fe_scr, rot_scr, edge_scr)
    types = edge_types(edge_scr, lcol)
    blank_lines(lines)
    to_lines(rot_scr, lines)

    zero = coef[D, 0] * 0.0
    y0 = coef[D, 0] * lines[0:ROWS, :]
    y1 = ahead_step(coef, lines[ROWS : 2 * ROWS, :], 1, y0, zero)
    p0 = coef[D, 0]
    p1 = coef[A, 1] * p0
    q1 = coef[D, 1]
    for ref, first, second in ((lines, y0, y1), (y_w1, p0, p1), (y_w2, zero, q1)):
        ref[0:ROWS, :] = first
        ref[ROWS : 2 * ROWS, :] = second

    def forward(i, carry):
        y1, y2, p1, p2, q1, q2 = carry
        near = coef[A, i]
        far = coef[B, i]
        y = near * y1 + (coef[D, i] * lines[at(i), :] + far * y2)
        p = near * p1 + far * p2
        q = near * q1 + far * q2
        lines[at(i), :] = y
        y_w1[at(i), :] = p
        y_w2[at(i), :] = q
        return y, y1, p, p1, q, q1

    y127, y126, p127, p126, q127, q126 = lax.fori_loop(
        2, LINES, forward, (y1, y0, p1, p0, q1, zero), unroll=LINES - 2
    )

    def reverse(i, carry, last=None):
        z1, z2, p1, p2, q1, q2, u1, u2, v1, v2 = carry
        near = coef[BACK_A, i + 2]
        far = coef[BACK_B, i + 2]
        d = coef[BACK_D, i + 2]
        z = near * z1 + (d * lines[at(i), :] + far * z2)
        p = near * p1 + (d * y_w1[at(i), :] + far * p2)
        q = near * q1 + (d * y_w2[at(i), :] + far * q2)
        if last == 0:
            u, v = d, zero
        elif last == 1:
            u, v = near * u1, d
        else:
            u = near * u1 + far * u2
            v = near * v1 + far * v2
        z_out[at(i), :] = z
        for k, part in enumerate((p, q, u, v)):
            resp[k, at(i), :] = part
        return z, z1, p, p1, q, q1, u, u1, v, v1

    carry = (zero,) * 10
    carry = reverse(LINES - 1, carry, 0)
    carry = reverse(LINES - 2, carry, 1)
    carry = lax.fori_loop(0, LINES - 2, lambda k, x: reverse(LINES - 3 - k, x), carry, unroll=LINES - 2)
    z0, z1, zp0, zp1, zq0, zq1, zu0, zu1, zv0, zv1 = carry

    ends = block_ends(turned_u, turned_s)
    a127, b0, g126, g127, g0, g1 = ends
    for k, part in enumerate(ends):
        ends_out[k] = part
    tiles = leaving_ends(y127, y126, z0, z1, ends)
    lq126, lq127, lq0, lq1, lf127, lf0 = types
    tiles = join(tiles + [lq126, lq127, lq0], [lq1, lf127, lf0])

    def fore(last, before):
        return a127 * last + g126 * before, g127 * last

    def aft(first, second):
        return b0 * first + g1 * second, g0 * first

    f1, f2 = fore(p127, p126), fore(q127, q126)
    g1_, g2_ = aft(zp0, zp1), aft(zq0, zq1)
    h1, h2 = aft(zu0, zu1), aft(zv0, zv1)
    sub = subs()
    static = []
    raw = []
    for ref in (turned_u, turned_s):
        for i in (CELLS - 2, 0):
            raw.append(jnp.where(sub == 0, spread(ref[i : i + 1, :]), spread(ref[i + 1 : i + 2, :])))
    for one, two in ((f1, f2), (g1_, g2_), (h1, h2)):
        for k in range(2):
            tile = jnp.where(sub < COMPS, one[k], roll(two[k], 3, 0))
            if raw:
                tile = jnp.where(sub < 2, raw.pop(0), tile)
            static.append(tile)
    tiles = [jnp.where(core == 0, one, two) for one, two in zip(tiles, static)] + tiles[6:]
    broadcast_tiles(send, tiles)


def solve_point(m, c1, c2):
    p = 1.0 - m[0]
    r = 1.0 - m[3]
    inverse = 1.0 / (p * r - m[1] * m[2])
    return (r * c1 + m[1] * c2) * inverse, (m[2] * c1 + p * c2) * inverse


def apply(m, x1, x2):
    return m[0] * x1 + m[1] * x2, m[2] * x1 + m[3] * x2


def after_map(f, m, c1, c2):
    product = (
        f[0] * m[0] + f[1] * m[2],
        f[0] * m[1] + f[1] * m[3],
        f[2] * m[0] + f[3] * m[2],
        f[2] * m[1] + f[3] * m[3],
    )
    c1, c2 = apply(f, c1, c2)
    return product, c1, c2


def unpack_static(static, device, stats, slot):
    sub = subs()
    sign = signs()

    def sets(tile):
        return jnp.where(sub < 2, spread(tile[2:3, :]), tile)

    raw = []
    for k in range(6):
        tile = static(device, k)
        base = 4 * (k // 2) + 2 * (k % 2)
        stats[STATS * slot + base] = sets(tile)
        stats[STATS * slot + base + 1] = sets(roll(tile, -3, 0))
        if k < 4:
            raw += [spread(tile[0:1, :]), spread(tile[1:2, :])]
    cell = [upwind(raw[k], raw[k + 4], sign) for k in range(4)]
    a126, _, g126 = cell[0]
    a127, _, g127 = cell[1]
    parts = (
        1.0 / (1.0 + a126 + g126),
        1.0 / (1.0 + a127 + g127),
        a126,
        a127,
        g126,
        g127,
        cell[2][2],
        cell[3][2],
    )
    for k, part in enumerate(parts):
        stats[STATS * slot + 12 + k] = part


def end_coefs(stats, k):
    return [stats[STATS * k + 12 + n] for n in range(6)]


def block_terms(types, stats):
    count = len(types)
    forward, backward = [], []
    for k in range(count):
        t, later = types[k], types[(k + 1) % count]
        following = STATS * ((k + 1) % count)
        r0, r1 = into_next(stats[following + 18], stats[following + 19], t[4], t[5], t[8])
        y127, y126 = into_previous(end_coefs(stats, k), later[6], later[7], later[9])
        forward.append(leave_forward(end_coefs(stats, k), t[0] + r0, t[1] + r1, y127, y126))
        backward.append((y127, y126))
    backward = [
        (types[k][2] + backward[k - 1][0], types[k][3] + backward[k - 1][1]) for k in range(count)
    ]
    return forward, backward


def leave_forward(coefs, w1, w2, y127, y126):
    _, _, _, a127, g126, g127 = coefs
    return w1 + a127 * y127 + g126 * y126, w2 + g127 * y127


def entering(forward, backward, stats):
    count = len(forward)

    def maps(k, base):
        return [stats[STATS * k + base + n] for n in range(4)]

    m, c1, c2 = maps(0, 0), *forward[0]
    for k in range(1, count):
        m, c1, c2 = after_map(maps(k, 0), m, c1, c2)
        c1, c2 = c1 + forward[k][0], c2 + forward[k][1]
    w = [solve_point(m, c1, c2)]
    for k in range(count - 1):
        n1, n2 = apply(maps(k, 0), *w[k])
        w.append((n1 + forward[k][0], n2 + forward[k][1]))
    m = None
    for k in [0] + list(range(count - 1, 0, -1)):
        h = maps(k, 8)
        s1, s2 = apply(maps(k, 4), *w[k])
        s1, s2 = s1 + backward[k][0], s2 + backward[k][1]
        if m is None:
            m, c1, c2 = h, s1, s2
        else:
            m, c1, c2 = after_map(h, m, c1, c2)
            c1, c2 = c1 + s1, c2 + s2
    return w[0] + solve_point(m, c1, c2)


def eta_solve(z_in, resp, enter, splat, eta_coef, lines, rot_scr):
    def correct(i, carry):
        total = z_in[at(i), :]
        for k in range(4):
            total = total + resp[k, at(i), :] * enter[k]
        lines[at(i), :] = total
        return carry

    lax.fori_loop(0, LINES, correct, 0, unroll=LINES)
    for k in range(GROUPS):
        z = [lines[pl.ds(64 * k + c, ROWS, stride=ROWS), :] for c in range(COMPS)]
        for c, part in enumerate(rot(splat, MIDDLE, z)):
            rot_scr[c, ROWS * k : ROWS * k + ROWS, :] = part
    to_lines(rot_scr, lines)
    ahead(eta_coef, lines)
    back(eta_coef, lines, lines)


def second_kernel(
    mine, other, z_in, resp, raw, splat, lcol, coef, ends, eta_coef, z_out, own, stats, send,
    qp, fx_scr, fe_scr, rot_scr, edge_scr, lines,
):
    me = lax.axis_index("xi")
    count = mine.shape[0]
    swapped = lax.rem(lax.axis_index("eta"), 2) == 1

    def dynamic(device, n):
        rows = slice(ROWS * n, ROWS * n + ROWS)
        if n == 6:
            return mine[device, rows, :]
        return jnp.where(swapped, other[device, rows, :], mine[device, rows, :])

    def static(device, n):
        rows = slice(ROWS * n, ROWS * n + ROWS)
        return jnp.where(swapped, mine[device, rows, :], other[device, rows, :])

    for k in range(count):
        unpack_static(static, lax.rem(me + k, count), stats, k)
    types = [separate([dynamic(lax.rem(me + k, count), n) for n in range(7)], 3) for k in range(count)]
    enter = entering(*block_terms(types, stats), stats)
    eta_solve(z_in, resp, enter, splat, eta_coef, lines, rot_scr)
    for k in range(GROUPS):
        z = [lines[pl.ds(64 * k + c, ROWS, stride=ROWS), :] for c in range(COMPS)]
        for c, part in enumerate(rot(splat, RIGHT, z)):
            qp[c, ROWS * k + ROWS : ROWS * k + 2 * ROWS, :] = raw[k, c] + part
    row = lax.axis_index("eta")
    for c in range(COMPS):
        own[c] = qp[c, at(row + 1), :]
    fluxes(qp, raw, splat, fx_scr, fe_scr)
    residuals(qp, raw, splat, fx_scr, fe_scr, rot_scr, edge_scr)
    types = edge_types(edge_scr, lcol)
    to_lines(rot_scr, lines)
    y127, y126 = ahead(coef, lines)
    z0, z1 = back(coef, lines, z_out)
    w1, w2, x1, x2 = leaving_ends(y127, y126, z0, z1, [ends[k] for k in range(6)])
    lq126, lq127, lq0, lq1, lf127, lf0 = types
    r0, r1 = into_next(stats[STATS + 18], stats[STATS + 19], lq126, lq127, lf127)
    y127, y126 = into_previous(end_coefs(stats, count - 1), lq0, lq1, lf0)
    tiles = join([w1 + r0, w2 + r1, x1 + y127, x2 + y126], [y127, y126])
    broadcast_tiles(send, tiles)


def last_kernel(
    recv, z_in, resp, splat, eta_coef, own, stats, final, increment, rot_scr, lines, few
):
    me = lax.axis_index("xi")
    count = recv.shape[0]
    types = []
    for k in range(count):
        device = lax.rem(me + k, count)
        types.append(separate([recv[device, ROWS * n : ROWS * n + ROWS, :] for n in range(4)], 2))
    forward = []
    for k in range(count):
        y127, y126 = types[(k + 1) % count][4:6]
        forward.append(leave_forward(end_coefs(stats, k), *types[k][0:2], y127, y126))
    enter = entering(forward, [t[2:4] for t in types], stats)
    eta_solve(z_in, resp, enter, splat, eta_coef, lines, rot_scr)
    row = lax.axis_index("eta")
    for j in range(ROWS):
        few[ROWS * j : ROWS * j + ROWS, :] = lines[at(row * ROWS + j), :]
    z = [few[pl.ds(c, ROWS, stride=ROWS), :] for c in range(COMPS)]
    for c, part in enumerate(rot(splat, RIGHT, z)):
        increment[c] = part
        final[c] = own[c] + part


def array(*shape):
    return jax.ShapeDtypeStruct(shape, F32)


def vmem(*shape):
    return pltpu.VMEM(shape, F32)


def call(kernel, name, operands, outs, scratch=()):
    return pl.pallas_call(
        kernel,
        out_shape=outs,
        in_specs=[pl.BlockSpec(memory_space=pltpu.VMEM) for _ in operands],
        out_specs=[pl.BlockSpec(memory_space=pltpu.VMEM) for _ in outs],
        scratch_shapes=list(scratch),
        compiler_params=pltpu.CompilerParams(vmem_limit_bytes=16 << 20),
        name=name,
    )(*operands)


def cell_scratch():
    return [
        vmem(COMPS, LINES + 2 * ROWS, CELLS),
        vmem(COMPS, GROUPS, ROWS, CELLS),
        vmem(COMPS, LINES + 2 * ROWS, CELLS),
        vmem(COMPS, LINES, CELLS),
        vmem(LINES, CELLS),
    ]


def exchange(send):
    xi_count = lax.axis_size("xi")
    eta_count = lax.axis_size("eta")
    groups = []
    for e in range(eta_count):
        other = (e + eta_count // 2) % eta_count
        groups.append(
            [k * eta_count + (e if k < xi_count // 2 else other) for k in range(xi_count)]
        )
    return lax.all_to_all(send, ("xi", "eta"), 0, 0, axis_index_groups=groups, tiled=True)


def per_device(
    flow_state,
    speed_xi,
    sound_xi,
    speed_eta,
    sound_eta,
    coupling,
    left_vectors,
    middle_vectors,
    right_vectors,
):
    xi_count = lax.axis_size("xi")
    flat = ROWS * LINES
    send, matrices = pl.pallas_call(
        pack_kernel,
        out_shape=[array(GROUPS // 2, FIELDS, ROWS, CELLS), array(4, COMPS, COMPS)],
        in_specs=[pl.BlockSpec(memory_space=pltpu.HBM)] * 9,
        out_specs=[pl.BlockSpec(memory_space=pltpu.HBM)] * 2,
        scratch_shapes=[vmem(FIELDS, ROWS, CELLS)]
        + [vmem(COMPS, COMPS)] * 4
        + [pltpu.SemaphoreType.DMA((9 + GROUPS // 2,))],
        compiler_params=pltpu.CompilerParams(vmem_limit_bytes=60 << 20),
        name="pack",
    )(
        flow_state[:, 0],
        speed_xi[0],
        sound_xi[0],
        speed_eta[0],
        sound_eta[0],
        coupling,
        left_vectors,
        middle_vectors,
        right_vectors,
    )
    groups = [[2 * k + core for k in range(GROUPS // 2)] for core in range(2)]
    mine = lax.all_to_all(send, "eta", 0, 0, axis_index_groups=groups, tiled=True)
    swap = [(k, k ^ 1) for k in range(GROUPS)]
    other = lax.ppermute(mine, "eta", swap)
    splat, lcol = call(
        splat_kernel, "splat", (matrices,), [array(100, ROWS, CELLS), array(COMPS, ROWS, CELLS)]
    )
    z_local, resp, coef, ends, raw, send = call(
        first_kernel,
        "first",
        (mine, other, splat, lcol),
        [
            array(flat, CELLS),
            array(4, flat, CELLS),
            array(6, LINES + 2, ROWS, CELLS),
            array(6, ROWS, CELLS),
            array(GROUPS, FIELDS, ROWS, CELLS),
            array(xi_count, FIRST, CELLS),
        ],
        cell_scratch()
        + [vmem(LINES, CELLS), vmem(LINES, CELLS), vmem(flat, CELLS), vmem(flat, CELLS), vmem(flat, CELLS)],
    )
    mine = exchange(send)
    other = lax.ppermute(mine, "eta", swap)
    (eta_coef,) = call(eta_static_kernel, "eta_static", (raw,), [array(6, LINES + 2, ROWS, CELLS)])
    z_local, own, stats, send = call(
        second_kernel,
        "second",
        (mine, other, z_local, resp, raw, splat, lcol, coef, ends, eta_coef),
        [
            array(flat, CELLS),
            array(COMPS, ROWS, CELLS),
            array(STATS * xi_count, ROWS, CELLS),
            array(xi_count, SECOND, CELLS),
        ],
        cell_scratch() + [vmem(flat, CELLS)],
    )
    recv = exchange(send)
    final, increment = call(
        last_kernel,
        "last",
        (recv, z_local, resp, splat, eta_coef, own, stats),
        [array(COMPS, ROWS, CELLS), array(COMPS, ROWS, CELLS)],
        [vmem(COMPS, LINES, CELLS), vmem(flat, CELLS), vmem(ROWS * ROWS, CELLS)],
    )
    return final[:, None], increment[:, None]


def solution(mesh):
    return jax.shard_map(
        per_device,
        mesh=mesh,
        in_specs=(
            P(None, None, "eta", "xi"),
            P(None, "eta", "xi"),
            P(None, "eta", "xi"),
            P(None, "eta", "xi"),
            P(None, "eta", "xi"),
            P(),
            P(),
            P(),
            P(),
        ),
        out_specs=(P(None, None, "eta", "xi"), P(None, None, "eta", "xi")),
        check_vma=False,
    )
```

```python
import jax
import jax.numpy as jnp
from jax import lax
from jax.experimental import pallas as pl
from jax.experimental.pallas import tpu as pltpu
from jax.sharding import PartitionSpec as P


ROWS = 8
CELLS = 128
COMPS = 5
DAMPING = 0.01
GROUPS = 16
LINES = GROUPS * ROWS
HALF = LINES // 2
FIELDS = 9
FIRST = 56
SECOND = 32
STATS = 20
F32 = jnp.float32
COUPLING, LEFT, MIDDLE, RIGHT = range(4)
A, B, D, BACK_A, BACK_B, BACK_D = range(6)


def lanes():
    return lax.broadcasted_iota(jnp.int32, (ROWS, CELLS), 1)


def subs():
    return lax.broadcasted_iota(jnp.int32, (ROWS, CELLS), 0)


def roll(x, shift, axis):
    return pltpu.roll(x, shift % x.shape[axis], axis)


def rot(splat, which, fields):
    out = []
    for a in range(COMPS):
        total = splat[25 * which + 5 * a] * fields[0]
        for b in range(1, COMPS):
            total = total + splat[25 * which + 5 * a + b] * fields[b]
        out.append(total)
    return out


def place(tile, source, cell, count, slot):
    lane = lanes()
    moved = roll(source, slot - cell, 1)
    return jnp.where((lane >= slot) & (lane < slot + count), moved, tile)


def spread(row):
    return jnp.broadcast_to(row, (ROWS, CELLS))


def signs():
    sub = subs()
    return jnp.where(sub == 3, 1.0, 0.0) - jnp.where(sub == 4, 1.0, 0.0)


def upwind(u, s, sign):
    g = 0.25 * (jnp.abs(u) + s)
    e = u + sign * s
    return jnp.maximum(e, 0.0) + g, jnp.maximum(-e, 0.0) + g, g


def pack_kernel(
    state, ux, sx, ue, se, coupling, left, middle, right, send, matrices, block, m0, m1, m2, m3, sem
):
    fields = [pltpu.make_async_copy(state, block.at[0:COMPS], sem.at[0])]
    for k, source in enumerate((ux, sx, ue, se)):
        fields.append(pltpu.make_async_copy(source, block.at[COMPS + k], sem.at[1 + k]))
    small = [
        pltpu.make_async_copy(source, target, sem.at[5 + k])
        for k, (source, target) in enumerate(zip((coupling, left, middle, right), (m0, m1, m2, m3)))
    ]
    for copy in fields + small:
        copy.start()
    for copy in fields:
        copy.wait()
    out = [pltpu.make_async_copy(block, send.at[p], sem.at[9 + p]) for p in range(send.shape[0])]
    for copy in out:
        copy.start()
    for k, source in enumerate((m0, m1, m2, m3)):
        small[k].wait()
        copy = pltpu.make_async_copy(source, matrices.at[k], sem.at[5 + k])
        copy.start()
        out.append(copy)
    for copy in out:
        copy.wait()


def splat_kernel(matrices, splat, lcol):
    sub = subs()
    for which in range(4):
        matrix = matrices[which]
        for a in range(COMPS):
            for b in range(COMPS):
                splat[25 * which + COMPS * a + b] = jnp.broadcast_to(
                    matrix[a : a + 1, b : b + 1], (ROWS, CELLS)
                )
    for b in range(COMPS):
        column = jnp.zeros((ROWS, CELLS), F32)
        for a in range(COMPS):
            column = jnp.where(sub == a, splat[25 * LEFT + COMPS * a + b], column)
        lcol[b] = column


def line_coefs(u_block, s_block, out):
    sign = signs()
    zero = u_block(0) * 0.0

    def body(k, carry):
        a1, g1, g2, d1, d2 = carry
        ub = u_block(k)
        sb = s_block(k)
        for r in range(ROWS):
            i = k * ROWS + r
            a, b, g = upwind(spread(ub[r : r + 1, :]), spread(sb[r : r + 1, :]), sign)
            da = 1.0 / (1.0 + a + g)
            db = 1.0 / (1.0 + b + g)
            out[A, i] = a1 * da
            out[B, i] = g2 * da
            out[D, i] = da
            out[BACK_D, i + 2] = db
            out[BACK_A, i + 1] = b * d1
            out[BACK_B, i] = g * d2
            a1, g1, g2, d1, d2 = a, g, g1, db, d1
        return a1, g1, g2, d1, d2

    lax.fori_loop(0, GROUPS, body, (zero,) * 5, unroll=GROUPS)
    out[BACK_A, LINES + 1] = zero
    out[BACK_B, LINES] = zero
    out[BACK_B, LINES + 1] = zero


def at(i):
    return pl.ds(pl.multiple_of(i * ROWS, ROWS), ROWS)


def eta_static_kernel(recv, coef, eta_coef, eta_halves, halves):
    line_coefs(lambda k: recv[k, 7], lambda k: recv[k, 8], eta_coef)
    half_responses(eta_coef, eta_halves)
    half_responses(coef, halves)


def seal(scr):
    for c in range(COMPS):
        scr[c, 0:ROWS, :] = jnp.zeros((ROWS, CELLS), F32)
        scr[c, LINES + ROWS : LINES + 2 * ROWS, :] = jnp.zeros((ROWS, CELLS), F32)


def near(scr, c, k, offset=0):
    base = (k + 1) * ROWS + offset
    return scr[c, base : base + ROWS, :]


def along(q_scr, flux_scr, c, k, damp):
    central = near(flux_scr, c, k, 1) - near(flux_scr, c, k, -1)
    fourth = (
        (near(q_scr, c, k, 2) + near(q_scr, c, k, -2))
        - 4.0 * (near(q_scr, c, k, 1) + near(q_scr, c, k, -1))
        + 6.0 * near(q_scr, c, k)
    )
    return -0.5 * central - damp * fourth


def flux_rows(q_scr, flux_scr, splat, u_of, s_of):
    for k in range(GROUPS):
        q = [near(q_scr, c, k) for c in range(COMPS)]
        p = rot(splat, COUPLING, q)
        u = u_of(k)
        s = s_of(k)
        for c in range(COMPS):
            base = (k + 1) * ROWS
            flux_scr[c, base : base + ROWS, :] = u * q[c] + s * p[c]


def residuals(scr, recv, turned_u, turned_s, splat, lcol, lines):
    qp, fe_scr, part_scr, qt_scr, fx_scr, sum_scr = scr
    for padded in (qp, fe_scr, qt_scr, fx_scr):
        seal(padded)
    for c in range(COMPS):
        qt_scr[c, ROWS : ROWS + LINES, :] = jnp.transpose(qp[c, ROWS : ROWS + LINES, :])
    flux_rows(qp, fe_scr, splat, lambda k: recv[k, 7], lambda k: recv[k, 8])
    for k in range(GROUPS):
        damp = DAMPING * (jnp.abs(recv[k, 7]) + recv[k, 8])
        for c in range(COMPS):
            part_scr[c, ROWS * k : ROWS * k + ROWS, :] = along(qp, fe_scr, c, k, damp)
    for c in range(COMPS):
        sum_scr[c] = jnp.transpose(part_scr[c])

    def block(ref, k):
        return ref[ROWS * k : ROWS * k + ROWS, :]

    flux_rows(qt_scr, fx_scr, splat, lambda k: block(turned_u, k), lambda k: block(turned_s, k))
    for k in range(GROUPS):
        damp = DAMPING * (jnp.abs(block(turned_u, k)) + block(turned_s, k))
        residual = [
            along(qt_scr, fx_scr, c, k, damp) + block(sum_scr.at[c], k) for c in range(COMPS)
        ]
        for c, value in enumerate(rot(splat, LEFT, residual)):
            lines[pl.ds(64 * k + c, ROWS, stride=ROWS), :] = value
    columns = [lcol[b] for b in range(COMPS)]

    def mix(source, cell):
        row = ROWS + cell
        total = columns[0] * spread(source[0, row : row + 1, :])
        for b in range(1, COMPS):
            total = total + columns[b] * spread(source[b, row : row + 1, :])
        return total

    last = CELLS - 1
    return [mix(qt_scr, cell) for cell in (last - 1, last, 0, 1)] + [
        mix(fx_scr, cell) for cell in (last, 0)
    ]


def to_lines(cells, out):
    for c in range(COMPS):
        out[pl.ds(c, LINES, stride=ROWS), :] = jnp.transpose(cells[c])


def blank_lines(out):
    zero = jnp.zeros((ROWS, CELLS), F32)
    for i in range(LINES):
        out[ROWS * i : ROWS * i + ROWS, :] = zero


def ahead_step(coef, source, i, y1, y2):
    return coef[A, i] * y1 + (coef[D, i] * source + coef[B, i] * y2)


def back_step(coef, source, i, z1, z2):
    return coef[BACK_A, i + 2] * z1 + (coef[BACK_D, i + 2] * source + coef[BACK_B, i + 2] * z2)


def half_responses(coef, out):
    zero = coef[D, 0] * 0.0
    one = zero + 1.0

    def body(k, carry):
        p1, p2, q1, q2, u1, u2, v1, v2 = carry
        i = HALF + k
        p = coef[A, i] * p1 + coef[B, i] * p2
        q = coef[A, i] * q1 + coef[B, i] * q2
        j = HALF - 1 - k
        u = coef[BACK_A, j + 2] * u1 + coef[BACK_B, j + 2] * u2
        v = coef[BACK_A, j + 2] * v1 + coef[BACK_B, j + 2] * v2
        out[0, k] = p
        out[1, k] = q
        out[2, j] = u
        out[3, j] = v
        return p, p1, q, q1, u, u1, v, v1

    lax.fori_loop(0, HALF, body, (one, zero, zero, one) * 2, unroll=HALF)


def sweep_pair(coef, halves, lines, out):
    zero = coef[D, 0] * 0.0

    def forward(i, carry):
        y1, y2, w1, w2 = carry
        j = i + HALF
        y = ahead_step(coef, lines[at(i), :], i, y1, y2)
        w = ahead_step(coef, lines[at(j), :], j, w1, w2)
        lines[at(i), :] = y
        lines[at(j), :] = w
        return y, y1, w, w1

    s1, s2, last, before = lax.fori_loop(0, HALF, forward, (zero,) * 4, unroll=HALF)
    last = last + (halves[0, HALF - 1] * s1 + halves[1, HALF - 1] * s2)
    before = before + (halves[0, HALF - 2] * s1 + halves[1, HALF - 2] * s2)

    def reverse(k, carry):
        z1, z2, x1, x2 = carry
        i = LINES - 1 - k
        j = HALF - 1 - k
        source = lines[at(i), :] + (halves[0, i - HALF] * s1 + halves[1, i - HALF] * s2)
        z = back_step(coef, source, i, z1, z2)
        x = back_step(coef, lines[at(j), :], j, x1, x2)
        out[at(i), :] = z
        out[at(j), :] = x
        return z, z1, x, x1

    t1, t2, first, second = lax.fori_loop(0, HALF, reverse, (zero,) * 4, unroll=HALF)
    first = first + (halves[2, 0] * t1 + halves[3, 0] * t2)
    second = second + (halves[2, 1] * t1 + halves[3, 1] * t2)

    def finish(j, carry):
        out[at(j), :] = out[at(j), :] + (halves[2, j] * t1 + halves[3, j] * t2)
        return carry

    lax.fori_loop(0, HALF, finish, 0, unroll=HALF)
    return last, before, first, second


def join(full, extras):
    sub = subs()
    for k, extra in enumerate(extras):
        full[2 * k] = jnp.where(sub < COMPS, full[2 * k], roll(extra, 5, 0))
        full[2 * k + 1] = jnp.where(sub < COMPS, full[2 * k + 1], roll(extra, 2, 0))
    return full


def separate(tiles, extras):
    sub = subs()
    return tiles + [
        jnp.where(sub < 3, roll(tiles[2 * k], 3, 0), roll(tiles[2 * k + 1], -2, 0))
        for k in range(extras)
    ]


def leaving_ends(y127, y126, z0, z1, ends):
    a127, b0, g126, g127, g0, g1 = ends
    return [a127 * y127 + g126 * y126, g127 * y127, b0 * z0 + g1 * z1, g0 * z0]


def into_next(g0, g1, lq126, lq127, lf127):
    damp = 4.0 * DAMPING
    return 0.5 * lf127 - damp * g0 * (lq126 - 4.0 * lq127), -damp * g1 * lq127


def into_previous(coefs, lq0, lq1, lf0):
    d126, d127, a126, _, g126, g127 = coefs
    damp = 4.0 * DAMPING
    r127 = -0.5 * lf0 - damp * g127 * (lq1 - 4.0 * lq0)
    y126 = d126 * (-damp * g126 * lq0)
    return d127 * (r127 + a126 * y126), y126


def block_ends(turned_u, turned_s):
    sign = signs()

    def cell(i):
        return upwind(spread(turned_u[i : i + 1, :]), spread(turned_s[i : i + 1, :]), sign)

    a127, _, g127 = cell(CELLS - 1)
    _, _, g126 = cell(CELLS - 2)
    _, b0, g0 = cell(0)
    _, _, g1 = cell(1)
    return a127, b0, g126, g127, g0, g1


def broadcast_tiles(send, tiles):
    for peer in range(send.shape[0]):
        for k, tile in enumerate(tiles):
            send[peer, ROWS * k : ROWS * k + ROWS, :] = tile


def first_kernel(
    mine, other, splat, lcol, z_out, resp, coef, ends_out, recv, turned_u, turned_s, send,
    qp, fe_scr, part_scr, qt_scr, fx_scr, sum_scr, lines, y_w1, y_w2,
):
    core = lax.rem(lax.axis_index("eta"), 2)
    for k in range(GROUPS // 2):
        for f in range(FIELDS):
            recv[2 * k + core, f] = mine[k, f]
            recv[2 * k + 1 - core, f] = other[k, f]
    for source, target in ((5, turned_u), (6, turned_s)):
        for k in range(GROUPS):
            part_scr[0, ROWS * k : ROWS * k + ROWS, :] = recv[k, source]
        target[...] = jnp.transpose(part_scr[0])
    line_coefs(lambda k: turned_u[at(k), :], lambda k: turned_s[at(k), :], coef)
    for k in range(GROUPS):
        for c in range(COMPS):
            qp[c, ROWS * k + ROWS : ROWS * k + 2 * ROWS, :] = recv[k, c]
    blank_lines(lines)
    scr = (qp, fe_scr, part_scr, qt_scr, fx_scr, sum_scr)
    types = residuals(scr, recv, turned_u, turned_s, splat, lcol, lines)

    zero = coef[D, 0] * 0.0
    y0 = coef[D, 0] * lines[0:ROWS, :]
    y1 = ahead_step(coef, lines[ROWS : 2 * ROWS, :], 1, y0, zero)
    p0 = coef[D, 0]
    p1 = coef[A, 1] * p0
    q1 = coef[D, 1]
    for ref, first, second in ((lines, y0, y1), (y_w1, p0, p1), (y_w2, zero, q1)):
        ref[0:ROWS, :] = first
        ref[ROWS : 2 * ROWS, :] = second

    def forward(i, carry):
        y1, y2, p1, p2, q1, q2 = carry
        near = coef[A, i]
        far = coef[B, i]
        y = near * y1 + (coef[D, i] * lines[at(i), :] + far * y2)
        p = near * p1 + far * p2
        q = near * q1 + far * q2
        lines[at(i), :] = y
        y_w1[at(i), :] = p
        y_w2[at(i), :] = q
        return y, y1, p, p1, q, q1

    y127, y126, p127, p126, q127, q126 = lax.fori_loop(
        2, LINES, forward, (y1, y0, p1, p0, q1, zero), unroll=LINES - 2
    )

    def reverse(i, carry, last=None):
        z1, z2, p1, p2, q1, q2, u1, u2, v1, v2 = carry
        near = coef[BACK_A, i + 2]
        far = coef[BACK_B, i + 2]
        d = coef[BACK_D, i + 2]
        z = near * z1 + (d * lines[at(i), :] + far * z2)
        p = near * p1 + (d * y_w1[at(i), :] + far * p2)
        q = near * q1 + (d * y_w2[at(i), :] + far * q2)
        if last == 0:
            u, v = d, zero
        elif last == 1:
            u, v = near * u1, d
        else:
            u = near * u1 + far * u2
            v = near * v1 + far * v2
        z_out[at(i), :] = z
        for k, part in enumerate((p, q, u, v)):
            resp[k, at(i), :] = part
        return z, z1, p, p1, q, q1, u, u1, v, v1

    carry = (zero,) * 10
    carry = reverse(LINES - 1, carry, 0)
    carry = reverse(LINES - 2, carry, 1)
    carry = lax.fori_loop(0, LINES - 2, lambda k, x: reverse(LINES - 3 - k, x), carry, unroll=LINES - 2)
    z0, z1, zp0, zp1, zq0, zq1, zu0, zu1, zv0, zv1 = carry

    ends = block_ends(turned_u, turned_s)
    a127, b0, g126, g127, g0, g1 = ends
    for k, part in enumerate(ends):
        ends_out[k] = part
    tiles = leaving_ends(y127, y126, z0, z1, ends)
    lq126, lq127, lq0, lq1, lf127, lf0 = types
    tiles = join(tiles + [lq126, lq127, lq0], [lq1, lf127, lf0])

    def fore(last, before):
        return a127 * last + g126 * before, g127 * last

    def aft(first, second):
        return b0 * first + g1 * second, g0 * first

    f1, f2 = fore(p127, p126), fore(q127, q126)
    g1_, g2_ = aft(zp0, zp1), aft(zq0, zq1)
    h1, h2 = aft(zu0, zu1), aft(zv0, zv1)
    sub = subs()
    static = []
    raw = []
    for ref in (turned_u, turned_s):
        for i in (CELLS - 2, 0):
            raw.append(jnp.where(sub == 0, spread(ref[i : i + 1, :]), spread(ref[i + 1 : i + 2, :])))
    for one, two in ((f1, f2), (g1_, g2_), (h1, h2)):
        for k in range(2):
            tile = jnp.where(sub < COMPS, one[k], roll(two[k], 3, 0))
            if raw:
                tile = jnp.where(sub < 2, raw.pop(0), tile)
            static.append(tile)
    tiles = [jnp.where(core == 0, one, two) for one, two in zip(tiles, static)] + tiles[6:]
    broadcast_tiles(send, tiles)


def solve_point(m, c1, c2):
    p = 1.0 - m[0]
    r = 1.0 - m[3]
    inverse = 1.0 / (p * r - m[1] * m[2])
    return (r * c1 + m[1] * c2) * inverse, (m[2] * c1 + p * c2) * inverse


def apply(m, x1, x2):
    return m[0] * x1 + m[1] * x2, m[2] * x1 + m[3] * x2


def after_map(f, m, c1, c2):
    product = (
        f[0] * m[0] + f[1] * m[2],
        f[0] * m[1] + f[1] * m[3],
        f[2] * m[0] + f[3] * m[2],
        f[2] * m[1] + f[3] * m[3],
    )
    c1, c2 = apply(f, c1, c2)
    return product, c1, c2


def unpack_static(static, device, stats, slot):
    sub = subs()
    sign = signs()

    def sets(tile):
        return jnp.where(sub < 2, spread(tile[2:3, :]), tile)

    raw = []
    for k in range(6):
        tile = static(device, k)
        base = 4 * (k // 2) + 2 * (k % 2)
        stats[STATS * slot + base] = sets(tile)
        stats[STATS * slot + base + 1] = sets(roll(tile, -3, 0))
        if k < 4:
            raw += [spread(tile[0:1, :]), spread(tile[1:2, :])]
    cell = [upwind(raw[k], raw[k + 4], sign) for k in range(4)]
    a126, _, g126 = cell[0]
    a127, _, g127 = cell[1]
    parts = (
        1.0 / (1.0 + a126 + g126),
        1.0 / (1.0 + a127 + g127),
        a126,
        a127,
        g126,
        g127,
        cell[2][2],
        cell[3][2],
    )
    for k, part in enumerate(parts):
        stats[STATS * slot + 12 + k] = part


def end_coefs(stats, k):
    return [stats[STATS * k + 12 + n] for n in range(6)]


def block_terms(types, stats):
    count = len(types)
    forward, backward = [], []
    for k in range(count):
        t, later = types[k], types[(k + 1) % count]
        following = STATS * ((k + 1) % count)
        r0, r1 = into_next(stats[following + 18], stats[following + 19], t[4], t[5], t[8])
        y127, y126 = into_previous(end_coefs(stats, k), later[6], later[7], later[9])
        forward.append(leave_forward(end_coefs(stats, k), t[0] + r0, t[1] + r1, y127, y126))
        backward.append((y127, y126))
    backward = [
        (types[k][2] + backward[k - 1][0], types[k][3] + backward[k - 1][1]) for k in range(count)
    ]
    return forward, backward


def leave_forward(coefs, w1, w2, y127, y126):
    _, _, _, a127, g126, g127 = coefs
    return w1 + a127 * y127 + g126 * y126, w2 + g127 * y127


def entering(forward, backward, stats):
    count = len(forward)

    def maps(k, base):
        return [stats[STATS * k + base + n] for n in range(4)]

    m, c1, c2 = maps(0, 0), *forward[0]
    for k in range(1, count):
        m, c1, c2 = after_map(maps(k, 0), m, c1, c2)
        c1, c2 = c1 + forward[k][0], c2 + forward[k][1]
    w = [solve_point(m, c1, c2)]
    for k in range(count - 1):
        n1, n2 = apply(maps(k, 0), *w[k])
        w.append((n1 + forward[k][0], n2 + forward[k][1]))
    m = None
    for k in [0] + list(range(count - 1, 0, -1)):
        h = maps(k, 8)
        s1, s2 = apply(maps(k, 4), *w[k])
        s1, s2 = s1 + backward[k][0], s2 + backward[k][1]
        if m is None:
            m, c1, c2 = h, s1, s2
        else:
            m, c1, c2 = after_map(h, m, c1, c2)
            c1, c2 = c1 + s1, c2 + s2
    return w[0] + solve_point(m, c1, c2)


def eta_solve(z_in, resp, enter, splat, eta_coef, eta_halves, lines, rot_scr):
    def correct(i, carry):
        total = z_in[at(i), :]
        for k in range(4):
            total = total + resp[k, at(i), :] * enter[k]
        lines[at(i), :] = total
        return carry

    lax.fori_loop(0, LINES, correct, 0, unroll=LINES)
    for k in range(GROUPS):
        z = [lines[pl.ds(64 * k + c, ROWS, stride=ROWS), :] for c in range(COMPS)]
        for c, part in enumerate(rot(splat, MIDDLE, z)):
            rot_scr[c, ROWS * k : ROWS * k + ROWS, :] = part
    to_lines(rot_scr, lines)
    sweep_pair(eta_coef, eta_halves, lines, lines)


def second_kernel(
    mine, other, z_in, resp, raw, turned_u, turned_s, splat, lcol, coef, ends, eta_coef, eta_halves, halves,
    z_out, own, stats, send,
    qp, fe_scr, part_scr, qt_scr, fx_scr, sum_scr, lines,
):
    me = lax.axis_index("xi")
    count = mine.shape[0]
    swapped = lax.rem(lax.axis_index("eta"), 2) == 1

    def dynamic(device, n):
        rows = slice(ROWS * n, ROWS * n + ROWS)
        if n == 6:
            return mine[device, rows, :]
        return jnp.where(swapped, other[device, rows, :], mine[device, rows, :])

    def static(device, n):
        rows = slice(ROWS * n, ROWS * n + ROWS)
        return jnp.where(swapped, mine[device, rows, :], other[device, rows, :])

    for k in range(count):
        unpack_static(static, lax.rem(me + k, count), stats, k)
    types = [separate([dynamic(lax.rem(me + k, count), n) for n in range(7)], 3) for k in range(count)]
    enter = entering(*block_terms(types, stats), stats)
    eta_solve(z_in, resp, enter, splat, eta_coef, eta_halves, lines, part_scr)
    for k in range(GROUPS):
        z = [lines[pl.ds(64 * k + c, ROWS, stride=ROWS), :] for c in range(COMPS)]
        for c, part in enumerate(rot(splat, RIGHT, z)):
            qp[c, ROWS * k + ROWS : ROWS * k + 2 * ROWS, :] = raw[k, c] + part
    row = lax.axis_index("eta")
    for c in range(COMPS):
        own[c] = qp[c, at(row + 1), :]
    scr = (qp, fe_scr, part_scr, qt_scr, fx_scr, sum_scr)
    types = residuals(scr, raw, turned_u, turned_s, splat, lcol, lines)
    y127, y126, z0, z1 = sweep_pair(coef, halves, lines, z_out)
    w1, w2, x1, x2 = leaving_ends(y127, y126, z0, z1, [ends[k] for k in range(6)])
    lq126, lq127, lq0, lq1, lf127, lf0 = types
    r0, r1 = into_next(stats[STATS + 18], stats[STATS + 19], lq126, lq127, lf127)
    y127, y126 = into_previous(end_coefs(stats, count - 1), lq0, lq1, lf0)
    tiles = join([w1 + r0, w2 + r1, x1 + y127, x2 + y126], [y127, y126])
    broadcast_tiles(send, tiles)


def last_kernel(
    recv, z_in, resp, splat, eta_coef, eta_halves, own, stats, final, increment, rot_scr, lines, few
):
    me = lax.axis_index("xi")
    count = recv.shape[0]
    types = []
    for k in range(count):
        device = lax.rem(me + k, count)
        types.append(separate([recv[device, ROWS * n : ROWS * n + ROWS, :] for n in range(4)], 2))
    forward = []
    for k in range(count):
        y127, y126 = types[(k + 1) % count][4:6]
        forward.append(leave_forward(end_coefs(stats, k), *types[k][0:2], y127, y126))
    enter = entering(forward, [t[2:4] for t in types], stats)
    eta_solve(z_in, resp, enter, splat, eta_coef, eta_halves, lines, rot_scr)
    row = lax.axis_index("eta")
    for j in range(ROWS):
        few[ROWS * j : ROWS * j + ROWS, :] = lines[at(row * ROWS + j), :]
    z = [few[pl.ds(c, ROWS, stride=ROWS), :] for c in range(COMPS)]
    for c, part in enumerate(rot(splat, RIGHT, z)):
        increment[c] = part
        final[c] = own[c] + part


def array(*shape):
    return jax.ShapeDtypeStruct(shape, F32)


def vmem(*shape):
    return pltpu.VMEM(shape, F32)


def call(kernel, name, operands, outs, scratch=()):
    return pl.pallas_call(
        kernel,
        out_shape=outs,
        in_specs=[pl.BlockSpec(memory_space=pltpu.VMEM) for _ in operands],
        out_specs=[pl.BlockSpec(memory_space=pltpu.VMEM) for _ in outs],
        scratch_shapes=list(scratch),
        compiler_params=pltpu.CompilerParams(vmem_limit_bytes=16 << 20),
        name=name,
    )(*operands)


def cell_scratch():
    padded = (COMPS, LINES + 2 * ROWS, CELLS)
    plain = (COMPS, LINES, CELLS)
    return [vmem(*shape) for shape in (padded, padded, plain, padded, padded, plain)]


def exchange(send):
    xi_count = lax.axis_size("xi")
    eta_count = lax.axis_size("eta")
    groups = []
    for e in range(eta_count):
        other = (e + eta_count // 2) % eta_count
        groups.append(
            [k * eta_count + (e if k < xi_count // 2 else other) for k in range(xi_count)]
        )
    return lax.all_to_all(send, ("xi", "eta"), 0, 0, axis_index_groups=groups, tiled=True)


def per_device(
    flow_state,
    speed_xi,
    sound_xi,
    speed_eta,
    sound_eta,
    coupling,
    left_vectors,
    middle_vectors,
    right_vectors,
):
    xi_count = lax.axis_size("xi")
    flat = ROWS * LINES
    send, matrices = pl.pallas_call(
        pack_kernel,
        out_shape=[array(GROUPS // 2, FIELDS, ROWS, CELLS), array(4, COMPS, COMPS)],
        in_specs=[pl.BlockSpec(memory_space=pltpu.HBM)] * 9,
        out_specs=[pl.BlockSpec(memory_space=pltpu.HBM)] * 2,
        scratch_shapes=[vmem(FIELDS, ROWS, CELLS)]
        + [vmem(COMPS, COMPS)] * 4
        + [pltpu.SemaphoreType.DMA((9 + GROUPS // 2,))],
        compiler_params=pltpu.CompilerParams(vmem_limit_bytes=60 << 20),
        name="pack",
    )(
        flow_state[:, 0],
        speed_xi[0],
        sound_xi[0],
        speed_eta[0],
        sound_eta[0],
        coupling,
        left_vectors,
        middle_vectors,
        right_vectors,
    )
    groups = [[2 * k + core for k in range(GROUPS // 2)] for core in range(2)]
    mine = lax.all_to_all(send, "eta", 0, 0, axis_index_groups=groups, tiled=True)
    swap = [(k, k ^ 1) for k in range(GROUPS)]
    other = lax.ppermute(mine, "eta", swap)
    splat, lcol = call(
        splat_kernel, "splat", (matrices,), [array(100, ROWS, CELLS), array(COMPS, ROWS, CELLS)]
    )
    z_local, resp, coef, ends, raw, turned_u, turned_s, send = call(
        first_kernel,
        "first",
        (mine, other, splat, lcol),
        [
            array(flat, CELLS),
            array(4, flat, CELLS),
            array(6, LINES + 2, ROWS, CELLS),
            array(6, ROWS, CELLS),
            array(GROUPS, FIELDS, ROWS, CELLS),
            array(CELLS, LINES),
            array(CELLS, LINES),
            array(xi_count, FIRST, CELLS),
        ],
        cell_scratch()
        + [vmem(flat, CELLS), vmem(flat, CELLS), vmem(flat, CELLS)],
    )
    mine = exchange(send)
    other = lax.ppermute(mine, "eta", swap)
    eta_coef, eta_halves, halves = call(
        eta_static_kernel,
        "eta_static",
        (raw, coef),
        [array(6, LINES + 2, ROWS, CELLS)] + [array(4, HALF, ROWS, CELLS)] * 2,
    )
    z_local, own, stats, send = call(
        second_kernel,
        "second",
        (mine, other, z_local, resp, raw, turned_u, turned_s, splat, lcol, coef, ends, eta_coef, eta_halves, halves),
        [
            array(flat, CELLS),
            array(COMPS, ROWS, CELLS),
            array(STATS * xi_count, ROWS, CELLS),
            array(xi_count, SECOND, CELLS),
        ],
        cell_scratch() + [vmem(flat, CELLS)],
    )
    recv = exchange(send)
    final, increment = call(
        last_kernel,
        "last",
        (recv, z_local, resp, splat, eta_coef, eta_halves, own, stats),
        [array(COMPS, ROWS, CELLS), array(COMPS, ROWS, CELLS)],
        [vmem(COMPS, LINES, CELLS), vmem(flat, CELLS), vmem(ROWS * ROWS, CELLS)],
    )
    return final[:, None], increment[:, None]


def solution(mesh):
    return jax.shard_map(
        per_device,
        mesh=mesh,
        in_specs=(
            P(None, None, "eta", "xi"),
            P(None, "eta", "xi"),
            P(None, "eta", "xi"),
            P(None, "eta", "xi"),
            P(None, "eta", "xi"),
            P(),
            P(),
            P(),
            P(),
        ),
        out_specs=(P(None, None, "eta", "xi"), P(None, None, "eta", "xi")),
        check_vma=False,
    )
```

```python
import jax
import jax.numpy as jnp
from jax import lax
from jax.experimental import pallas as pl
from jax.experimental.pallas import tpu as pltpu
from jax.sharding import PartitionSpec as P


ROWS = 8
CELLS = 128
COMPS = 5
DAMPING = 0.01
GROUPS = 16
LINES = GROUPS * ROWS
HALF = LINES // 2
FIELDS = 9
FIRST = 48
SECOND = 32
STATS = 20
F32 = jnp.float32
COUPLING, LEFT, MIDDLE, RIGHT = range(4)
A, B, D, BACK_A, BACK_B, BACK_D = range(6)


def lanes():
    return lax.broadcasted_iota(jnp.int32, (ROWS, CELLS), 1)


def subs():
    return lax.broadcasted_iota(jnp.int32, (ROWS, CELLS), 0)


def roll(x, shift, axis):
    return pltpu.roll(x, shift % x.shape[axis], axis)


def rot(splat, which, fields):
    out = []
    for a in range(COMPS):
        total = splat[25 * which + 5 * a] * fields[0]
        for b in range(1, COMPS):
            total = total + splat[25 * which + 5 * a + b] * fields[b]
        out.append(total)
    return out


def place(tile, source, cell, count, slot):
    lane = lanes()
    moved = roll(source, slot - cell, 1)
    return jnp.where((lane >= slot) & (lane < slot + count), moved, tile)


def spread(row):
    return jnp.broadcast_to(row, (ROWS, CELLS))


def signs():
    sub = subs()
    return jnp.where(sub == 3, 1.0, 0.0) - jnp.where(sub == 4, 1.0, 0.0)


def upwind(u, s, sign):
    g = 0.25 * (jnp.abs(u) + s)
    e = u + sign * s
    return jnp.maximum(e, 0.0) + g, jnp.maximum(-e, 0.0) + g, g


def pack_kernel(
    state, ux, sx, ue, se, coupling, left, middle, right, send, matrices, block, m0, m1, m2, m3, sem
):
    fields = [pltpu.make_async_copy(state, block.at[0:COMPS], sem.at[0])]
    for k, source in enumerate((ux, sx, ue, se)):
        fields.append(pltpu.make_async_copy(source, block.at[COMPS + k], sem.at[1 + k]))
    small = [
        pltpu.make_async_copy(source, target, sem.at[5 + k])
        for k, (source, target) in enumerate(zip((coupling, left, middle, right), (m0, m1, m2, m3)))
    ]
    for copy in fields + small:
        copy.start()
    for copy in fields:
        copy.wait()
    out = [pltpu.make_async_copy(block, send.at[p], sem.at[9 + p]) for p in range(send.shape[0])]
    for copy in out:
        copy.start()
    for k, source in enumerate((m0, m1, m2, m3)):
        small[k].wait()
        copy = pltpu.make_async_copy(source, matrices.at[k], sem.at[5 + k])
        copy.start()
        out.append(copy)
    for copy in out:
        copy.wait()


def splat_kernel(matrices, splat, lcol):
    sub = subs()
    for which in range(4):
        matrix = matrices[which]
        for a in range(COMPS):
            for b in range(COMPS):
                splat[25 * which + COMPS * a + b] = jnp.broadcast_to(
                    matrix[a : a + 1, b : b + 1], (ROWS, CELLS)
                )
    for b in range(COMPS):
        column = jnp.zeros((ROWS, CELLS), F32)
        for a in range(COMPS):
            column = jnp.where(sub == a, splat[25 * LEFT + COMPS * a + b], column)
        lcol[b] = column


def line_coefs(u_block, s_block, out):
    sign = signs()
    zero = u_block(0) * 0.0

    def body(k, carry):
        a1, g1, g2, d1, d2 = carry
        ub = u_block(k)
        sb = s_block(k)
        for r in range(ROWS):
            i = k * ROWS + r
            a, b, g = upwind(spread(ub[r : r + 1, :]), spread(sb[r : r + 1, :]), sign)
            da = 1.0 / (1.0 + a + g)
            db = 1.0 / (1.0 + b + g)
            out[A, i] = a1 * da
            out[B, i] = g2 * da
            out[D, i] = da
            out[BACK_D, i + 2] = db
            out[BACK_A, i + 1] = b * d1
            out[BACK_B, i] = g * d2
            a1, g1, g2, d1, d2 = a, g, g1, db, d1
        return a1, g1, g2, d1, d2

    lax.fori_loop(0, GROUPS, body, (zero,) * 5, unroll=GROUPS)
    out[BACK_A, LINES + 1] = zero
    out[BACK_B, LINES] = zero
    out[BACK_B, LINES + 1] = zero


def at(i):
    return pl.ds(pl.multiple_of(i * ROWS, ROWS), ROWS)


def eta_static_kernel(recv, coef, eta_coef, eta_halves, halves):
    line_coefs(lambda k: recv[k, 7], lambda k: recv[k, 8], eta_coef)
    half_responses(eta_coef, eta_halves)
    half_responses(coef, halves)


def seal(scr):
    for c in range(COMPS):
        scr[c, 0:ROWS, :] = jnp.zeros((ROWS, CELLS), F32)
        scr[c, LINES + ROWS : LINES + 2 * ROWS, :] = jnp.zeros((ROWS, CELLS), F32)


def near(scr, c, k, offset=0):
    base = (k + 1) * ROWS + offset
    return scr[c, base : base + ROWS, :]


def along(q_scr, flux_scr, c, k, damp):
    central = near(flux_scr, c, k, 1) - near(flux_scr, c, k, -1)
    fourth = (
        (near(q_scr, c, k, 2) + near(q_scr, c, k, -2))
        - 4.0 * (near(q_scr, c, k, 1) + near(q_scr, c, k, -1))
        + 6.0 * near(q_scr, c, k)
    )
    return -0.5 * central - damp * fourth


def flux_rows(q_scr, flux_scr, splat, u_of, s_of):
    for k in range(GROUPS):
        q = [near(q_scr, c, k) for c in range(COMPS)]
        p = rot(splat, COUPLING, q)
        u = u_of(k)
        s = s_of(k)
        for c in range(COMPS):
            base = (k + 1) * ROWS
            flux_scr[c, base : base + ROWS, :] = u * q[c] + s * p[c]


def residuals(scr, recv, turned_u, turned_s, splat, lcol, lines):
    qp, fe_scr, part_scr, qt_scr, fx_scr, sum_scr = scr
    for padded in (qp, fe_scr, qt_scr, fx_scr):
        seal(padded)
    for c in range(COMPS):
        qt_scr[c, ROWS : ROWS + LINES, :] = jnp.transpose(qp[c, ROWS : ROWS + LINES, :])
    flux_rows(qp, fe_scr, splat, lambda k: recv[k, 7], lambda k: recv[k, 8])
    for k in range(GROUPS):
        damp = DAMPING * (jnp.abs(recv[k, 7]) + recv[k, 8])
        for c in range(COMPS):
            part_scr[c, ROWS * k : ROWS * k + ROWS, :] = along(qp, fe_scr, c, k, damp)
    for c in range(COMPS):
        sum_scr[c] = jnp.transpose(part_scr[c])

    def block(ref, k):
        return ref[ROWS * k : ROWS * k + ROWS, :]

    flux_rows(qt_scr, fx_scr, splat, lambda k: block(turned_u, k), lambda k: block(turned_s, k))
    for k in range(GROUPS):
        damp = DAMPING * (jnp.abs(block(turned_u, k)) + block(turned_s, k))
        residual = [
            along(qt_scr, fx_scr, c, k, damp) + block(sum_scr.at[c], k) for c in range(COMPS)
        ]
        for c, value in enumerate(rot(splat, LEFT, residual)):
            lines[pl.ds(64 * k + c, ROWS, stride=ROWS), :] = value
    columns = [lcol[b] for b in range(COMPS)]

    def mix(source, cell):
        row = ROWS + cell
        total = columns[0] * spread(source[0, row : row + 1, :])
        for b in range(1, COMPS):
            total = total + columns[b] * spread(source[b, row : row + 1, :])
        return total

    last = CELLS - 1
    return [mix(qt_scr, cell) for cell in (last - 1, last, 0, 1)] + [
        mix(fx_scr, cell) for cell in (last, 0)
    ]


def to_lines(cells, out):
    for c in range(COMPS):
        out[pl.ds(c, LINES, stride=ROWS), :] = jnp.transpose(cells[c])


def blank_lines(out):
    zero = jnp.zeros((ROWS, CELLS), F32)
    for i in range(LINES):
        out[ROWS * i : ROWS * i + ROWS, :] = zero


def ahead_step(coef, source, i, y1, y2):
    return coef[A, i] * y1 + (coef[D, i] * source + coef[B, i] * y2)


def back_step(coef, source, i, z1, z2):
    return coef[BACK_A, i + 2] * z1 + (coef[BACK_D, i + 2] * source + coef[BACK_B, i + 2] * z2)


def half_responses(coef, out):
    zero = coef[D, 0] * 0.0
    one = zero + 1.0

    def body(k, carry):
        p1, p2, q1, q2, u1, u2, v1, v2 = carry
        i = HALF + k
        p = coef[A, i] * p1 + coef[B, i] * p2
        q = coef[A, i] * q1 + coef[B, i] * q2
        j = HALF - 1 - k
        u = coef[BACK_A, j + 2] * u1 + coef[BACK_B, j + 2] * u2
        v = coef[BACK_A, j + 2] * v1 + coef[BACK_B, j + 2] * v2
        out[0, k] = p
        out[1, k] = q
        out[2, j] = u
        out[3, j] = v
        return p, p1, q, q1, u, u1, v, v1

    lax.fori_loop(0, HALF, body, (one, zero, zero, one) * 2, unroll=HALF)


def sweep_pair(coef, halves, lines, out):
    zero = coef[D, 0] * 0.0

    def forward(i, carry):
        y1, y2, w1, w2 = carry
        j = i + HALF
        y = ahead_step(coef, lines[at(i), :], i, y1, y2)
        w = ahead_step(coef, lines[at(j), :], j, w1, w2)
        lines[at(i), :] = y
        lines[at(j), :] = w
        return y, y1, w, w1

    s1, s2, last, before = lax.fori_loop(0, HALF, forward, (zero,) * 4, unroll=HALF)
    last = last + (halves[0, HALF - 1] * s1 + halves[1, HALF - 1] * s2)
    before = before + (halves[0, HALF - 2] * s1 + halves[1, HALF - 2] * s2)

    def reverse(k, carry):
        z1, z2, x1, x2 = carry
        i = LINES - 1 - k
        j = HALF - 1 - k
        source = lines[at(i), :] + (halves[0, i - HALF] * s1 + halves[1, i - HALF] * s2)
        z = back_step(coef, source, i, z1, z2)
        x = back_step(coef, lines[at(j), :], j, x1, x2)
        out[at(i), :] = z
        out[at(j), :] = x
        return z, z1, x, x1

    t1, t2, first, second = lax.fori_loop(0, HALF, reverse, (zero,) * 4, unroll=HALF)
    first = first + (halves[2, 0] * t1 + halves[3, 0] * t2)
    second = second + (halves[2, 1] * t1 + halves[3, 1] * t2)

    def finish(j, carry):
        out[at(j), :] = out[at(j), :] + (halves[2, j] * t1 + halves[3, j] * t2)
        return carry

    lax.fori_loop(0, HALF, finish, 0, unroll=HALF)
    return last, before, first, second


def join(full, extras):
    sub = subs()
    for k, extra in enumerate(extras):
        full[2 * k] = jnp.where(sub < COMPS, full[2 * k], roll(extra, 5, 0))
        full[2 * k + 1] = jnp.where(sub < COMPS, full[2 * k + 1], roll(extra, 2, 0))
    return full


def separate(tiles, extras):
    sub = subs()
    return tiles + [
        jnp.where(sub < 3, roll(tiles[2 * k], 3, 0), roll(tiles[2 * k + 1], -2, 0))
        for k in range(extras)
    ]


def join_six(full, other, extras):
    sub = subs()
    e0, e1, e2, e3 = extras
    full = [jnp.where(sub < COMPS, tile, roll(e, 5, 0)) for tile, e in zip(full, extras)] + [
        jnp.where(sub < COMPS, full[4], jnp.where(sub == 7, roll(e2, 4, 0), roll(e0, 2, 0))),
        jnp.where(sub < COMPS, full[5], jnp.where(sub == 7, roll(e2, 3, 0), roll(e1, 2, 0))),
    ]
    return full, jnp.where(sub < 2, roll(e3, -3, 0), other)


def separate_six(t, other):
    sub = subs()
    rest = (
        roll(t[4], -2, 0),
        roll(t[5], -2, 0),
        jnp.where(sub == 3, roll(t[4], -4, 0), roll(t[5], -3, 0)),
        roll(other, 3, 0),
    )
    return t + [jnp.where(sub < 3, roll(t[k], 3, 0), part) for k, part in enumerate(rest)]


def leaving_ends(y127, y126, z0, z1, ends):
    a127, b0, g126, g127, g0, g1 = ends
    return [a127 * y127 + g126 * y126, g127 * y127, b0 * z0 + g1 * z1, g0 * z0]


def into_next(g0, g1, lq126, lq127, lf127):
    damp = 4.0 * DAMPING
    return 0.5 * lf127 - damp * g0 * (lq126 - 4.0 * lq127), -damp * g1 * lq127


def into_previous(coefs, lq0, lq1, lf0):
    d126, d127, a126, _, g126, g127 = coefs
    damp = 4.0 * DAMPING
    r127 = -0.5 * lf0 - damp * g127 * (lq1 - 4.0 * lq0)
    y126 = d126 * (-damp * g126 * lq0)
    return d127 * (r127 + a126 * y126), y126


def block_ends(turned_u, turned_s):
    sign = signs()

    def cell(i):
        return upwind(spread(turned_u[i : i + 1, :]), spread(turned_s[i : i + 1, :]), sign)

    a127, _, g127 = cell(CELLS - 1)
    _, _, g126 = cell(CELLS - 2)
    _, b0, g0 = cell(0)
    _, _, g1 = cell(1)
    return a127, b0, g126, g127, g0, g1


def broadcast_tiles(send, tiles):
    for peer in range(send.shape[0]):
        for k, tile in enumerate(tiles):
            send[peer, ROWS * k : ROWS * k + ROWS, :] = tile


def first_kernel(
    mine, other, splat, lcol, z_out, resp, coef, ends_out, recv, turned_u, turned_s, send,
    qp, fe_scr, part_scr, qt_scr, fx_scr, sum_scr, lines, y_w1, y_w2,
):
    core = lax.rem(lax.axis_index("eta"), 2)
    for k in range(GROUPS // 2):
        for f in range(FIELDS):
            recv[2 * k + core, f] = mine[k, f]
            recv[2 * k + 1 - core, f] = other[k, f]
    for source, target in ((5, turned_u), (6, turned_s)):
        for k in range(GROUPS):
            part_scr[0, ROWS * k : ROWS * k + ROWS, :] = recv[k, source]
        target[...] = jnp.transpose(part_scr[0])
    line_coefs(lambda k: turned_u[at(k), :], lambda k: turned_s[at(k), :], coef)
    for k in range(GROUPS):
        for c in range(COMPS):
            qp[c, ROWS * k + ROWS : ROWS * k + 2 * ROWS, :] = recv[k, c]
    blank_lines(lines)
    scr = (qp, fe_scr, part_scr, qt_scr, fx_scr, sum_scr)
    types = residuals(scr, recv, turned_u, turned_s, splat, lcol, lines)

    zero = coef[D, 0] * 0.0
    y0 = coef[D, 0] * lines[0:ROWS, :]
    y1 = ahead_step(coef, lines[ROWS : 2 * ROWS, :], 1, y0, zero)
    p0 = coef[D, 0]
    p1 = coef[A, 1] * p0
    q1 = coef[D, 1]
    for ref, first, second in ((lines, y0, y1), (y_w1, p0, p1), (y_w2, zero, q1)):
        ref[0:ROWS, :] = first
        ref[ROWS : 2 * ROWS, :] = second

    def forward(i, carry):
        y1, y2, p1, p2, q1, q2 = carry
        near = coef[A, i]
        far = coef[B, i]
        y = near * y1 + (coef[D, i] * lines[at(i), :] + far * y2)
        p = near * p1 + far * p2
        q = near * q1 + far * q2
        lines[at(i), :] = y
        y_w1[at(i), :] = p
        y_w2[at(i), :] = q
        return y, y1, p, p1, q, q1

    y127, y126, p127, p126, q127, q126 = lax.fori_loop(
        2, LINES, forward, (y1, y0, p1, p0, q1, zero), unroll=LINES - 2
    )

    def reverse(i, carry, last=None):
        z1, z2, p1, p2, q1, q2, u1, u2, v1, v2 = carry
        near = coef[BACK_A, i + 2]
        far = coef[BACK_B, i + 2]
        d = coef[BACK_D, i + 2]
        z = near * z1 + (d * lines[at(i), :] + far * z2)
        p = near * p1 + (d * y_w1[at(i), :] + far * p2)
        q = near * q1 + (d * y_w2[at(i), :] + far * q2)
        if last == 0:
            u, v = d, zero
        elif last == 1:
            u, v = near * u1, d
        else:
            u = near * u1 + far * u2
            v = near * v1 + far * v2
        z_out[at(i), :] = z
        for k, part in enumerate((p, q, u, v)):
            resp[k, at(i), :] = part
        return z, z1, p, p1, q, q1, u, u1, v, v1

    carry = (zero,) * 10
    carry = reverse(LINES - 1, carry, 0)
    carry = reverse(LINES - 2, carry, 1)
    carry = lax.fori_loop(0, LINES - 2, lambda k, x: reverse(LINES - 3 - k, x), carry, unroll=LINES - 2)
    z0, z1, zp0, zp1, zq0, zq1, zu0, zu1, zv0, zv1 = carry

    ends = block_ends(turned_u, turned_s)
    a127, b0, g126, g127, g0, g1 = ends
    for k, part in enumerate(ends):
        ends_out[k] = part
    tiles = leaving_ends(y127, y126, z0, z1, ends)
    lq126, lq127, lq0, lq1, lf127, lf0 = types
    tiles += [lq126, lq127]

    def fore(last, before):
        return a127 * last + g126 * before, g127 * last

    def aft(first, second):
        return b0 * first + g1 * second, g0 * first

    f1, f2 = fore(p127, p126), fore(q127, q126)
    g1_, g2_ = aft(zp0, zp1), aft(zq0, zq1)
    h1, h2 = aft(zu0, zu1), aft(zv0, zv1)
    sub = subs()
    static = []
    raw = []
    for ref in (turned_u, turned_s):
        for i in (CELLS - 2, 0):
            raw.append(jnp.where(sub == 0, spread(ref[i : i + 1, :]), spread(ref[i + 1 : i + 2, :])))
    for one, two in ((f1, f2), (g1_, g2_), (h1, h2)):
        for k in range(2):
            tile = jnp.where(sub < COMPS, one[k], roll(two[k], 3, 0))
            if raw:
                tile = jnp.where(sub < 2, raw.pop(0), tile)
            static.append(tile)
    tiles, static[4] = join_six(tiles, static[4], (lq0, lq1, lf127, lf0))
    tiles = [jnp.where(core == 0, one, two) for one, two in zip(tiles, static)]
    broadcast_tiles(send, tiles)


def solve_point(m, c1, c2):
    p = 1.0 - m[0]
    r = 1.0 - m[3]
    inverse = 1.0 / (p * r - m[1] * m[2])
    return (r * c1 + m[1] * c2) * inverse, (m[2] * c1 + p * c2) * inverse


def apply(m, x1, x2):
    return m[0] * x1 + m[1] * x2, m[2] * x1 + m[3] * x2


def after_map(f, m, c1, c2):
    product = (
        f[0] * m[0] + f[1] * m[2],
        f[0] * m[1] + f[1] * m[3],
        f[2] * m[0] + f[3] * m[2],
        f[2] * m[1] + f[3] * m[3],
    )
    c1, c2 = apply(f, c1, c2)
    return product, c1, c2


def unpack_static(static, device, stats, slot):
    sub = subs()
    sign = signs()

    def sets(tile):
        return jnp.where(sub < 2, spread(tile[2:3, :]), tile)

    raw = []
    for k in range(6):
        tile = static(device, k)
        base = 4 * (k // 2) + 2 * (k % 2)
        stats[STATS * slot + base] = sets(tile)
        stats[STATS * slot + base + 1] = sets(roll(tile, -3, 0))
        if k < 4:
            raw += [spread(tile[0:1, :]), spread(tile[1:2, :])]
    cell = [upwind(raw[k], raw[k + 4], sign) for k in range(4)]
    a126, _, g126 = cell[0]
    a127, _, g127 = cell[1]
    parts = (
        1.0 / (1.0 + a126 + g126),
        1.0 / (1.0 + a127 + g127),
        a126,
        a127,
        g126,
        g127,
        cell[2][2],
        cell[3][2],
    )
    for k, part in enumerate(parts):
        stats[STATS * slot + 12 + k] = part


def end_coefs(stats, k):
    return [stats[STATS * k + 12 + n] for n in range(6)]


def block_terms(types, stats):
    count = len(types)
    forward, backward = [], []
    for k in range(count):
        t, later = types[k], types[(k + 1) % count]
        following = STATS * ((k + 1) % count)
        r0, r1 = into_next(stats[following + 18], stats[following + 19], t[4], t[5], t[8])
        y127, y126 = into_previous(end_coefs(stats, k), later[6], later[7], later[9])
        forward.append(leave_forward(end_coefs(stats, k), t[0] + r0, t[1] + r1, y127, y126))
        backward.append((y127, y126))
    backward = [
        (types[k][2] + backward[k - 1][0], types[k][3] + backward[k - 1][1]) for k in range(count)
    ]
    return forward, backward


def leave_forward(coefs, w1, w2, y127, y126):
    _, _, _, a127, g126, g127 = coefs
    return w1 + a127 * y127 + g126 * y126, w2 + g127 * y127


def entering(forward, backward, stats):
    count = len(forward)

    def maps(k, base):
        return [stats[STATS * k + base + n] for n in range(4)]

    m, c1, c2 = maps(0, 0), *forward[0]
    for k in range(1, count):
        m, c1, c2 = after_map(maps(k, 0), m, c1, c2)
        c1, c2 = c1 + forward[k][0], c2 + forward[k][1]
    w = [solve_point(m, c1, c2)]
    for k in range(count - 1):
        n1, n2 = apply(maps(k, 0), *w[k])
        w.append((n1 + forward[k][0], n2 + forward[k][1]))
    m = None
    for k in [0] + list(range(count - 1, 0, -1)):
        h = maps(k, 8)
        s1, s2 = apply(maps(k, 4), *w[k])
        s1, s2 = s1 + backward[k][0], s2 + backward[k][1]
        if m is None:
            m, c1, c2 = h, s1, s2
        else:
            m, c1, c2 = after_map(h, m, c1, c2)
            c1, c2 = c1 + s1, c2 + s2
    return w[0] + solve_point(m, c1, c2)


def eta_solve(z_in, resp, enter, splat, eta_coef, eta_halves, lines, rot_scr):
    def correct(i, carry):
        total = z_in[at(i), :]
        for k in range(4):
            total = total + resp[k, at(i), :] * enter[k]
        lines[at(i), :] = total
        return carry

    lax.fori_loop(0, LINES, correct, 0, unroll=LINES)
    for k in range(GROUPS):
        z = [lines[pl.ds(64 * k + c, ROWS, stride=ROWS), :] for c in range(COMPS)]
        for c, part in enumerate(rot(splat, MIDDLE, z)):
            rot_scr[c, ROWS * k : ROWS * k + ROWS, :] = part
    to_lines(rot_scr, lines)
    sweep_pair(eta_coef, eta_halves, lines, lines)


def second_kernel(
    mine, other, z_in, resp, raw, turned_u, turned_s, splat, lcol, coef, ends, eta_coef, eta_halves, halves,
    z_out, own, stats, send,
    qp, fe_scr, part_scr, qt_scr, fx_scr, sum_scr, lines,
):
    me = lax.axis_index("xi")
    count = mine.shape[0]
    swapped = lax.rem(lax.axis_index("eta"), 2) == 1

    def dynamic(device, n):
        rows = slice(ROWS * n, ROWS * n + ROWS)
        return jnp.where(swapped, other[device, rows, :], mine[device, rows, :])

    def static(device, n):
        rows = slice(ROWS * n, ROWS * n + ROWS)
        return jnp.where(swapped, mine[device, rows, :], other[device, rows, :])

    for k in range(count):
        unpack_static(static, lax.rem(me + k, count), stats, k)
    types = []
    for k in range(count):
        device = lax.rem(me + k, count)
        types.append(separate_six([dynamic(device, n) for n in range(6)], static(device, 4)))
    enter = entering(*block_terms(types, stats), stats)
    eta_solve(z_in, resp, enter, splat, eta_coef, eta_halves, lines, part_scr)
    for k in range(GROUPS):
        z = [lines[pl.ds(64 * k + c, ROWS, stride=ROWS), :] for c in range(COMPS)]
        for c, part in enumerate(rot(splat, RIGHT, z)):
            qp[c, ROWS * k + ROWS : ROWS * k + 2 * ROWS, :] = raw[k, c] + part
    row = lax.axis_index("eta")
    for c in range(COMPS):
        own[c] = qp[c, at(row + 1), :]
    scr = (qp, fe_scr, part_scr, qt_scr, fx_scr, sum_scr)
    types = residuals(scr, raw, turned_u, turned_s, splat, lcol, lines)
    y127, y126, z0, z1 = sweep_pair(coef, halves, lines, z_out)
    w1, w2, x1, x2 = leaving_ends(y127, y126, z0, z1, [ends[k] for k in range(6)])
    lq126, lq127, lq0, lq1, lf127, lf0 = types
    r0, r1 = into_next(stats[STATS + 18], stats[STATS + 19], lq126, lq127, lf127)
    y127, y126 = into_previous(end_coefs(stats, count - 1), lq0, lq1, lf0)
    tiles = join([w1 + r0, w2 + r1, x1 + y127, x2 + y126], [y127, y126])
    broadcast_tiles(send, tiles)


def last_kernel(
    recv, z_in, resp, splat, eta_coef, eta_halves, own, stats, final, increment, rot_scr, lines, few
):
    me = lax.axis_index("xi")
    count = recv.shape[0]
    types = []
    for k in range(count):
        device = lax.rem(me + k, count)
        types.append(separate([recv[device, ROWS * n : ROWS * n + ROWS, :] for n in range(4)], 2))
    forward = []
    for k in range(count):
        y127, y126 = types[(k + 1) % count][4:6]
        forward.append(leave_forward(end_coefs(stats, k), *types[k][0:2], y127, y126))
    enter = entering(forward, [t[2:4] for t in types], stats)
    eta_solve(z_in, resp, enter, splat, eta_coef, eta_halves, lines, rot_scr)
    row = lax.axis_index("eta")
    for j in range(ROWS):
        few[ROWS * j : ROWS * j + ROWS, :] = lines[at(row * ROWS + j), :]
    z = [few[pl.ds(c, ROWS, stride=ROWS), :] for c in range(COMPS)]
    for c, part in enumerate(rot(splat, RIGHT, z)):
        increment[c] = part
        final[c] = own[c] + part


def array(*shape):
    return jax.ShapeDtypeStruct(shape, F32)


def vmem(*shape):
    return pltpu.VMEM(shape, F32)


def call(kernel, name, operands, outs, scratch=()):
    return pl.pallas_call(
        kernel,
        out_shape=outs,
        in_specs=[pl.BlockSpec(memory_space=pltpu.VMEM) for _ in operands],
        out_specs=[pl.BlockSpec(memory_space=pltpu.VMEM) for _ in outs],
        scratch_shapes=list(scratch),
        compiler_params=pltpu.CompilerParams(vmem_limit_bytes=16 << 20),
        name=name,
    )(*operands)


def cell_scratch():
    padded = (COMPS, LINES + 2 * ROWS, CELLS)
    plain = (COMPS, LINES, CELLS)
    return [vmem(*shape) for shape in (padded, padded, plain, padded, padded, plain)]


def exchange(send):
    xi_count = lax.axis_size("xi")
    eta_count = lax.axis_size("eta")
    groups = []
    for e in range(eta_count):
        other = (e + eta_count // 2) % eta_count
        groups.append(
            [k * eta_count + (e if k < xi_count // 2 else other) for k in range(xi_count)]
        )
    return lax.all_to_all(send, ("xi", "eta"), 0, 0, axis_index_groups=groups, tiled=True)


def per_device(
    flow_state,
    speed_xi,
    sound_xi,
    speed_eta,
    sound_eta,
    coupling,
    left_vectors,
    middle_vectors,
    right_vectors,
):
    xi_count = lax.axis_size("xi")
    flat = ROWS * LINES
    send, matrices = pl.pallas_call(
        pack_kernel,
        out_shape=[array(GROUPS // 2, FIELDS, ROWS, CELLS), array(4, COMPS, COMPS)],
        in_specs=[pl.BlockSpec(memory_space=pltpu.HBM)] * 9,
        out_specs=[pl.BlockSpec(memory_space=pltpu.HBM)] * 2,
        scratch_shapes=[vmem(FIELDS, ROWS, CELLS)]
        + [vmem(COMPS, COMPS)] * 4
        + [pltpu.SemaphoreType.DMA((9 + GROUPS // 2,))],
        compiler_params=pltpu.CompilerParams(vmem_limit_bytes=60 << 20),
        name="pack",
    )(
        flow_state[:, 0],
        speed_xi[0],
        sound_xi[0],
        speed_eta[0],
        sound_eta[0],
        coupling,
        left_vectors,
        middle_vectors,
        right_vectors,
    )
    groups = [[2 * k + core for k in range(GROUPS // 2)] for core in range(2)]
    mine = lax.all_to_all(send, "eta", 0, 0, axis_index_groups=groups, tiled=True)
    swap = [(k, k ^ 1) for k in range(GROUPS)]
    other = lax.ppermute(mine, "eta", swap)
    splat, lcol = call(
        splat_kernel, "splat", (matrices,), [array(100, ROWS, CELLS), array(COMPS, ROWS, CELLS)]
    )
    z_local, resp, coef, ends, raw, turned_u, turned_s, send = call(
        first_kernel,
        "first",
        (mine, other, splat, lcol),
        [
            array(flat, CELLS),
            array(4, flat, CELLS),
            array(6, LINES + 2, ROWS, CELLS),
            array(6, ROWS, CELLS),
            array(GROUPS, FIELDS, ROWS, CELLS),
            array(CELLS, LINES),
            array(CELLS, LINES),
            array(xi_count, FIRST, CELLS),
        ],
        cell_scratch()
        + [vmem(flat, CELLS), vmem(flat, CELLS), vmem(flat, CELLS)],
    )
    mine = exchange(send)
    other = lax.ppermute(mine, "eta", swap)
    eta_coef, eta_halves, halves = call(
        eta_static_kernel,
        "eta_static",
        (raw, coef),
        [array(6, LINES + 2, ROWS, CELLS)] + [array(4, HALF, ROWS, CELLS)] * 2,
    )
    z_local, own, stats, send = call(
        second_kernel,
        "second",
        (mine, other, z_local, resp, raw, turned_u, turned_s, splat, lcol, coef, ends, eta_coef, eta_halves, halves),
        [
            array(flat, CELLS),
            array(COMPS, ROWS, CELLS),
            array(STATS * xi_count, ROWS, CELLS),
            array(xi_count, SECOND, CELLS),
        ],
        cell_scratch() + [vmem(flat, CELLS)],
    )
    recv = exchange(send)
    final, increment = call(
        last_kernel,
        "last",
        (recv, z_local, resp, splat, eta_coef, eta_halves, own, stats),
        [array(COMPS, ROWS, CELLS), array(COMPS, ROWS, CELLS)],
        [vmem(COMPS, LINES, CELLS), vmem(flat, CELLS), vmem(ROWS * ROWS, CELLS)],
    )
    return final[:, None], increment[:, None]


def solution(mesh):
    return jax.shard_map(
        per_device,
        mesh=mesh,
        in_specs=(
            P(None, None, "eta", "xi"),
            P(None, "eta", "xi"),
            P(None, "eta", "xi"),
            P(None, "eta", "xi"),
            P(None, "eta", "xi"),
            P(),
            P(),
            P(),
            P(),
        ),
        out_specs=(P(None, None, "eta", "xi"), P(None, None, "eta", "xi")),
        check_vma=False,
    )
```

```python
import jax
import jax.numpy as jnp
from jax import lax
from jax.experimental import pallas as pl
from jax.experimental.pallas import tpu as pltpu
from jax.sharding import PartitionSpec as P


ROWS = 8
CELLS = 128
COMPS = 5
DAMPING = 0.01
GROUPS = 16
LINES = GROUPS * ROWS
HALF = LINES // 2
FIELDS = 9
FIRST = 48
SECOND = 32
STATS = 20
F32 = jnp.float32
COUPLING, LEFT, MIDDLE, RIGHT = range(4)
A, B, D, BACK_A, BACK_B, BACK_D = range(6)


def lanes():
    return lax.broadcasted_iota(jnp.int32, (ROWS, CELLS), 1)


def subs():
    return lax.broadcasted_iota(jnp.int32, (ROWS, CELLS), 0)


def roll(x, shift, axis):
    return pltpu.roll(x, shift % x.shape[axis], axis)


def rot(splat, which, fields):
    out = []
    for a in range(COMPS):
        total = splat[25 * which + 5 * a] * fields[0]
        for b in range(1, COMPS):
            total = total + splat[25 * which + 5 * a + b] * fields[b]
        out.append(total)
    return out


def place(tile, source, cell, count, slot):
    lane = lanes()
    moved = roll(source, slot - cell, 1)
    return jnp.where((lane >= slot) & (lane < slot + count), moved, tile)


def spread(row):
    return jnp.broadcast_to(row, (ROWS, CELLS))


def signs():
    sub = subs()
    return jnp.where(sub == 3, 1.0, 0.0) - jnp.where(sub == 4, 1.0, 0.0)


def upwind(u, s, sign):
    g = 0.25 * (jnp.abs(u) + s)
    e = u + sign * s
    return jnp.maximum(e, 0.0) + g, jnp.maximum(-e, 0.0) + g, g


def pack_kernel(
    state, ux, sx, ue, se, coupling, left, middle, right, send, matrices, block, m0, m1, m2, m3, sem
):
    fields = [pltpu.make_async_copy(state, block.at[0:COMPS], sem.at[0])]
    for k, source in enumerate((ux, sx, ue, se)):
        fields.append(pltpu.make_async_copy(source, block.at[COMPS + k], sem.at[1 + k]))
    small = [
        pltpu.make_async_copy(source, target, sem.at[5 + k])
        for k, (source, target) in enumerate(zip((coupling, left, middle, right), (m0, m1, m2, m3)))
    ]
    for copy in fields + small:
        copy.start()
    for copy in fields:
        copy.wait()
    out = [pltpu.make_async_copy(block, send.at[p], sem.at[9 + p]) for p in range(send.shape[0])]
    for copy in out:
        copy.start()
    for k, source in enumerate((m0, m1, m2, m3)):
        small[k].wait()
        copy = pltpu.make_async_copy(source, matrices.at[k], sem.at[5 + k])
        copy.start()
        out.append(copy)
    for copy in out:
        copy.wait()


def splat_kernel(matrices, splat, lcol):
    sub = subs()
    for which in range(4):
        matrix = matrices[which]
        for a in range(COMPS):
            for b in range(COMPS):
                splat[25 * which + COMPS * a + b] = jnp.broadcast_to(
                    matrix[a : a + 1, b : b + 1], (ROWS, CELLS)
                )
    for b in range(COMPS):
        column = jnp.zeros((ROWS, CELLS), F32)
        for a in range(COMPS):
            column = jnp.where(sub == a, splat[25 * LEFT + COMPS * a + b], column)
        lcol[b] = column


def line_coefs(u_block, s_block, out):
    sign = signs()
    zero = u_block(0) * 0.0

    def body(k, carry):
        a1, g1, g2, d1, d2 = carry
        ub = u_block(k)
        sb = s_block(k)
        for r in range(ROWS):
            i = k * ROWS + r
            a, b, g = upwind(spread(ub[r : r + 1, :]), spread(sb[r : r + 1, :]), sign)
            da = 1.0 / (1.0 + a + g)
            db = 1.0 / (1.0 + b + g)
            out[A, i] = a1 * da
            out[B, i] = g2 * da
            out[D, i] = da
            out[BACK_D, i + 2] = db
            out[BACK_A, i + 1] = b * d1
            out[BACK_B, i] = g * d2
            a1, g1, g2, d1, d2 = a, g, g1, db, d1
        return a1, g1, g2, d1, d2

    lax.fori_loop(0, GROUPS, body, (zero,) * 5, unroll=GROUPS)
    out[BACK_A, LINES + 1] = zero
    out[BACK_B, LINES] = zero
    out[BACK_B, LINES + 1] = zero


def at(i):
    return pl.ds(pl.multiple_of(i * ROWS, ROWS), ROWS)


def eta_static_kernel(recv, coef, eta_coef, eta_halves, halves):
    line_coefs(lambda k: recv[k, 7], lambda k: recv[k, 8], eta_coef)
    half_responses(eta_coef, eta_halves)
    half_responses(coef, halves)


def seal(scr):
    for c in range(COMPS):
        scr[c, 0:ROWS, :] = jnp.zeros((ROWS, CELLS), F32)
        scr[c, LINES + ROWS : LINES + 2 * ROWS, :] = jnp.zeros((ROWS, CELLS), F32)


def near(scr, c, k, offset=0):
    base = (k + 1) * ROWS + offset
    return scr[c, base : base + ROWS, :]


def along(q_scr, flux_scr, c, k, damp):
    central = near(flux_scr, c, k, 1) - near(flux_scr, c, k, -1)
    fourth = (
        (near(q_scr, c, k, 2) + near(q_scr, c, k, -2))
        - 4.0 * (near(q_scr, c, k, 1) + near(q_scr, c, k, -1))
        + 6.0 * near(q_scr, c, k)
    )
    return -0.5 * central - damp * fourth


def flux_rows(q_scr, flux_scr, splat, u_of, s_of):
    for k in range(GROUPS):
        q = [near(q_scr, c, k) for c in range(COMPS)]
        p = rot(splat, COUPLING, q)
        u = u_of(k)
        s = s_of(k)
        for c in range(COMPS):
            base = (k + 1) * ROWS
            flux_scr[c, base : base + ROWS, :] = u * q[c] + s * p[c]


def residuals(scr, recv, turned_u, turned_s, splat, lcol, lines):
    qp, fe_scr, part_scr, qt_scr, fx_scr, sum_scr = scr
    for padded in (qp, fe_scr, qt_scr, fx_scr):
        seal(padded)
    for c in range(COMPS):
        qt_scr[c, ROWS : ROWS + LINES, :] = jnp.transpose(qp[c, ROWS : ROWS + LINES, :])
    flux_rows(qp, fe_scr, splat, lambda k: recv[k, 7], lambda k: recv[k, 8])
    for k in range(GROUPS):
        damp = DAMPING * (jnp.abs(recv[k, 7]) + recv[k, 8])
        for c in range(COMPS):
            part_scr[c, ROWS * k : ROWS * k + ROWS, :] = along(qp, fe_scr, c, k, damp)
    for c in range(COMPS):
        sum_scr[c] = jnp.transpose(part_scr[c])

    def block(ref, k):
        return ref[ROWS * k : ROWS * k + ROWS, :]

    flux_rows(qt_scr, fx_scr, splat, lambda k: block(turned_u, k), lambda k: block(turned_s, k))
    for k in range(GROUPS):
        damp = DAMPING * (jnp.abs(block(turned_u, k)) + block(turned_s, k))
        residual = [
            along(qt_scr, fx_scr, c, k, damp) + block(sum_scr.at[c], k) for c in range(COMPS)
        ]
        for c, value in enumerate(rot(splat, LEFT, residual)):
            lines[pl.ds(64 * k + c, ROWS, stride=ROWS), :] = value
    columns = [lcol[b] for b in range(COMPS)]

    def mix(source, cell):
        row = ROWS + cell
        total = columns[0] * spread(source[0, row : row + 1, :])
        for b in range(1, COMPS):
            total = total + columns[b] * spread(source[b, row : row + 1, :])
        return total

    last = CELLS - 1
    return [mix(qt_scr, cell) for cell in (last - 1, last, 0, 1)] + [
        mix(fx_scr, cell) for cell in (last, 0)
    ]


def to_lines(cells, out):
    for c in range(COMPS):
        out[pl.ds(c, LINES, stride=ROWS), :] = jnp.transpose(cells[c])


def blank_lines(out):
    zero = jnp.zeros((ROWS, CELLS), F32)
    for i in range(LINES):
        out[ROWS * i : ROWS * i + ROWS, :] = zero


def ahead_step(coef, source, i, y1, y2):
    return coef[A, i] * y1 + (coef[D, i] * source + coef[B, i] * y2)


def back_step(coef, source, i, z1, z2):
    return coef[BACK_A, i + 2] * z1 + (coef[BACK_D, i + 2] * source + coef[BACK_B, i + 2] * z2)


def half_responses(coef, out):
    zero = coef[D, 0] * 0.0
    one = zero + 1.0

    def body(k, carry):
        p1, p2, q1, q2, u1, u2, v1, v2 = carry
        i = HALF + k
        p = coef[A, i] * p1 + coef[B, i] * p2
        q = coef[A, i] * q1 + coef[B, i] * q2
        j = HALF - 1 - k
        u = coef[BACK_A, j + 2] * u1 + coef[BACK_B, j + 2] * u2
        v = coef[BACK_A, j + 2] * v1 + coef[BACK_B, j + 2] * v2
        out[0, k] = p
        out[1, k] = q
        out[2, j] = u
        out[3, j] = v
        return p, p1, q, q1, u, u1, v, v1

    lax.fori_loop(0, HALF, body, (one, zero, zero, one) * 2, unroll=HALF)


def sweep_pair(coef, halves, lines, out, whole=True):
    zero = coef[D, 0] * 0.0

    def forward(i, carry):
        y1, y2, w1, w2 = carry
        j = i + HALF
        y = ahead_step(coef, lines[at(i), :], i, y1, y2)
        w = ahead_step(coef, lines[at(j), :], j, w1, w2)
        lines[at(i), :] = y
        lines[at(j), :] = w
        return y, y1, w, w1

    s1, s2, last, before = lax.fori_loop(0, HALF, forward, (zero,) * 4, unroll=HALF)
    last = last + (halves[0, HALF - 1] * s1 + halves[1, HALF - 1] * s2)
    before = before + (halves[0, HALF - 2] * s1 + halves[1, HALF - 2] * s2)

    def reverse(k, carry):
        z1, z2, x1, x2 = carry
        i = LINES - 1 - k
        j = HALF - 1 - k
        source = lines[at(i), :] + (halves[0, i - HALF] * s1 + halves[1, i - HALF] * s2)
        z = back_step(coef, source, i, z1, z2)
        x = back_step(coef, lines[at(j), :], j, x1, x2)
        out[at(i), :] = z
        out[at(j), :] = x
        return z, z1, x, x1

    t1, t2, first, second = lax.fori_loop(0, HALF, reverse, (zero,) * 4, unroll=HALF)
    if not whole:
        return t1, t2
    first = first + (halves[2, 0] * t1 + halves[3, 0] * t2)
    second = second + (halves[2, 1] * t1 + halves[3, 1] * t2)

    def finish(j, carry):
        out[at(j), :] = out[at(j), :] + (halves[2, j] * t1 + halves[3, j] * t2)
        return carry

    lax.fori_loop(0, HALF, finish, 0, unroll=HALF)
    return last, before, first, second


def join(full, extras):
    sub = subs()
    for k, extra in enumerate(extras):
        full[2 * k] = jnp.where(sub < COMPS, full[2 * k], roll(extra, 5, 0))
        full[2 * k + 1] = jnp.where(sub < COMPS, full[2 * k + 1], roll(extra, 2, 0))
    return full


def separate(tiles, extras):
    sub = subs()
    return tiles + [
        jnp.where(sub < 3, roll(tiles[2 * k], 3, 0), roll(tiles[2 * k + 1], -2, 0))
        for k in range(extras)
    ]


def join_six(full, other, extras):
    sub = subs()
    e0, e1, e2, e3 = extras
    full = [jnp.where(sub < COMPS, tile, roll(e, 5, 0)) for tile, e in zip(full, extras)] + [
        jnp.where(sub < COMPS, full[4], jnp.where(sub == 7, roll(e2, 4, 0), roll(e0, 2, 0))),
        jnp.where(sub < COMPS, full[5], jnp.where(sub == 7, roll(e2, 3, 0), roll(e1, 2, 0))),
    ]
    return full, jnp.where(sub < 2, roll(e3, -3, 0), other)


def separate_six(t, other):
    sub = subs()
    rest = (
        roll(t[4], -2, 0),
        roll(t[5], -2, 0),
        jnp.where(sub == 3, roll(t[4], -4, 0), roll(t[5], -3, 0)),
        roll(other, 3, 0),
    )
    return t + [jnp.where(sub < 3, roll(t[k], 3, 0), part) for k, part in enumerate(rest)]


def leaving_ends(y127, y126, z0, z1, ends):
    a127, b0, g126, g127, g0, g1 = ends
    return [a127 * y127 + g126 * y126, g127 * y127, b0 * z0 + g1 * z1, g0 * z0]


def into_next(g0, g1, lq126, lq127, lf127):
    damp = 4.0 * DAMPING
    return 0.5 * lf127 - damp * g0 * (lq126 - 4.0 * lq127), -damp * g1 * lq127


def into_previous(coefs, lq0, lq1, lf0):
    d126, d127, a126, _, g126, g127 = coefs
    damp = 4.0 * DAMPING
    r127 = -0.5 * lf0 - damp * g127 * (lq1 - 4.0 * lq0)
    y126 = d126 * (-damp * g126 * lq0)
    return d127 * (r127 + a126 * y126), y126


def block_ends(turned_u, turned_s):
    sign = signs()

    def cell(i):
        return upwind(spread(turned_u[i : i + 1, :]), spread(turned_s[i : i + 1, :]), sign)

    a127, _, g127 = cell(CELLS - 1)
    _, _, g126 = cell(CELLS - 2)
    _, b0, g0 = cell(0)
    _, _, g1 = cell(1)
    return a127, b0, g126, g127, g0, g1


def broadcast_tiles(send, tiles):
    for peer in range(send.shape[0]):
        for k, tile in enumerate(tiles):
            send[peer, ROWS * k : ROWS * k + ROWS, :] = tile


def first_kernel(
    mine, other, splat, lcol, z_out, resp, coef, ends_out, recv, turned_u, turned_s, send,
    qp, fe_scr, part_scr, qt_scr, fx_scr, sum_scr, lines, y_w1, y_w2,
):
    core = lax.rem(lax.axis_index("eta"), 2)
    for k in range(GROUPS // 2):
        for f in range(FIELDS):
            recv[2 * k + core, f] = mine[k, f]
            recv[2 * k + 1 - core, f] = other[k, f]
    for source, target in ((5, turned_u), (6, turned_s)):
        for k in range(GROUPS):
            part_scr[0, ROWS * k : ROWS * k + ROWS, :] = recv[k, source]
        target[...] = jnp.transpose(part_scr[0])
    line_coefs(lambda k: turned_u[at(k), :], lambda k: turned_s[at(k), :], coef)
    for k in range(GROUPS):
        for c in range(COMPS):
            qp[c, ROWS * k + ROWS : ROWS * k + 2 * ROWS, :] = recv[k, c]
    blank_lines(lines)
    scr = (qp, fe_scr, part_scr, qt_scr, fx_scr, sum_scr)
    types = residuals(scr, recv, turned_u, turned_s, splat, lcol, lines)

    zero = coef[D, 0] * 0.0
    y0 = coef[D, 0] * lines[0:ROWS, :]
    y1 = ahead_step(coef, lines[ROWS : 2 * ROWS, :], 1, y0, zero)
    p0 = coef[D, 0]
    p1 = coef[A, 1] * p0
    q1 = coef[D, 1]
    for ref, first, second in ((lines, y0, y1), (y_w1, p0, p1), (y_w2, zero, q1)):
        ref[0:ROWS, :] = first
        ref[ROWS : 2 * ROWS, :] = second

    def forward(i, carry):
        y1, y2, p1, p2, q1, q2 = carry
        near = coef[A, i]
        far = coef[B, i]
        y = near * y1 + (coef[D, i] * lines[at(i), :] + far * y2)
        p = near * p1 + far * p2
        q = near * q1 + far * q2
        lines[at(i), :] = y
        y_w1[at(i), :] = p
        y_w2[at(i), :] = q
        return y, y1, p, p1, q, q1

    y127, y126, p127, p126, q127, q126 = lax.fori_loop(
        2, LINES, forward, (y1, y0, p1, p0, q1, zero), unroll=LINES - 2
    )

    def reverse(i, carry, last=None):
        z1, z2, p1, p2, q1, q2, u1, u2, v1, v2 = carry
        near = coef[BACK_A, i + 2]
        far = coef[BACK_B, i + 2]
        d = coef[BACK_D, i + 2]
        z = near * z1 + (d * lines[at(i), :] + far * z2)
        p = near * p1 + (d * y_w1[at(i), :] + far * p2)
        q = near * q1 + (d * y_w2[at(i), :] + far * q2)
        if last == 0:
            u, v = d, zero
        elif last == 1:
            u, v = near * u1, d
        else:
            u = near * u1 + far * u2
            v = near * v1 + far * v2
        z_out[at(i), :] = z
        for k, part in enumerate((p, q, u, v)):
            resp[k, at(i), :] = part
        return z, z1, p, p1, q, q1, u, u1, v, v1

    carry = (zero,) * 10
    carry = reverse(LINES - 1, carry, 0)
    carry = reverse(LINES - 2, carry, 1)
    carry = lax.fori_loop(0, LINES - 2, lambda k, x: reverse(LINES - 3 - k, x), carry, unroll=LINES - 2)
    z0, z1, zp0, zp1, zq0, zq1, zu0, zu1, zv0, zv1 = carry

    ends = block_ends(turned_u, turned_s)
    a127, b0, g126, g127, g0, g1 = ends
    for k, part in enumerate(ends):
        ends_out[k] = part
    tiles = leaving_ends(y127, y126, z0, z1, ends)
    lq126, lq127, lq0, lq1, lf127, lf0 = types
    tiles += [lq126, lq127]

    def fore(last, before):
        return a127 * last + g126 * before, g127 * last

    def aft(first, second):
        return b0 * first + g1 * second, g0 * first

    f1, f2 = fore(p127, p126), fore(q127, q126)
    g1_, g2_ = aft(zp0, zp1), aft(zq0, zq1)
    h1, h2 = aft(zu0, zu1), aft(zv0, zv1)
    sub = subs()
    static = []
    raw = []
    for ref in (turned_u, turned_s):
        for i in (CELLS - 2, 0):
            raw.append(jnp.where(sub == 0, spread(ref[i : i + 1, :]), spread(ref[i + 1 : i + 2, :])))
    for one, two in ((f1, f2), (g1_, g2_), (h1, h2)):
        for k in range(2):
            tile = jnp.where(sub < COMPS, one[k], roll(two[k], 3, 0))
            if raw:
                tile = jnp.where(sub < 2, raw.pop(0), tile)
            static.append(tile)
    tiles, static[4] = join_six(tiles, static[4], (lq0, lq1, lf127, lf0))
    tiles = [jnp.where(core == 0, one, two) for one, two in zip(tiles, static)]
    broadcast_tiles(send, tiles)


def solve_point(m, c1, c2):
    p = 1.0 - m[0]
    r = 1.0 - m[3]
    inverse = 1.0 / (p * r - m[1] * m[2])
    return (r * c1 + m[1] * c2) * inverse, (m[2] * c1 + p * c2) * inverse


def apply(m, x1, x2):
    return m[0] * x1 + m[1] * x2, m[2] * x1 + m[3] * x2


def after_map(f, m, c1, c2):
    product = (
        f[0] * m[0] + f[1] * m[2],
        f[0] * m[1] + f[1] * m[3],
        f[2] * m[0] + f[3] * m[2],
        f[2] * m[1] + f[3] * m[3],
    )
    c1, c2 = apply(f, c1, c2)
    return product, c1, c2


def unpack_static(static, device, stats, slot):
    sub = subs()
    sign = signs()

    def sets(tile):
        return jnp.where(sub < 2, spread(tile[2:3, :]), tile)

    raw = []
    for k in range(6):
        tile = static(device, k)
        base = 4 * (k // 2) + 2 * (k % 2)
        stats[STATS * slot + base] = sets(tile)
        stats[STATS * slot + base + 1] = sets(roll(tile, -3, 0))
        if k < 4:
            raw += [spread(tile[0:1, :]), spread(tile[1:2, :])]
    cell = [upwind(raw[k], raw[k + 4], sign) for k in range(4)]
    a126, _, g126 = cell[0]
    a127, _, g127 = cell[1]
    parts = (
        1.0 / (1.0 + a126 + g126),
        1.0 / (1.0 + a127 + g127),
        a126,
        a127,
        g126,
        g127,
        cell[2][2],
        cell[3][2],
    )
    for k, part in enumerate(parts):
        stats[STATS * slot + 12 + k] = part


def end_coefs(stats, k):
    return [stats[STATS * k + 12 + n] for n in range(6)]


def block_terms(types, stats):
    count = len(types)
    forward, backward = [], []
    for k in range(count):
        t, later = types[k], types[(k + 1) % count]
        following = STATS * ((k + 1) % count)
        r0, r1 = into_next(stats[following + 18], stats[following + 19], t[4], t[5], t[8])
        y127, y126 = into_previous(end_coefs(stats, k), later[6], later[7], later[9])
        forward.append(leave_forward(end_coefs(stats, k), t[0] + r0, t[1] + r1, y127, y126))
        backward.append((y127, y126))
    backward = [
        (types[k][2] + backward[k - 1][0], types[k][3] + backward[k - 1][1]) for k in range(count)
    ]
    return forward, backward


def leave_forward(coefs, w1, w2, y127, y126):
    _, _, _, a127, g126, g127 = coefs
    return w1 + a127 * y127 + g126 * y126, w2 + g127 * y127


def entering(forward, backward, stats):
    count = len(forward)

    def maps(k, base):
        return [stats[STATS * k + base + n] for n in range(4)]

    m, c1, c2 = maps(0, 0), *forward[0]
    for k in range(1, count):
        m, c1, c2 = after_map(maps(k, 0), m, c1, c2)
        c1, c2 = c1 + forward[k][0], c2 + forward[k][1]
    w = [solve_point(m, c1, c2)]
    for k in range(count - 1):
        n1, n2 = apply(maps(k, 0), *w[k])
        w.append((n1 + forward[k][0], n2 + forward[k][1]))
    m = None
    for k in [0] + list(range(count - 1, 0, -1)):
        h = maps(k, 8)
        s1, s2 = apply(maps(k, 4), *w[k])
        s1, s2 = s1 + backward[k][0], s2 + backward[k][1]
        if m is None:
            m, c1, c2 = h, s1, s2
        else:
            m, c1, c2 = after_map(h, m, c1, c2)
            c1, c2 = c1 + s1, c2 + s2
    return w[0] + solve_point(m, c1, c2)


def eta_solve(z_in, resp, enter, splat, eta_coef, eta_halves, lines, rot_scr, whole=True):
    def correct(i, carry):
        total = z_in[at(i), :]
        for k in range(4):
            total = total + resp[k, at(i), :] * enter[k]
        lines[at(i), :] = total
        return carry

    lax.fori_loop(0, LINES, correct, 0, unroll=LINES)
    for k in range(GROUPS):
        z = [lines[pl.ds(64 * k + c, ROWS, stride=ROWS), :] for c in range(COMPS)]
        for c, part in enumerate(rot(splat, MIDDLE, z)):
            rot_scr[c, ROWS * k : ROWS * k + ROWS, :] = part
    to_lines(rot_scr, lines)
    return sweep_pair(eta_coef, eta_halves, lines, lines, whole)


def second_kernel(
    mine, other, z_in, resp, raw, turned_u, turned_s, splat, lcol, coef, ends, eta_coef, eta_halves, halves,
    z_out, own, stats, send,
    qp, fe_scr, part_scr, qt_scr, fx_scr, sum_scr, lines,
):
    me = lax.axis_index("xi")
    count = mine.shape[0]
    swapped = lax.rem(lax.axis_index("eta"), 2) == 1

    def dynamic(device, n):
        rows = slice(ROWS * n, ROWS * n + ROWS)
        return jnp.where(swapped, other[device, rows, :], mine[device, rows, :])

    def static(device, n):
        rows = slice(ROWS * n, ROWS * n + ROWS)
        return jnp.where(swapped, mine[device, rows, :], other[device, rows, :])

    for k in range(count):
        unpack_static(static, lax.rem(me + k, count), stats, k)
    types = []
    for k in range(count):
        device = lax.rem(me + k, count)
        types.append(separate_six([dynamic(device, n) for n in range(6)], static(device, 4)))
    enter = entering(*block_terms(types, stats), stats)
    eta_solve(z_in, resp, enter, splat, eta_coef, eta_halves, lines, part_scr)
    for k in range(GROUPS):
        z = [lines[pl.ds(64 * k + c, ROWS, stride=ROWS), :] for c in range(COMPS)]
        for c, part in enumerate(rot(splat, RIGHT, z)):
            qp[c, ROWS * k + ROWS : ROWS * k + 2 * ROWS, :] = raw[k, c] + part
    row = lax.axis_index("eta")
    for c in range(COMPS):
        own[c] = qp[c, at(row + 1), :]
    scr = (qp, fe_scr, part_scr, qt_scr, fx_scr, sum_scr)
    types = residuals(scr, raw, turned_u, turned_s, splat, lcol, lines)
    y127, y126, z0, z1 = sweep_pair(coef, halves, lines, z_out)
    w1, w2, x1, x2 = leaving_ends(y127, y126, z0, z1, [ends[k] for k in range(6)])
    lq126, lq127, lq0, lq1, lf127, lf0 = types
    r0, r1 = into_next(stats[STATS + 18], stats[STATS + 19], lq126, lq127, lf127)
    y127, y126 = into_previous(end_coefs(stats, count - 1), lq0, lq1, lf0)
    tiles = join([w1 + r0, w2 + r1, x1 + y127, x2 + y126], [y127, y126])
    broadcast_tiles(send, tiles)


def last_kernel(
    recv, z_in, resp, splat, eta_coef, eta_halves, own, stats, final, increment, rot_scr, lines, few
):
    me = lax.axis_index("xi")
    count = recv.shape[0]
    types = []
    for k in range(count):
        device = lax.rem(me + k, count)
        types.append(separate([recv[device, ROWS * n : ROWS * n + ROWS, :] for n in range(4)], 2))
    forward = []
    for k in range(count):
        y127, y126 = types[(k + 1) % count][4:6]
        forward.append(leave_forward(end_coefs(stats, k), *types[k][0:2], y127, y126))
    enter = entering(forward, [t[2:4] for t in types], stats)
    t1, t2 = eta_solve(z_in, resp, enter, splat, eta_coef, eta_halves, lines, rot_scr, False)
    row = lax.axis_index("eta")
    for j in range(ROWS):
        at_row = row * ROWS + j
        low = jnp.minimum(at_row, HALF - 1)
        added = eta_halves[2, low] * t1 + eta_halves[3, low] * t2
        value = lines[at(at_row), :]
        few[ROWS * j : ROWS * j + ROWS, :] = jnp.where(at_row < HALF, value + added, value)
    z = [few[pl.ds(c, ROWS, stride=ROWS), :] for c in range(COMPS)]
    for c, part in enumerate(rot(splat, RIGHT, z)):
        increment[c] = part
        final[c] = own[c] + part


def array(*shape):
    return jax.ShapeDtypeStruct(shape, F32)


def vmem(*shape):
    return pltpu.VMEM(shape, F32)


def call(kernel, name, operands, outs, scratch=()):
    return pl.pallas_call(
        kernel,
        out_shape=outs,
        in_specs=[pl.BlockSpec(memory_space=pltpu.VMEM) for _ in operands],
        out_specs=[pl.BlockSpec(memory_space=pltpu.VMEM) for _ in outs],
        scratch_shapes=list(scratch),
        compiler_params=pltpu.CompilerParams(vmem_limit_bytes=16 << 20),
        name=name,
    )(*operands)


def cell_scratch():
    padded = (COMPS, LINES + 2 * ROWS, CELLS)
    plain = (COMPS, LINES, CELLS)
    return [vmem(*shape) for shape in (padded, padded, plain, padded, padded, plain)]


def exchange(send):
    xi_count = lax.axis_size("xi")
    eta_count = lax.axis_size("eta")
    groups = []
    for e in range(eta_count):
        other = (e + eta_count // 2) % eta_count
        groups.append(
            [k * eta_count + (e if k < xi_count // 2 else other) for k in range(xi_count)]
        )
    return lax.all_to_all(send, ("xi", "eta"), 0, 0, axis_index_groups=groups, tiled=True)


def per_device(
    flow_state,
    speed_xi,
    sound_xi,
    speed_eta,
    sound_eta,
    coupling,
    left_vectors,
    middle_vectors,
    right_vectors,
):
    xi_count = lax.axis_size("xi")
    flat = ROWS * LINES
    send, matrices = pl.pallas_call(
        pack_kernel,
        out_shape=[array(GROUPS // 2, FIELDS, ROWS, CELLS), array(4, COMPS, COMPS)],
        in_specs=[pl.BlockSpec(memory_space=pltpu.HBM)] * 9,
        out_specs=[pl.BlockSpec(memory_space=pltpu.HBM)] * 2,
        scratch_shapes=[vmem(FIELDS, ROWS, CELLS)]
        + [vmem(COMPS, COMPS)] * 4
        + [pltpu.SemaphoreType.DMA((9 + GROUPS // 2,))],
        compiler_params=pltpu.CompilerParams(vmem_limit_bytes=60 << 20),
        name="pack",
    )(
        flow_state[:, 0],
        speed_xi[0],
        sound_xi[0],
        speed_eta[0],
        sound_eta[0],
        coupling,
        left_vectors,
        middle_vectors,
        right_vectors,
    )
    groups = [[2 * k + core for k in range(GROUPS // 2)] for core in range(2)]
    mine = lax.all_to_all(send, "eta", 0, 0, axis_index_groups=groups, tiled=True)
    swap = [(k, k ^ 1) for k in range(GROUPS)]
    other = lax.ppermute(mine, "eta", swap)
    splat, lcol = call(
        splat_kernel, "splat", (matrices,), [array(100, ROWS, CELLS), array(COMPS, ROWS, CELLS)]
    )
    z_local, resp, coef, ends, raw, turned_u, turned_s, send = call(
        first_kernel,
        "first",
        (mine, other, splat, lcol),
        [
            array(flat, CELLS),
            array(4, flat, CELLS),
            array(6, LINES + 2, ROWS, CELLS),
            array(6, ROWS, CELLS),
            array(GROUPS, FIELDS, ROWS, CELLS),
            array(CELLS, LINES),
            array(CELLS, LINES),
            array(xi_count, FIRST, CELLS),
        ],
        cell_scratch()
        + [vmem(flat, CELLS), vmem(flat, CELLS), vmem(flat, CELLS)],
    )
    mine = exchange(send)
    other = lax.ppermute(mine, "eta", swap)
    eta_coef, eta_halves, halves = call(
        eta_static_kernel,
        "eta_static",
        (raw, coef),
        [array(6, LINES + 2, ROWS, CELLS)] + [array(4, HALF, ROWS, CELLS)] * 2,
    )
    z_local, own, stats, send = call(
        second_kernel,
        "second",
        (mine, other, z_local, resp, raw, turned_u, turned_s, splat, lcol, coef, ends, eta_coef, eta_halves, halves),
        [
            array(flat, CELLS),
            array(COMPS, ROWS, CELLS),
            array(STATS * xi_count, ROWS, CELLS),
            array(xi_count, SECOND, CELLS),
        ],
        cell_scratch() + [vmem(flat, CELLS)],
    )
    recv = exchange(send)
    final, increment = call(
        last_kernel,
        "last",
        (recv, z_local, resp, splat, eta_coef, eta_halves, own, stats),
        [array(COMPS, ROWS, CELLS), array(COMPS, ROWS, CELLS)],
        [vmem(COMPS, LINES, CELLS), vmem(flat, CELLS), vmem(ROWS * ROWS, CELLS)],
    )
    return final[:, None], increment[:, None]


def solution(mesh):
    return jax.shard_map(
        per_device,
        mesh=mesh,
        in_specs=(
            P(None, None, "eta", "xi"),
            P(None, "eta", "xi"),
            P(None, "eta", "xi"),
            P(None, "eta", "xi"),
            P(None, "eta", "xi"),
            P(),
            P(),
            P(),
            P(),
        ),
        out_specs=(P(None, None, "eta", "xi"), P(None, None, "eta", "xi")),
        check_vma=False,
    )
```
